128 devices in a mesh: prefix: 16 (over z, x_hi, core), resp: 8 (over y, x_lo).
Axes of the slice: x: 4 (x_hi: 2, x_lo: 2; x = x_hi * 2 + x_lo), y: 4, z: 4, core: 2. Of those that a mesh axis runs over, the one named last changes fastest.
Arguments:
- resp_query: bfloat16 [16, 1024, 5120], P('prefix', 'resp'), may hold values from -120 to 120
- resp_keys: bfloat16 [16, 1024, 1024], P('prefix', 'resp'), may hold values from -5 to 5
- resp_values: bfloat16 [16, 1024, 1024], P('prefix', 'resp'), may hold values from -5 to 5
- resp_out: bfloat16 [16, 1024, 5120], P('prefix', 'resp'), may hold values from -6 to 6
- resp_grad: bfloat16 [16, 1024, 5120], P('prefix', 'resp'), may hold values from -24 to 24
- prompt_keys: bfloat16 [1024, 1024], P('prefix'), may hold values from -4 to 4
- prompt_values: bfloat16 [1024, 1024], P('prefix'), may hold values from -5 to 5
- resp_lengths: int32 [16], P('prefix'), may hold values from 1 to 1024, 10240 in all
Outputs:
- grad_query: bfloat16 [16, 1024, 5120], P('prefix', 'resp')
- grad_resp_keys: bfloat16 [16, 1024, 1024], P('prefix', 'resp')
- grad_resp_values: bfloat16 [16, 1024, 1024], P('prefix', 'resp')
- grad_prompt_keys: bfloat16 [1024, 1024], P(('prefix', 'resp'))
- grad_prompt_values: bfloat16 [1024, 1024], P(('prefix', 'resp'))
The draws below stay inside these ranges and needn't reach their ends.
Inputs may be any that keep to these rules, and one draw needn't show every extreme that they name: `resp_lengths`: one response fills all 1024 slots.
All inputs are finite; a program needn't handle non-finite values. No bound on the sum of `resp_lengths` on one device may be relied on, other than what follows from the above.
Results may differ from the reference program's by a relative error of at most 0.019.
Values may be sent and summed in bfloat16 or wider, within the bound.
No kernel may reach another device: no remote copies, remote signals or barrier semaphores. Data moves between devices by JAX's collectives and lax.ppermute only.
A program may use at most 192 MiB of HBM per device.

```python
import math
import jax
import jax.numpy as jnp
import numpy as np
from jax import lax

HEADS = 40
KV_HEADS = 8
HEAD_DIM = 128
POS_DEV = 128
LEN = 1024
RESPONSES = 16
PROMPT = 1024


def shared_keys(key):
    return jax.random.truncated_normal(key, -4.0, 4.0, (PROMPT, KV_HEADS * HEAD_DIM), jnp.float32)


def draw_prompt_keys(key, part):
    shared = shared_keys(key)
    return shared.astype(jnp.bfloat16)


def draw_resp_query(key, part):
    key = jax.random.fold_in(key, 9)
    queries = jax.random.truncated_normal(key, -4.0, 4.0, (RESPONSES, LEN, HEADS * HEAD_DIM), jnp.float32)
    return queries.astype(jnp.bfloat16)


def block_levels(stream_key, dims, cuts, low, top_value):
    gain = 1.0
    for dim, shards_of in cuts:
        steps = jax.random.uniform(jax.random.fold_in(jax.random.fold_in(stream_key, 6), dim), (shards_of,), jnp.float32, low / len(cuts), top_value / len(cuts))
        gain = gain * jnp.repeat(jnp.exp(steps), dims[dim] // shards_of).reshape((-1,) + (1,) * (len(dims) - 1 - dim))
    return gain


def length_profile(amount, total, bound, skew):
    portions = [(1 << 20) // math.isqrt(grade ** skew) + 1 for grade in range(2, amount + 1)]
    surplus, given = total - bound - (amount - 1), [1] * (amount - 1)
    while surplus > 0:
        movable = [i for i in range(amount - 1) if given[i] < bound]
        pool, left = sum([portions[i] for i in movable]), surplus
        for i in movable:
            extra = min(bound - given[i], max(1, left * portions[i] // pool), surplus)
            given[i] = given[i] + extra
            surplus = surplus - extra
    return np.array([bound] + given)


def ragged_sizes(rng, amount, total, most, lean):
    if amount == 2:
        one = jax.random.randint(rng, (), max(1, total - most), min(most, total - 1) + 1)
        return jnp.stack([one, total - one])
    tallies = jnp.asarray(length_profile(amount, total, most, lean), jnp.int32)
    twos = (amount - 1) // 2
    source_of, receiver = tallies[1:1 + 2 * twos:2], tallies[2:2 + 2 * twos:2]
    margin = jnp.minimum(source_of - 1, most - receiver)
    shifted = jax.random.randint(jax.random.fold_in(rng, 1), (twos,), 0, 1 << 20) % (margin + 1)
    tallies = tallies.at[1:1 + 2 * twos:2].set(source_of - shifted).at[2:2 + 2 * twos:2].set(receiver + shifted)
    return tallies[jax.random.permutation(jax.random.fold_in(rng, 2), amount)]


def centred(key, extent, width, bound, cuts=(), kind=jnp.bfloat16):
    entries = jax.random.normal(key, extent, jnp.float32) * width
    if len(cuts) > 0:
        entries = block_levels(key, extent, cuts, -0.22, 0.18) * entries
    return jnp.clip(entries, min=-bound, max=bound).astype(kind)


def setup_inputs(seed: int = 0) -> dict:
    seeds = jax.random.split(jax.random.key(seed), 9)
    return {
        "resp_query": draw_resp_query(jax.random.fold_in(seeds[8], 71), 0),
        "resp_keys": centred(seeds[1], (RESPONSES, LEN, KV_HEADS * HEAD_DIM), 1.0, 5.0, ((0, 16), (1, 8))),
        "resp_values": centred(seeds[2], (RESPONSES, LEN, KV_HEADS * HEAD_DIM), 1.0, 5.0, ((0, 16), (1, 8))),
        "resp_out": centred(seeds[3], (RESPONSES, LEN, HEADS * HEAD_DIM), 1.0, 6.0, ((0, 16), (1, 8))),
        "resp_grad": jnp.clip(jax.random.uniform(seeds[4], (RESPONSES, LEN, HEADS * HEAD_DIM), jnp.float32, -24.0, 24.0) * block_levels(seeds[4], (RESPONSES, LEN, HEADS * HEAD_DIM), ((0, 16), (1, 8)), -0.4, 0.0), -24.0, 24.0).astype(jnp.bfloat16),
        "prompt_keys": draw_prompt_keys(jax.random.fold_in(seeds[8], 71), 0),
        "prompt_values": centred(seeds[6], (PROMPT, KV_HEADS * HEAD_DIM), 1.0, 5.0, ((0, 16),)),
        "resp_lengths": ragged_sizes(seeds[7], RESPONSES, RESPONSES * LEN * 5 // 8, LEN, 0).astype(jnp.int32),
    }


def attend(queries, grads, outputs, keys_all, values_all, allowed, live_rows):
    row_count = queries.shape[0]
    key_count = keys_all.shape[0]
    group_size = HEADS // KV_HEADS
    score_scale = HEAD_DIM ** -0.5
    query_heads = queries.astype(jnp.float32).reshape(row_count, KV_HEADS, group_size, HEAD_DIM)
    grad_heads = grads.astype(jnp.float32).reshape(row_count, KV_HEADS, group_size, HEAD_DIM)
    out_heads = outputs.astype(jnp.float32).reshape(row_count, KV_HEADS, group_size, HEAD_DIM)
    key_heads = keys_all.astype(jnp.float32).reshape(key_count, KV_HEADS, HEAD_DIM)
    value_heads = values_all.astype(jnp.float32).reshape(key_count, KV_HEADS, HEAD_DIM)
    scores = jnp.einsum("bkgd,nkd->bkgn", query_heads, key_heads) * score_scale
    scores = jnp.where(allowed[:, None, None, :], scores, -jnp.inf)
    highest = jnp.max(scores, axis=-1, keepdims=True)
    log_total = highest + jnp.log(jnp.sum(jnp.exp(scores - highest), axis=-1, keepdims=True))
    weights = jnp.exp(scores - log_total) * live_rows.astype(jnp.float32)[:, None, None, None]
    weights_low = lax.optimization_barrier(weights.astype(jnp.bfloat16)).astype(jnp.float32)
    grad_dot = jnp.sum(grad_heads * out_heads, axis=-1, keepdims=True)
    weight_grad = jnp.einsum("bkgd,nkd->bkgn", grad_heads, value_heads)
    score_grad = score_scale * weights * (weight_grad - grad_dot)
    score_grad = lax.optimization_barrier(score_grad.astype(jnp.bfloat16)).astype(jnp.float32)
    query_grad = jnp.einsum("bkgn,nkd->bkgd", score_grad, key_heads).reshape(row_count, HEADS * HEAD_DIM)
    key_grad = jnp.einsum("bkgn,bkgd->nkd", score_grad, query_heads).reshape(key_count, KV_HEADS * HEAD_DIM)
    value_grad = jnp.einsum("bkgn,bkgd->nkd", weights_low, grad_heads).reshape(key_count, KV_HEADS * HEAD_DIM)
    return query_grad, key_grad, value_grad


def reference(resp_query, resp_keys, resp_values, resp_out, resp_grad, prompt_keys, prompt_values, resp_lengths):
    block_rows = POS_DEV
    kv_width = KV_HEADS * HEAD_DIM
    key_slot = jnp.arange(LEN, dtype=jnp.int32)

    def one_response(carried, inputs):
        queries, keys_own, values_own, outputs, grads, length = inputs
        keys_all = jnp.concatenate([prompt_keys, keys_own], axis=0)
        values_all = jnp.concatenate([prompt_values, values_own], axis=0)

        def one_block(running, block_index):
            row_start = (block_index * block_rows).astype(jnp.int32)
            slot_index = row_start + jnp.arange(block_rows, dtype=jnp.int32)
            allowed = jnp.concatenate([jnp.ones((block_rows, PROMPT), dtype=jnp.bool_), key_slot[None, :] <= slot_index[:, None]], axis=1)
            pieces = [lax.dynamic_slice_in_dim(source, row_start, block_rows, 0) for source in (queries, grads, outputs)]
            query_grad, key_grad, value_grad = attend(pieces[0], pieces[1], pieces[2], keys_all, values_all, allowed, slot_index < length)
            return (running[0] + key_grad, running[1] + value_grad), query_grad

        empty = jnp.zeros((PROMPT + LEN, kv_width), jnp.float32)
        sums, query_grads = lax.scan(one_block, (empty, empty), jnp.arange(LEN // block_rows, dtype=jnp.int32))
        grad_query = query_grads.reshape(LEN, HEADS * HEAD_DIM).astype(jnp.bfloat16)
        new_carry = (carried[0] + sums[0][:PROMPT], carried[1] + sums[1][:PROMPT])
        return new_carry, (grad_query, sums[0][PROMPT:].astype(jnp.bfloat16), sums[1][PROMPT:].astype(jnp.bfloat16))

    begin = jnp.zeros((PROMPT, kv_width), jnp.float32)
    totals, results = lax.scan(one_response, (begin, begin), (resp_query, resp_keys, resp_values, resp_out, resp_grad, resp_lengths))
    return results[0], results[1], results[2], totals[0].astype(jnp.bfloat16), totals[1].astype(jnp.bfloat16)
```

```python
import jax
import jax.numpy as jnp
from jax import lax
from jax.experimental import pallas as pl
from jax.experimental.pallas import tpu as pltpu
from jax.sharding import PartitionSpec as P

HEADS = 40
KV_HEADS = 8
GROUP = HEADS // KV_HEADS
HEAD_DIM = 128
SCALE = HEAD_DIM ** (-0.5)
EXP2_SCALE = SCALE * 1.4426950408889634
QW = GROUP * HEAD_DIM
KVD = 3 * HEAD_DIM
SEND_W = 2 * QW + KVD
BACK_W = QW + 2 * HEAD_DIM
TILE = 256
WIDE_TILE = 512
VMEM_LIMIT = 56 * 1024 * 1024

NT = (((1,), (1,)), ((), ()))
NN = (((1,), (0,)), ((), ()))


def dot(a, b, dims):
    return lax.dot_general(a, b, dims, preferred_element_type=jnp.float32)


def pack_kernel(q_ref, g_ref, o_ref, k_ref, v_ref, send_ref):
    send_ref[0, :, 0:HEAD_DIM] = k_ref[...]
    send_ref[0, :, HEAD_DIM : 2 * HEAD_DIM] = v_ref[...]
    for j in range(GROUP):
        cols = slice(j * HEAD_DIM, (j + 1) * HEAD_DIM)
        at = KVD + 2 * j * HEAD_DIM
        send_ref[0, :, at : at + HEAD_DIM] = q_ref[:, cols]
        send_ref[0, :, at + HEAD_DIM : at + 2 * HEAD_DIM] = g_ref[:, cols]
    product = g_ref[...].astype(jnp.float32) * o_ref[...].astype(jnp.float32)
    high = product.astype(jnp.bfloat16)
    low = (product - high.astype(jnp.float32)).astype(jnp.bfloat16)
    row = lax.broadcasted_iota(jnp.int32, (QW, HEAD_DIM), 0) // HEAD_DIM
    lane = lax.broadcasted_iota(jnp.int32, (QW, HEAD_DIM), 1)
    mine = (lane >= 3 * row) & (lane < 3 * row + 3)
    ones = jnp.where(mine, 1.0, 0.0).astype(jnp.bfloat16)
    left = dot(high, ones, NN) + dot(low, ones, NN)
    part = lax.broadcasted_iota(jnp.int32, left.shape, 1) % 3
    first = left.astype(jnp.bfloat16).astype(jnp.float32)
    second = (left - first).astype(jnp.bfloat16).astype(jnp.float32)
    third = left - first - second
    deltas = jnp.where(part == 0, first, jnp.where(part == 1, second, third))
    send_ref[0, :, 2 * HEAD_DIM : KVD] = deltas.astype(jnp.bfloat16)


def pack(q, g, o, k, v):
    rows = q.shape[0]
    wide = pl.BlockSpec((rows, QW), lambda h: (0, h))
    thin = pl.BlockSpec((rows, HEAD_DIM), lambda h: (0, h))
    return pl.pallas_call(
        pack_kernel,
        grid=(KV_HEADS,),
        in_specs=[wide, wide, wide, thin, thin],
        out_specs=pl.BlockSpec((1, rows, SEND_W), lambda h: (h, 0, 0)),
        out_shape=jax.ShapeDtypeStruct((KV_HEADS, rows, SEND_W), jnp.bfloat16),
        name="pack",
    )(q, g, o, k, v)


def unpack_kernel(back_ref, q_ref, k_ref, v_ref):
    q_ref[...] = back_ref[0, :, 0:QW]
    k_ref[...] = back_ref[0, :, QW : QW + HEAD_DIM]
    v_ref[...] = back_ref[0, :, QW + HEAD_DIM :]


def unpack(back):
    rows = back.shape[1]
    wide = pl.BlockSpec((rows, QW), lambda h: (0, h))
    thin = pl.BlockSpec((rows, HEAD_DIM), lambda h: (0, h))
    return pl.pallas_call(
        unpack_kernel,
        grid=(KV_HEADS,),
        in_specs=[pl.BlockSpec((1, rows, BACK_W), lambda h: (h, 0, 0))],
        out_specs=[wide, thin, thin],
        out_shape=[
            jax.ShapeDtypeStruct((rows, KV_HEADS * QW), jnp.bfloat16),
            jax.ShapeDtypeStruct((rows, KV_HEADS * HEAD_DIM), jnp.bfloat16),
            jax.ShapeDtypeStruct((rows, KV_HEADS * HEAD_DIM), jnp.bfloat16),
        ],
        name="unpack",
    )(back)


def attend_kernel(
    len_ref, x_ref, pkv_ref, back_ref, pg_ref, k_all, v_all, k_t, qs, gs, e_all, m_all, l_all, p_s, l_s, dq_t, dk, dv
):
    slots = x_ref.shape[0]
    prompt = pkv_ref.shape[0]
    wide = GROUP * TILE
    parts = prompt // WIDE_TILE
    length = len_ref[0]
    k_all[0:prompt] = pkv_ref[:, 0:HEAD_DIM]
    v_all[0:prompt] = pkv_ref[:, HEAD_DIM:]
    k_all[prompt:] = x_ref[:, 0:HEAD_DIM]
    v_all[prompt:] = x_ref[:, HEAD_DIM : 2 * HEAD_DIM]
    for t in range((prompt + slots) // TILE):
        rows = slice(t * TILE, (t + 1) * TILE)
        k_t[:, rows] = k_all[rows].astype(jnp.float32).T.astype(jnp.bfloat16)
    dk[...] = jnp.zeros_like(dk)
    dv[...] = jnp.zeros_like(dv)
    back_ref[...] = jnp.zeros_like(back_ref)

    seen = lax.broadcasted_iota(jnp.int32, (TILE, TILE), 0) <= lax.broadcasted_iota(
        jnp.int32, (TILE, TILE), 1
    )

    def heads(j):
        return slice(j * TILE, (j + 1) * TILE)

    def select(j, size):
        lane = lax.broadcasted_iota(jnp.int32, (size, HEAD_DIM), 1)
        return jnp.where((lane >= 3 * j) & (lane < 3 * j + 3), -1.0, 0.0).astype(jnp.bfloat16)

    def score_tile(rows, size, index, diagonal):
        for j in range(GROUP):
            s = dot(k_all[rows], qs[heads(j)], NT)
            if diagonal:
                s = jnp.where(seen, s, -jnp.inf)
            top = jnp.max(s, axis=0, keepdims=True)
            e = jnp.exp2((s - top) * EXP2_SCALE)
            m_all[pl.ds(index, 1), heads(j)] = top
            l_all[pl.ds(index, 1), heads(j)] = jnp.sum(e, axis=0, keepdims=True)
            e_all[rows, heads(j)] = e

    def grad_tile(rows, size, index, at):
        for j in range(GROUP):
            shifted = dot(
                jnp.concatenate([v_all[rows], select(j, size)], axis=1), gs[heads(j)], NT
            )
            p = e_all[rows, heads(j)] * m_all[pl.ds(index, 1), heads(j)]
            p_s[at : at + size, heads(j)] = p.astype(jnp.bfloat16)
            l_s[at : at + size, heads(j)] = (p * shifted).astype(jnp.bfloat16)

    def grad_sums(rows, size):
        dv[rows] += dot(p_s[0:size], gs[:, 0:HEAD_DIM], NN)
        dk[rows] += dot(l_s[0:size], qs[...], NN)
        return dot(k_t[:, rows], l_s[0:size], NN)

    def slot_block(i, carry):
        here = pl.ds(pl.multiple_of(i * TILE, TILE), TILE)
        for j in range(GROUP):
            at = KVD + 2 * j * HEAD_DIM
            qs[heads(j)] = x_ref[here, at : at + HEAD_DIM]
            gs[heads(j), 0:HEAD_DIM] = x_ref[here, at + HEAD_DIM : at + 2 * HEAD_DIM]
            gs[heads(j), HEAD_DIM:] = x_ref[here, 2 * HEAD_DIM : KVD]

        def own(t):
            return pl.ds(pl.multiple_of(prompt + t * TILE, TILE), TILE)

        for t in range(parts):
            score_tile(slice(t * WIDE_TILE, (t + 1) * WIDE_TILE), WIDE_TILE, t, False)
        score_tile(own(i), TILE, parts + i, True)

        def score_body(t, carry):
            score_tile(own(t), TILE, parts + t, False)
            return carry

        lax.fori_loop(0, i, score_body, 0)

        tile_index = lax.broadcasted_iota(jnp.int32, m_all.shape, 0)
        tops = jnp.where(tile_index <= parts + i, m_all[...], -jnp.inf)
        sums = jnp.where(tile_index <= parts + i, l_all[...], 0.0)
        weight = jnp.exp2((tops - jnp.max(tops, axis=0, keepdims=True)) * EXP2_SCALE)
        total = jnp.sum(weight * sums, axis=0, keepdims=True)
        slot = lax.broadcasted_iota(jnp.int32, (1, wide), 1) % TILE + i * TILE
        live = jnp.where(slot < length, 1.0, 0.0)
        m_all[...] = weight * (live / total)

        for t in range(parts):
            grad_tile(slice(t * WIDE_TILE, (t + 1) * WIDE_TILE), WIDE_TILE, t, t * WIDE_TILE)
        dq_t[...] = grad_sums(slice(0, prompt), prompt)

        def grad_body(t, carry):
            grad_tile(own(t), TILE, parts + t, 0)
            dq_t[...] += grad_sums(own(t), TILE)
            return carry

        lax.fori_loop(0, i + 1, grad_body, 0)
        for j in range(GROUP):
            back_ref[here, j * HEAD_DIM : (j + 1) * HEAD_DIM] = (
                (dq_t[:, heads(j)] * SCALE).T.astype(jnp.bfloat16)
            )
        return carry

    lax.fori_loop(0, lax.div(length + TILE - 1, TILE), slot_block, 0)
    back_ref[:, QW : QW + HEAD_DIM] = (dk[prompt:] * SCALE).astype(jnp.bfloat16)
    back_ref[:, QW + HEAD_DIM :] = dv[prompt:].astype(jnp.bfloat16)
    pg_ref[:, 0:HEAD_DIM] = (dk[0:prompt] * SCALE).astype(jnp.bfloat16)
    pg_ref[:, HEAD_DIM:] = dv[0:prompt].astype(jnp.bfloat16)


def attend(lengths, x, pkv):
    slots = x.shape[0]
    prompt = pkv.shape[0]
    keys = slots + prompt
    wide = GROUP * TILE
    vmem = pl.BlockSpec(memory_space=pltpu.VMEM)
    return pl.pallas_call(
        attend_kernel,
        in_specs=[pl.BlockSpec(memory_space=pltpu.SMEM), vmem, vmem],
        out_specs=[vmem, vmem],
        out_shape=[
            jax.ShapeDtypeStruct((slots, BACK_W), jnp.bfloat16),
            jax.ShapeDtypeStruct((prompt, 2 * HEAD_DIM), jnp.bfloat16),
        ],
        scratch_shapes=[
            pltpu.VMEM((keys, HEAD_DIM), jnp.bfloat16),
            pltpu.VMEM((keys, HEAD_DIM), jnp.bfloat16),
            pltpu.VMEM((HEAD_DIM, keys), jnp.bfloat16),
            pltpu.VMEM((wide, HEAD_DIM), jnp.bfloat16),
            pltpu.VMEM((wide, 2 * HEAD_DIM), jnp.bfloat16),
            pltpu.VMEM((keys, wide), jnp.float32),
            pltpu.VMEM((8, wide), jnp.float32),
            pltpu.VMEM((8, wide), jnp.float32),
            pltpu.VMEM((prompt, wide), jnp.bfloat16),
            pltpu.VMEM((prompt, wide), jnp.bfloat16),
            pltpu.VMEM((HEAD_DIM, wide), jnp.float32),
            pltpu.VMEM((keys, HEAD_DIM), jnp.float32),
            pltpu.VMEM((keys, HEAD_DIM), jnp.float32),
        ],
        compiler_params=pltpu.CompilerParams(vmem_limit_bytes=VMEM_LIMIT),
        name="attend",
    )(lengths, x, pkv)


def local(
    resp_query,
    resp_keys,
    resp_values,
    resp_out,
    resp_grad,
    prompt_keys,
    prompt_values,
    resp_lengths,
):
    head = lax.axis_index("resp")
    cut = lambda a: lax.dynamic_slice_in_dim(a, head * HEAD_DIM, HEAD_DIM, 1)
    pkv = jnp.concatenate([cut(prompt_keys), cut(prompt_values)], axis=1)
    responses = lax.axis_size("prefix")
    part, width = pkv.shape
    copies = jnp.broadcast_to(pkv[None], (responses, part, width))
    send = pack(resp_query[0], resp_grad[0], resp_out[0], resp_keys[0], resp_values[0])
    x = lax.all_to_all(send, "resp", 0, 0, tiled=True)
    rows = x.shape[1]
    pkv = lax.all_to_all(copies, "prefix", 0, 0, tiled=True).reshape(responses * part, width)
    back, pg = attend(resp_lengths, x.reshape(KV_HEADS * rows, SEND_W), pkv)
    pg = lax.all_to_all(pg.reshape(responses, part, width), "prefix", 0, 0, tiled=True)
    back = lax.all_to_all(back.reshape(KV_HEADS, rows, BACK_W), "resp", 0, 0, tiled=True)
    pg = jnp.sum(pg.astype(jnp.float32), axis=0).astype(jnp.bfloat16)
    own = part // KV_HEADS
    pg = lax.all_to_all(pg.reshape(KV_HEADS, own, width), "resp", 0, 0, tiled=True)
    pg = pg.reshape(KV_HEADS, own, 2, HEAD_DIM).transpose(2, 1, 0, 3).reshape(2, own, KV_HEADS * HEAD_DIM)
    grad_query, grad_keys, grad_values = unpack(back)
    return (grad_query[None], grad_keys[None], grad_values[None], pg[0], pg[1])


def solution(mesh):
    return jax.shard_map(
        local,
        mesh=mesh,
        in_specs=(
            P("prefix", "resp", None),
            P("prefix", "resp", None),
            P("prefix", "resp", None),
            P("prefix", "resp", None),
            P("prefix", "resp", None),
            P("prefix", None),
            P("prefix", None),
            P("prefix"),
        ),
        out_specs=(
            P("prefix", "resp", None),
            P("prefix", "resp", None),
            P("prefix", "resp", None),
            P(("prefix", "resp"), None),
            P(("prefix", "resp"), None),
        ),
        check_vma=False,
    )
```

```python
import functools

import jax
import jax.numpy as jnp
from jax import lax
from jax.experimental import pallas as pl
from jax.experimental.pallas import tpu as pltpu
from jax.sharding import PartitionSpec as P

HEADS = 40
KV_HEADS = 8
GROUP = HEADS // KV_HEADS
HEAD_DIM = 128
SCALE = HEAD_DIM ** (-0.5)
EXP2_SCALE = SCALE * 1.4426950408889634
QW = GROUP * HEAD_DIM
KVD = 3 * HEAD_DIM
TILE = 256
WIDE_TILE = 512
PACK_ROWS = 32
CHUNKS = ((0, 1), (2, 3, 4))
GATHER_BITS = (1, 0, 2, 3)

NT = (((1,), (1,)), ((), ()))
NN = (((1,), (0,)), ((), ()))
BF16 = jnp.bfloat16
F32 = jnp.float32
ANY = pl.BlockSpec(memory_space=pl.ANY)
VMEM = pl.BlockSpec(memory_space=pltpu.VMEM)
SMEM = pl.BlockSpec(memory_space=pltpu.SMEM)


def dot(a, b, dims):
    return lax.dot_general(a, b, dims, preferred_element_type=F32)


def params(mib):
    return pltpu.CompilerParams(vmem_limit_bytes=mib * 1024 * 1024)


def times(index, size):
    return pl.multiple_of(index * size, size)


def send_width(chunk):
    return (KVD if chunk == 0 else 0) + 2 * HEAD_DIM * len(CHUNKS[chunk])


def back_width(chunk):
    return (2 * HEAD_DIM if chunk == len(CHUNKS) - 1 else 0) + HEAD_DIM * len(CHUNKS[chunk])


def gather_mask(index):
    return sum(((index >> step) & 1) << bit for step, bit in enumerate(GATHER_BITS))


def pack_kernel(place_ref, q_ref, g_ref, o_ref, k_ref, v_ref, *rest):
    outs, deltas_ref = rest[:-1], rest[-1]
    me = place_ref[1]
    rows = q_ref.shape[0]
    highs, lows = [], []
    for h in range(KV_HEADS):
        wide = slice(h * QW, (h + 1) * QW)
        product = g_ref[:, wide].astype(F32) * o_ref[:, wide].astype(F32)
        high = product.astype(BF16)
        highs.append(high)
        lows.append((product - high.astype(F32)).astype(BF16))
    row = lax.broadcasted_iota(jnp.int32, (QW, HEAD_DIM), 0) // HEAD_DIM
    lane = lax.broadcasted_iota(jnp.int32, (QW, HEAD_DIM), 1)
    ones = jnp.where((lane >= 3 * row) & (lane < 3 * row + 3), 1.0, 0.0).astype(BF16)
    left = dot(jnp.concatenate(highs), ones, NN) + dot(jnp.concatenate(lows), ones, NN)
    part = lax.broadcasted_iota(jnp.int32, left.shape, 1) % 3
    first = left.astype(BF16).astype(F32)
    second = (left - first).astype(BF16).astype(F32)
    third = left - first - second
    deltas = jnp.where(part == 0, first, jnp.where(part == 1, second, third))
    deltas_ref[...] = deltas.astype(BF16)
    for d in range(KV_HEADS):
        h = me ^ d
        for c, chunk in enumerate(CHUNKS):
            out = outs[c * KV_HEADS + d]
            at = 0
            if c == 0:
                thin = pl.ds(times(h, HEAD_DIM), HEAD_DIM)
                out[:, 0:HEAD_DIM] = k_ref[:, thin]
                out[:, HEAD_DIM : 2 * HEAD_DIM] = v_ref[:, thin]
                out[:, 2 * HEAD_DIM : KVD] = deltas_ref[pl.ds(times(h, rows), rows)]
                at = KVD
            size = len(chunk) * HEAD_DIM
            cols = pl.ds(pl.multiple_of(h * QW + chunk[0] * HEAD_DIM, HEAD_DIM), size)
            out[:, at : at + size] = q_ref[:, cols]
            out[:, at + size : at + 2 * size] = g_ref[:, cols]


def pack(place, q, g, o, k, v):
    rows = q.shape[0]
    block = min(PACK_ROWS, rows)
    wide = pl.BlockSpec((block, KV_HEADS * QW), lambda i: (i, 0))
    thin = pl.BlockSpec((block, KV_HEADS * HEAD_DIM), lambda i: (i, 0))
    widths = [send_width(c) for c in range(len(CHUNKS)) for d in range(KV_HEADS)]
    outs = pl.pallas_call(
        pack_kernel,
        grid=(rows // block,),
        in_specs=[SMEM, wide, wide, wide, thin, thin],
        out_specs=[pl.BlockSpec((block, w), lambda i: (i, 0)) for w in widths],
        out_shape=[jax.ShapeDtypeStruct((rows, w), BF16) for w in widths],
        scratch_shapes=[pltpu.VMEM((KV_HEADS * block, HEAD_DIM), BF16)],
        compiler_params=params(60),
        name="pack",
    )(place, q, g, o, k, v)
    return [outs[c * KV_HEADS : (c + 1) * KV_HEADS] for c in range(len(CHUNKS))]


def start_all(copies, sems):
    started = [pltpu.make_async_copy(src, dst, sems.at[n]) for n, (src, dst) in enumerate(copies)]
    for copy in started:
        copy.start()
    return started


def unpack_kernel(place_ref, *refs):
    count = len(CHUNKS) * KV_HEADS
    backs, (q_ref, k_ref, v_ref, sems) = refs[:count], refs[count:]
    me = place_ref[1]
    copies = []
    for c, chunk in enumerate(CHUNKS):
        size = len(chunk) * HEAD_DIM
        for d in range(KV_HEADS):
            back = backs[c * KV_HEADS + d]
            h = me ^ d
            cols = pl.ds(pl.multiple_of(h * QW + chunk[0] * HEAD_DIM, HEAD_DIM), size)
            copies.append((back.at[:, 0:size], q_ref.at[:, cols]))
            if c == len(CHUNKS) - 1:
                thin = pl.ds(times(h, HEAD_DIM), HEAD_DIM)
                copies.append((back.at[:, size : size + HEAD_DIM], k_ref.at[:, thin]))
                copies.append((back.at[:, size + HEAD_DIM :], v_ref.at[:, thin]))
    for copy in start_all(copies, sems):
        copy.wait()


def unpack(place, backs):
    flat = [a for chunk in backs for a in chunk]
    rows = flat[0].shape[0]
    return pl.pallas_call(
        unpack_kernel,
        in_specs=[SMEM] + [ANY] * len(flat),
        out_specs=[ANY] * 3,
        out_shape=[
            jax.ShapeDtypeStruct((rows, KV_HEADS * QW), BF16),
            jax.ShapeDtypeStruct((rows, KV_HEADS * HEAD_DIM), BF16),
            jax.ShapeDtypeStruct((rows, KV_HEADS * HEAD_DIM), BF16),
        ],
        scratch_shapes=[pltpu.SemaphoreType.DMA((len(flat) + 2 * KV_HEADS,))],
        compiler_params=params(4),
        name="unpack",
    )(place, *flat)


def attend_kernel(chunk, prompt, place_ref, *refs):
    refs = list(refs)
    take = lambda n: [refs.pop(0) for _ in range(n)]
    first, last = chunk == 0, chunk == len(CHUNKS) - 1
    heads = CHUNKS[chunk]
    wide = len(heads) * TILE
    size = len(heads) * HEAD_DIM
    x_in = take(KV_HEADS)
    if first:
        (pkv_in,) = take(1)
    else:
        dk_in, dv_in, k_all, v_all, k_t, d_all = take(6)
    back_out = take(KV_HEADS)
    if last:
        pg_out = take(lax.axis_size("prefix"))
    else:
        dk, dv = take(2)
        if first:
            k_all, v_all, k_t, d_all = take(4)
    x_ref, back_ref, in_sems, out_sems, qs, gs, e_all, m_all, l_all, p_s, l_s, dq_t = take(12)
    if last:
        pg_ref, dk, dv = take(3)
        if first:
            k_all, v_all, k_t, d_all = take(4)
    if first:
        (pkv_ref,) = take(1)

    parts = prompt // WIDE_TILE
    slots = x_ref.shape[0]
    length, me, me_prefix = place_ref[0], place_ref[1], place_ref[2]
    rows = slots // KV_HEADS
    at = KVD if first else 0
    copies = [
        (x_in[d], x_ref.at[pl.ds(times(me ^ d, rows), rows)]) for d in range(KV_HEADS)
    ]
    if first:
        sources = pkv_in.shape[0]
        share = prompt // sources
        copies += [
            (pkv_in.at[f], pkv_ref.at[pl.ds(times(me_prefix ^ gather_mask(f), share), share)])
            for f in range(sources)
        ]
    else:
        copies += [(dk_in, dk), (dv_in, dv)]
    copies = start_all(copies, in_sems)
    back_ref[...] = jnp.zeros_like(back_ref)
    if first:
        dk[...] = jnp.zeros_like(dk)
        dv[...] = jnp.zeros_like(dv)
    for copy in copies:
        copy.wait()
    if first:
        k_all[0:prompt] = pkv_ref[:, 0:HEAD_DIM]
        v_all[0:prompt] = pkv_ref[:, HEAD_DIM:]
        k_all[prompt:] = x_ref[:, 0:HEAD_DIM]
        v_all[prompt:] = x_ref[:, HEAD_DIM : 2 * HEAD_DIM]
        d_all[...] = x_ref[:, 2 * HEAD_DIM : KVD]
        for t in range((prompt + slots) // TILE):
            block = slice(t * TILE, (t + 1) * TILE)
            k_t[:, block] = k_all[block].astype(F32).T.astype(BF16)

    seen = lax.broadcasted_iota(jnp.int32, (TILE, TILE), 0) <= lax.broadcasted_iota(
        jnp.int32, (TILE, TILE), 1
    )

    def lanes(j):
        return slice(j * TILE, (j + 1) * TILE)

    def select(head, size):
        lane = lax.broadcasted_iota(jnp.int32, (size, HEAD_DIM), 1)
        return jnp.where((lane >= 3 * head) & (lane < 3 * head + 3), -1.0, 0.0).astype(BF16)

    def score_tile(block, index, diagonal):
        for j in range(len(heads)):
            s = dot(k_all[block], qs[lanes(j)], NT)
            if diagonal:
                s = jnp.where(seen, s, -jnp.inf)
            top = jnp.max(s, axis=0, keepdims=True)
            e = jnp.exp2((s - top) * EXP2_SCALE)
            m_all[pl.ds(index, 1), lanes(j)] = top
            l_all[pl.ds(index, 1), lanes(j)] = jnp.sum(e, axis=0, keepdims=True)
            e_all[block, lanes(j)] = e

    def grad_tile(block, keys, index, at):
        for j, head in enumerate(heads):
            shifted = dot(
                jnp.concatenate([v_all[block], select(head, keys)], axis=1), gs[lanes(j)], NT
            )
            p = e_all[block, lanes(j)] * m_all[pl.ds(index, 1), lanes(j)]
            p_s[at : at + keys, lanes(j)] = p.astype(BF16)
            l_s[at : at + keys, lanes(j)] = (p * shifted).astype(BF16)

    def grad_sums(block, keys):
        dv[block] += dot(p_s[0:keys], gs[:, 0:HEAD_DIM], NN)
        dk[block] += dot(l_s[0:keys], qs[...], NN)
        return dot(k_t[:, block], l_s[0:keys], NN)

    def slot_block(i, carry):
        here = pl.ds(times(i, TILE), TILE)
        for j in range(len(heads)):
            col = at + j * HEAD_DIM
            qs[lanes(j)] = x_ref[here, col : col + HEAD_DIM]
            gs[lanes(j), 0:HEAD_DIM] = x_ref[here, col + size : col + size + HEAD_DIM]
            gs[lanes(j), HEAD_DIM:] = d_all[here]

        def own(t):
            return pl.ds(pl.multiple_of(prompt + t * TILE, TILE), TILE)

        for t in range(parts):
            score_tile(slice(t * WIDE_TILE, (t + 1) * WIDE_TILE), t, False)
        score_tile(own(i), parts + i, True)

        def score_body(t, carry):
            score_tile(own(t), parts + t, False)
            return carry

        lax.fori_loop(0, i, score_body, 0)

        tile_index = lax.broadcasted_iota(jnp.int32, m_all.shape, 0)
        tops = jnp.where(tile_index <= parts + i, m_all[...], -jnp.inf)
        sums = jnp.where(tile_index <= parts + i, l_all[...], 0.0)
        weight = jnp.exp2((tops - jnp.max(tops, axis=0, keepdims=True)) * EXP2_SCALE)
        total = jnp.sum(weight * sums, axis=0, keepdims=True)
        slot = lax.broadcasted_iota(jnp.int32, (1, wide), 1) % TILE + i * TILE
        live = jnp.where(slot < length, 1.0, 0.0)
        m_all[...] = weight * (live / total)

        for t in range(parts):
            grad_tile(slice(t * WIDE_TILE, (t + 1) * WIDE_TILE), WIDE_TILE, t, t * WIDE_TILE)
        dq_t[...] = grad_sums(slice(0, prompt), prompt)

        def grad_body(t, carry):
            grad_tile(own(t), TILE, parts + t, 0)
            dq_t[...] += grad_sums(own(t), TILE)
            return carry

        lax.fori_loop(0, i + 1, grad_body, 0)
        for j in range(len(heads)):
            back_ref[here, j * HEAD_DIM : (j + 1) * HEAD_DIM] = (
                (dq_t[:, lanes(j)] * SCALE).T.astype(BF16)
            )
        return carry

    lax.fori_loop(0, lax.div(length + TILE - 1, TILE), slot_block, 0)
    copies = []
    if last:
        pg_ref[:, 0:HEAD_DIM] = (dk[0:prompt] * SCALE).astype(BF16)
        pg_ref[:, HEAD_DIM:] = dv[0:prompt].astype(BF16)
        share = prompt // len(pg_out)
        copies += [
            (pg_ref.at[pl.ds(times(me_prefix ^ d, share), share)], out)
            for d, out in enumerate(pg_out)
        ]
        back_ref[:, size : size + HEAD_DIM] = (dk[prompt:] * SCALE).astype(BF16)
        back_ref[:, size + HEAD_DIM :] = dv[prompt:].astype(BF16)
    copies += [
        (back_ref.at[pl.ds(times(me ^ d, rows), rows)], back_out[d]) for d in range(KV_HEADS)
    ]
    for copy in start_all(copies, out_sems):
        copy.wait()


def attend(chunk, prompt, place, x, carried):
    first, last = chunk == 0, chunk == len(CHUNKS) - 1
    rows = x[0].shape[0]
    slots = rows * KV_HEADS
    keys = slots + prompt
    wide = len(CHUNKS[chunk]) * TILE
    size = len(CHUNKS[chunk]) * HEAD_DIM
    responses = lax.axis_size("prefix")
    sums = [((keys, HEAD_DIM), F32)] * 2
    shared = [((keys, HEAD_DIM), BF16)] * 2 + [((HEAD_DIM, keys), BF16), ((slots, HEAD_DIM), BF16)]
    outs = [((rows, back_width(chunk)), BF16)] * KV_HEADS
    specs = [ANY] * KV_HEADS
    if last:
        outs += [((prompt // responses, 2 * HEAD_DIM), BF16)] * responses
        specs += [ANY] * responses
    else:
        outs += sums
        specs += [VMEM] * 2
        if first:
            outs += shared
            specs += [VMEM] * 4
    scratch = [
        pltpu.VMEM((slots, send_width(chunk)), BF16),
        pltpu.VMEM((slots, back_width(chunk)), BF16),
        pltpu.SemaphoreType.DMA((KV_HEADS + (responses if first else 2),)),
        pltpu.SemaphoreType.DMA((KV_HEADS + (responses if last else 0),)),
        pltpu.VMEM((wide, HEAD_DIM), BF16),
        pltpu.VMEM((wide, 2 * HEAD_DIM), BF16),
        pltpu.VMEM((keys, wide), F32),
        pltpu.VMEM((8, wide), F32),
        pltpu.VMEM((8, wide), F32),
        pltpu.VMEM((prompt, wide), BF16),
        pltpu.VMEM((prompt, wide), BF16),
        pltpu.VMEM((HEAD_DIM, wide), F32),
    ]
    if last:
        scratch += [pltpu.VMEM((prompt, 2 * HEAD_DIM), BF16)]
        scratch += [pltpu.VMEM(shape, dtype) for shape, dtype in sums]
        if first:
            scratch += [pltpu.VMEM(shape, dtype) for shape, dtype in shared]
    if first:
        scratch += [pltpu.VMEM((prompt, 2 * HEAD_DIM), BF16)]
    carried_specs = [ANY] if first else [ANY] * 2 + [VMEM] * 4
    return pl.pallas_call(
        functools.partial(attend_kernel, chunk, prompt),
        in_specs=[SMEM] + [ANY] * KV_HEADS + carried_specs,
        out_specs=specs,
        out_shape=[jax.ShapeDtypeStruct(shape, dtype) for shape, dtype in outs],
        scratch_shapes=scratch,
        compiler_params=params(40),
        cost_estimate=pl.CostEstimate(
            flops=10 * slots * (prompt + slots) * size, transcendentals=0, bytes_accessed=8 * slots * size
        ),
        name="attend%d" % chunk,
    )(place, *x, *carried)


def sum_kernel(place_ref, *refs):
    parts, outs, total = refs[:-KV_HEADS - 1], refs[-KV_HEADS - 1 : -1], refs[-1]
    value = parts[0][...].astype(F32)
    for part in parts[1:]:
        value = value + part[...].astype(F32)
    total[...] = value
    own = outs[0].shape[0]
    for d, out in enumerate(outs):
        out[...] = total[pl.ds(times(place_ref[1] ^ d, own), own)]


def sum_parts(place, parts):
    rows, width = parts[0].shape
    own = rows // KV_HEADS
    return pl.pallas_call(
        sum_kernel,
        in_specs=[SMEM] + [VMEM] * len(parts),
        out_specs=[VMEM] * KV_HEADS,
        out_shape=[jax.ShapeDtypeStruct((own, width), F32)] * KV_HEADS,
        scratch_shapes=[pltpu.VMEM((rows, width), F32)],
        compiler_params=params(4),
        name="sum_parts",
    )(place, *parts)


def spread_kernel(place_ref, *refs):
    parts, (k_ref, v_ref) = refs[:KV_HEADS], refs[KV_HEADS:]
    for d, part in enumerate(parts):
        cols = pl.ds(times(place_ref[1] ^ d, HEAD_DIM), HEAD_DIM)
        k_ref[:, cols] = part[:, 0:HEAD_DIM]
        v_ref[:, cols] = part[:, HEAD_DIM:]


def spread_heads(place, parts):
    shape = jax.ShapeDtypeStruct((parts[0].shape[0], KV_HEADS * HEAD_DIM), F32)
    return pl.pallas_call(
        spread_kernel,
        in_specs=[SMEM] + [VMEM] * KV_HEADS,
        out_specs=[VMEM] * 2,
        out_shape=[shape] * 2,
        compiler_params=params(4),
        name="spread_heads",
    )(place, *parts)


def swap(value, axis, d):
    return lax.ppermute(value, axis, [(i, i ^ d) for i in range(lax.axis_size(axis))])


def swap_all(values, axis):
    return [values[0]] + [swap(values[d], axis, d) for d in range(1, len(values))]


def gather_prompt(value):
    value = value[None]
    for bit in GATHER_BITS:
        value = jnp.concatenate([value, swap(value, "prefix", 1 << bit)])
    return value


def local(
    resp_query,
    resp_keys,
    resp_values,
    resp_out,
    resp_grad,
    prompt_keys,
    prompt_values,
    resp_lengths,
):
    head = lax.axis_index("resp")
    prompt = prompt_keys.shape[0] * lax.axis_size("prefix")
    place = jnp.stack([resp_lengths[0], head, lax.axis_index("prefix")])
    cut = lambda a: lax.dynamic_slice_in_dim(a, head * HEAD_DIM, HEAD_DIM, 1)
    pkv = gather_prompt(jnp.concatenate([cut(prompt_keys), cut(prompt_values)], axis=1))
    sends = pack(place, resp_query[0], resp_grad[0], resp_out[0], resp_keys[0], resp_values[0])
    arrived = [swap_all(send, "resp") for send in sends]
    carried = [pkv]
    shared = []
    backs = []
    for chunk, x in enumerate(arrived):
        outs = attend(chunk, prompt, place, x, carried)
        back, outs = outs[:KV_HEADS], outs[KV_HEADS:]
        if chunk == len(CHUNKS) - 1:
            pg = swap_all(outs, "prefix")
        else:
            shared = shared or outs[2:]
            carried = outs[:2] + shared
        backs.append(swap_all(back, "resp"))
    pg = spread_heads(place, swap_all(sum_parts(place, pg), "resp"))
    grad_query, grad_keys, grad_values = unpack(place, backs)
    return (
        grad_query[None],
        grad_keys[None],
        grad_values[None],
        pg[0].astype(BF16),
        pg[1].astype(BF16),
    )


def solution(mesh):
    return jax.shard_map(
        local,
        mesh=mesh,
        in_specs=(
            P("prefix", "resp", None),
            P("prefix", "resp", None),
            P("prefix", "resp", None),
            P("prefix", "resp", None),
            P("prefix", "resp", None),
            P("prefix", None),
            P("prefix", None),
            P("prefix"),
        ),
        out_specs=(
            P("prefix", "resp", None),
            P("prefix", "resp", None),
            P("prefix", "resp", None),
            P(("prefix", "resp"), None),
            P(("prefix", "resp"), None),
        ),
        check_vma=False,
    )
```

```python
import jax
import jax.numpy as jnp
from jax import lax
from jax.experimental import pallas as pl
from jax.experimental.pallas import tpu as pltpu
from jax.sharding import PartitionSpec as P

HEADS = 40
KV_HEADS = 8
GROUP = HEADS // KV_HEADS
HEAD_DIM = 128
SCALE = HEAD_DIM ** (-0.5)
EXP2_SCALE = SCALE * 1.4426950408889634
QW = GROUP * HEAD_DIM
KVD = 3 * HEAD_DIM
TILE = 256
WIDE_TILE = 512
PACK_ROWS = 32
GATHER_BITS = (1, 0, 2, 3)
SEND_W = KVD + 2 * QW
BACK_W = QW + 2 * HEAD_DIM
NEAR = 4

NT = (((1,), (1,)), ((), ()))
NN = (((1,), (0,)), ((), ()))
BF16 = jnp.bfloat16
F32 = jnp.float32
ANY = pl.BlockSpec(memory_space=pl.ANY)
VMEM = pl.BlockSpec(memory_space=pltpu.VMEM)
SMEM = pl.BlockSpec(memory_space=pltpu.SMEM)


def dot(a, b, dims):
    return lax.dot_general(a, b, dims, preferred_element_type=F32)


def params(mib):
    return pltpu.CompilerParams(vmem_limit_bytes=mib * 1024 * 1024)


def times(index, size):
    return pl.multiple_of(index * size, size)


def gather_mask(index):
    return sum(((index >> step) & 1) << bit for step, bit in enumerate(GATHER_BITS))


def pack_kernel(q_ref, g_ref, o_ref, k_ref, v_ref, send_ref):
    rows = q_ref.shape[0]
    highs, lows = [], []
    for h in range(KV_HEADS):
        thin = slice(h * HEAD_DIM, (h + 1) * HEAD_DIM)
        wide = slice(h * QW, (h + 1) * QW)
        send_ref[h, :, 0:HEAD_DIM] = k_ref[:, thin]
        send_ref[h, :, HEAD_DIM : 2 * HEAD_DIM] = v_ref[:, thin]
        send_ref[h, :, KVD : KVD + QW] = q_ref[:, wide]
        send_ref[h, :, KVD + QW :] = g_ref[:, wide]
        product = g_ref[:, wide].astype(F32) * o_ref[:, wide].astype(F32)
        high = product.astype(BF16)
        highs.append(high)
        lows.append((product - high.astype(F32)).astype(BF16))
    row = lax.broadcasted_iota(jnp.int32, (QW, HEAD_DIM), 0) // HEAD_DIM
    lane = lax.broadcasted_iota(jnp.int32, (QW, HEAD_DIM), 1)
    ones = jnp.where((lane >= 3 * row) & (lane < 3 * row + 3), 1.0, 0.0).astype(BF16)
    left = dot(jnp.concatenate(highs), ones, NN) + dot(jnp.concatenate(lows), ones, NN)
    part = lax.broadcasted_iota(jnp.int32, left.shape, 1) % 3
    first = left.astype(BF16).astype(F32)
    second = (left - first).astype(BF16).astype(F32)
    third = left - first - second
    deltas = jnp.where(part == 0, first, jnp.where(part == 1, second, third)).astype(BF16)
    for h in range(KV_HEADS):
        send_ref[h, :, 2 * HEAD_DIM : KVD] = deltas[h * rows : (h + 1) * rows]


def pack(q, g, o, k, v):
    rows = q.shape[0]
    block = min(PACK_ROWS, rows)
    wide = pl.BlockSpec((block, KV_HEADS * QW), lambda i: (i, 0))
    thin = pl.BlockSpec((block, KV_HEADS * HEAD_DIM), lambda i: (i, 0))
    return pl.pallas_call(
        pack_kernel,
        grid=(rows // block,),
        in_specs=[wide, wide, wide, thin, thin],
        out_specs=pl.BlockSpec((KV_HEADS, block, SEND_W), lambda i: (0, i, 0)),
        out_shape=jax.ShapeDtypeStruct((KV_HEADS, rows, SEND_W), BF16),
        compiler_params=params(60),
        name="pack",
    )(q, g, o, k, v)


def start_all(copies, sems):
    started = [pltpu.make_async_copy(src, dst, sems.at[n]) for n, (src, dst) in enumerate(copies)]
    for copy in started:
        copy.start()
    return started


def unpack_kernel(back_ref, q_ref, k_ref, v_ref, sems):
    copies = []
    for h in range(KV_HEADS):
        thin = slice(h * HEAD_DIM, (h + 1) * HEAD_DIM)
        wide = slice(h * QW, (h + 1) * QW)
        copies.append((back_ref.at[h, :, 0:QW], q_ref.at[:, wide]))
        copies.append((back_ref.at[h, :, QW : QW + HEAD_DIM], k_ref.at[:, thin]))
        copies.append((back_ref.at[h, :, QW + HEAD_DIM :], v_ref.at[:, thin]))
    for copy in start_all(copies, sems):
        copy.wait()


def unpack(back):
    rows = back.shape[1]
    return pl.pallas_call(
        unpack_kernel,
        in_specs=[ANY],
        out_specs=[ANY] * 3,
        out_shape=[
            jax.ShapeDtypeStruct((rows, KV_HEADS * QW), BF16),
            jax.ShapeDtypeStruct((rows, KV_HEADS * HEAD_DIM), BF16),
            jax.ShapeDtypeStruct((rows, KV_HEADS * HEAD_DIM), BF16),
        ],
        scratch_shapes=[pltpu.SemaphoreType.DMA((3 * KV_HEADS,))],
        compiler_params=params(4),
        name="unpack",
    )(back)


def attend_kernel(place_ref, x_in, pkv_in, back_out, *refs):
    pg_out, refs = refs[:NEAR], refs[NEAR:]
    x_ref, pkv_ref, back_ref, pg_ref, sems, k_all, v_all, k_t, d_all, qs, gs = refs[:11]
    e_all, m_all, l_all, p_s, l_s, dq_t, dk, dv = refs[11:]
    prompt = pkv_ref.shape[0]
    slots = x_ref.shape[0]
    wide = GROUP * TILE
    heads, size, at = range(GROUP), QW, KVD
    parts = prompt // WIDE_TILE
    length, me_prefix = place_ref[0], place_ref[1]
    sources = pkv_in.shape[0]
    share = prompt // sources
    copies = [(x_in, x_ref)] + [
        (pkv_in.at[f], pkv_ref.at[pl.ds(times(me_prefix ^ gather_mask(f), share), share)])
        for f in range(sources)
    ]
    copies = start_all(copies, sems)
    back_ref[...] = jnp.zeros_like(back_ref)
    dk[...] = jnp.zeros_like(dk)
    dv[...] = jnp.zeros_like(dv)
    for copy in copies:
        copy.wait()
    k_all[0:prompt] = pkv_ref[:, 0:HEAD_DIM]
    v_all[0:prompt] = pkv_ref[:, HEAD_DIM:]
    k_all[prompt:] = x_ref[:, 0:HEAD_DIM]
    v_all[prompt:] = x_ref[:, HEAD_DIM : 2 * HEAD_DIM]
    d_all[...] = x_ref[:, 2 * HEAD_DIM : KVD]
    for t in range((prompt + slots) // TILE):
        block = slice(t * TILE, (t + 1) * TILE)
        k_t[:, block] = k_all[block].astype(F32).T.astype(BF16)

    seen = lax.broadcasted_iota(jnp.int32, (TILE, TILE), 0) <= lax.broadcasted_iota(
        jnp.int32, (TILE, TILE), 1
    )

    def lanes(j):
        return slice(j * TILE, (j + 1) * TILE)

    def select(j, size):
        lane = lax.broadcasted_iota(jnp.int32, (size, HEAD_DIM), 1)
        return jnp.where((lane >= 3 * j) & (lane < 3 * j + 3), -1.0, 0.0).astype(BF16)

    def score_tile(block, index, diagonal):
        for j in heads:
            s = dot(k_all[block], qs[lanes(j)], NT)
            if diagonal:
                s = jnp.where(seen, s, -jnp.inf)
            top = jnp.max(s, axis=0, keepdims=True)
            e = jnp.exp2((s - top) * EXP2_SCALE)
            m_all[pl.ds(index, 1), lanes(j)] = top
            l_all[pl.ds(index, 1), lanes(j)] = jnp.sum(e, axis=0, keepdims=True)
            e_all[block, lanes(j)] = e

    def grad_tile(block, keys, index, at):
        for j in heads:
            shifted = dot(
                jnp.concatenate([v_all[block], select(j, keys)], axis=1), gs[lanes(j)], NT
            )
            p = e_all[block, lanes(j)] * m_all[pl.ds(index, 1), lanes(j)]
            p_s[at : at + keys, lanes(j)] = p.astype(BF16)
            l_s[at : at + keys, lanes(j)] = (p * shifted).astype(BF16)

    def grad_sums(block, keys):
        dv[block] += dot(p_s[0:keys], gs[:, 0:HEAD_DIM], NN)
        dk[block] += dot(l_s[0:keys], qs[...], NN)
        return dot(k_t[:, block], l_s[0:keys], NN)

    def slot_block(i, carry):
        here = pl.ds(times(i, TILE), TILE)
        for j in heads:
            col = at + j * HEAD_DIM
            qs[lanes(j)] = x_ref[here, col : col + HEAD_DIM]
            gs[lanes(j), 0:HEAD_DIM] = x_ref[here, col + size : col + size + HEAD_DIM]
            gs[lanes(j), HEAD_DIM:] = d_all[here]

        def own(t):
            return pl.ds(pl.multiple_of(prompt + t * TILE, TILE), TILE)

        for t in range(parts):
            score_tile(slice(t * WIDE_TILE, (t + 1) * WIDE_TILE), t, False)
        score_tile(own(i), parts + i, True)

        def score_body(t, carry):
            score_tile(own(t), parts + t, False)
            return carry

        lax.fori_loop(0, i, score_body, 0)

        tile_index = lax.broadcasted_iota(jnp.int32, m_all.shape, 0)
        tops = jnp.where(tile_index <= parts + i, m_all[...], -jnp.inf)
        sums = jnp.where(tile_index <= parts + i, l_all[...], 0.0)
        weight = jnp.exp2((tops - jnp.max(tops, axis=0, keepdims=True)) * EXP2_SCALE)
        total = jnp.sum(weight * sums, axis=0, keepdims=True)
        slot = lax.broadcasted_iota(jnp.int32, (1, wide), 1) % TILE + i * TILE
        live = jnp.where(slot < length, 1.0, 0.0)
        m_all[...] = weight * (live / total)

        for t in range(parts):
            grad_tile(slice(t * WIDE_TILE, (t + 1) * WIDE_TILE), WIDE_TILE, t, t * WIDE_TILE)
        dq_t[...] = grad_sums(slice(0, prompt), prompt)

        def grad_body(t, carry):
            grad_tile(own(t), TILE, parts + t, 0)
            dq_t[...] += grad_sums(own(t), TILE)
            return carry

        lax.fori_loop(0, i + 1, grad_body, 0)
        for j in heads:
            back_ref[here, j * HEAD_DIM : (j + 1) * HEAD_DIM] = (
                (dq_t[:, lanes(j)] * SCALE).T.astype(BF16)
            )
        return carry

    lax.fori_loop(0, lax.div(length + TILE - 1, TILE), slot_block, 0)
    pg_ref[:, 0:HEAD_DIM] = (dk[0:prompt] * SCALE).astype(BF16)
    pg_ref[:, HEAD_DIM:] = dv[0:prompt].astype(BF16)
    back_ref[:, size : size + HEAD_DIM] = (dk[prompt:] * SCALE).astype(BF16)
    back_ref[:, size + HEAD_DIM :] = dv[prompt:].astype(BF16)
    near = me_prefix % NEAR
    copies = [
        (pg_ref.at[pl.ds(times(far * NEAR + (near ^ d), share), share)], out.at[far])
        for d, out in enumerate(pg_out)
        for far in range(sources // NEAR)
    ]
    for copy in start_all([(back_ref, back_out)] + copies, sems):
        copy.wait()


def attend(place, x, pkv):
    slots, width = x.shape
    responses, share, prompt_width = pkv.shape
    prompt = responses * share
    keys = slots + prompt
    wide = GROUP * TILE
    part = ((responses // NEAR, share, prompt_width), BF16)
    outs = [((slots, BACK_W), BF16)] + [part] * NEAR
    return pl.pallas_call(
        attend_kernel,
        in_specs=[SMEM, ANY, ANY],
        out_specs=[ANY] * len(outs),
        out_shape=[jax.ShapeDtypeStruct(shape, dtype) for shape, dtype in outs],
        scratch_shapes=[
            pltpu.VMEM((slots, width), BF16),
            pltpu.VMEM((prompt, prompt_width), BF16),
            pltpu.VMEM((slots, BACK_W), BF16),
            pltpu.VMEM((prompt, prompt_width), BF16),
            pltpu.SemaphoreType.DMA((1 + responses,)),
            pltpu.VMEM((keys, HEAD_DIM), BF16),
            pltpu.VMEM((keys, HEAD_DIM), BF16),
            pltpu.VMEM((HEAD_DIM, keys), BF16),
            pltpu.VMEM((slots, HEAD_DIM), BF16),
            pltpu.VMEM((wide, HEAD_DIM), BF16),
            pltpu.VMEM((wide, 2 * HEAD_DIM), BF16),
            pltpu.VMEM((keys, wide), F32),
            pltpu.VMEM((8, wide), F32),
            pltpu.VMEM((8, wide), F32),
            pltpu.VMEM((prompt, wide), BF16),
            pltpu.VMEM((prompt, wide), BF16),
            pltpu.VMEM((HEAD_DIM, wide), F32),
            pltpu.VMEM((keys, HEAD_DIM), F32),
            pltpu.VMEM((keys, HEAD_DIM), F32),
        ],
        compiler_params=params(44),
        cost_estimate=pl.CostEstimate(
            flops=10 * slots * keys * QW, transcendentals=0, bytes_accessed=8 * slots * QW
        ),
        name="attend",
    )(place, x, pkv)


def near_kernel(place_ref, *refs):
    parts, outs, total = refs[:NEAR], refs[NEAR:-1], refs[-1]
    value = parts[0][...].astype(F32)
    for part in parts[1:]:
        value = value + part[...].astype(F32)
    total[...] = value
    for d, out in enumerate(outs):
        out[...] = total[(place_ref[1] // NEAR) ^ d]


def sum_near(place, parts):
    far, share, width = parts[0].shape
    return pl.pallas_call(
        near_kernel,
        in_specs=[SMEM] + [VMEM] * NEAR,
        out_specs=[VMEM] * far,
        out_shape=[jax.ShapeDtypeStruct((share, width), F32)] * far,
        scratch_shapes=[pltpu.VMEM((far, share, width), F32)],
        compiler_params=params(4),
        cost_estimate=pl.CostEstimate(flops=5 * 10**10, transcendentals=0, bytes_accessed=2**20),
        name="sum_near",
    )(place, *parts)


def swap(value, axis, d):
    return lax.ppermute(value, axis, [(i, i ^ d) for i in range(lax.axis_size(axis))])


def local(
    resp_query,
    resp_keys,
    resp_values,
    resp_out,
    resp_grad,
    prompt_keys,
    prompt_values,
    resp_lengths,
):
    head = lax.axis_index("resp")
    responses = lax.axis_size("prefix")
    rows = resp_query.shape[1]
    place = jnp.stack([resp_lengths[0], lax.axis_index("prefix")])
    cut = lambda a: lax.dynamic_slice_in_dim(a, head * HEAD_DIM, HEAD_DIM, 1)
    pkv = jnp.concatenate([cut(prompt_keys), cut(prompt_values)], axis=1)[None]
    first = swap(pkv, "prefix", 1 << GATHER_BITS[0])
    send = pack(resp_query[0], resp_grad[0], resp_out[0], resp_keys[0], resp_values[0])
    x = lax.all_to_all(send, "resp", 0, 0, tiled=True)
    pkv, first, _ = lax.optimization_barrier((pkv, first, send))
    pkv = jnp.concatenate([pkv, first])
    for bit in GATHER_BITS[1:]:
        pkv = jnp.concatenate([pkv, swap(pkv, "prefix", 1 << bit)])
    outs = attend(place, x.reshape(KV_HEADS * rows, SEND_W), pkv)
    back, parts = outs[0], outs[1:]
    back = lax.all_to_all(back.reshape(KV_HEADS, rows, BACK_W), "resp", 0, 0, tiled=True)
    parts = [parts[0]] + [swap(parts[d], "prefix", d) for d in range(1, NEAR)]
    parts = sum_near(place, parts)
    parts = [parts[0]] + [swap(parts[d], "prefix", NEAR * d) for d in range(1, len(parts))]
    share, width = parts[0].shape
    total = sum(parts[1:], parts[0]).astype(BF16).reshape(KV_HEADS, share // KV_HEADS, width)
    back, total = lax.optimization_barrier((back, total))
    total = lax.all_to_all(total, "resp", 0, 0, tiled=True)
    total = total.reshape(KV_HEADS, share // KV_HEADS, 2, HEAD_DIM).transpose(2, 1, 0, 3)
    total = total.reshape(2, share // KV_HEADS, KV_HEADS * HEAD_DIM)
    grad_query, grad_keys, grad_values = unpack(back)
    return (grad_query[None], grad_keys[None], grad_values[None], total[0], total[1])


def solution(mesh):
    return jax.shard_map(
        local,
        mesh=mesh,
        in_specs=(
            P("prefix", "resp", None),
            P("prefix", "resp", None),
            P("prefix", "resp", None),
            P("prefix", "resp", None),
            P("prefix", "resp", None),
            P("prefix", None),
            P("prefix", None),
            P("prefix"),
        ),
        out_specs=(
            P("prefix", "resp", None),
            P("prefix", "resp", None),
            P("prefix", "resp", None),
            P(("prefix", "resp"), None),
            P(("prefix", "resp"), None),
        ),
        check_vma=False,
    )
```

```python
import jax
import jax.numpy as jnp
from jax import lax
from jax.experimental import pallas as pl
from jax.experimental.pallas import tpu as pltpu
from jax.sharding import PartitionSpec as P

HEADS = 40
KV_HEADS = 8
GROUP = HEADS // KV_HEADS
HEAD_DIM = 128
SCALE = HEAD_DIM ** (-0.5)
EXP2_SCALE = SCALE * 1.4426950408889634
QW = GROUP * HEAD_DIM
KVD = 3 * HEAD_DIM
TILE = 256
WIDE_TILE = 512
PACK_ROWS = 32
GATHER_BITS = (1, 0, 2, 3)
SEND_W = KVD + 2 * QW
BACK_W = QW + 2 * HEAD_DIM
NEAR = 4

NN = (((1,), (0,)), ((), ()))
BF16 = jnp.bfloat16
F32 = jnp.float32
ANY = pl.BlockSpec(memory_space=pl.ANY)
HBM = pl.BlockSpec(memory_space=pltpu.HBM)
VMEM = pl.BlockSpec(memory_space=pltpu.VMEM)
SMEM = pl.BlockSpec(memory_space=pltpu.SMEM)


def dot(a, b, dims):
    return lax.dot_general(a, b, dims, preferred_element_type=F32)


def params(mib):
    return pltpu.CompilerParams(vmem_limit_bytes=mib * 1024 * 1024)


def times(index, size):
    return pl.multiple_of(index * size, size)


def gather_mask(index):
    return sum(((index >> step) & 1) << bit for step, bit in enumerate(GATHER_BITS))


def pack_kernel(q_ref, g_ref, o_ref, k_ref, v_ref, send_ref):
    rows = q_ref.shape[0]
    highs, lows = [], []
    for h in range(KV_HEADS):
        thin = slice(h * HEAD_DIM, (h + 1) * HEAD_DIM)
        wide = slice(h * QW, (h + 1) * QW)
        send_ref[h, :, 0:HEAD_DIM] = k_ref[:, thin]
        send_ref[h, :, HEAD_DIM : 2 * HEAD_DIM] = v_ref[:, thin]
        send_ref[h, :, KVD : KVD + QW] = q_ref[:, wide]
        send_ref[h, :, KVD + QW :] = g_ref[:, wide]
        product = g_ref[:, wide].astype(F32) * o_ref[:, wide].astype(F32)
        high = product.astype(BF16)
        highs.append(high)
        lows.append((product - high.astype(F32)).astype(BF16))
    row = lax.broadcasted_iota(jnp.int32, (QW, HEAD_DIM), 0) // HEAD_DIM
    lane = lax.broadcasted_iota(jnp.int32, (QW, HEAD_DIM), 1)
    ones = jnp.where((lane >= 3 * row) & (lane < 3 * row + 3), 1.0, 0.0).astype(BF16)
    left = dot(jnp.concatenate(highs), ones, NN) + dot(jnp.concatenate(lows), ones, NN)
    part = lax.broadcasted_iota(jnp.int32, left.shape, 1) % 3
    first = left.astype(BF16).astype(F32)
    second = (left - first).astype(BF16).astype(F32)
    third = left - first - second
    deltas = jnp.where(part == 0, first, jnp.where(part == 1, second, third)).astype(BF16)
    for h in range(KV_HEADS):
        send_ref[h, :, 2 * HEAD_DIM : KVD] = deltas[h * rows : (h + 1) * rows]


def pack(q, g, o, k, v):
    rows = q.shape[0]
    block = min(PACK_ROWS, rows)
    wide = pl.BlockSpec((block, KV_HEADS * QW), lambda i: (i, 0))
    thin = pl.BlockSpec((block, KV_HEADS * HEAD_DIM), lambda i: (i, 0))
    return pl.pallas_call(
        pack_kernel,
        grid=(rows // block,),
        in_specs=[wide, wide, wide, thin, thin],
        out_specs=pl.BlockSpec((KV_HEADS, block, SEND_W), lambda i: (0, i, 0)),
        out_shape=jax.ShapeDtypeStruct((KV_HEADS, rows, SEND_W), BF16),
        compiler_params=params(60),
        cost_estimate=pl.CostEstimate(flops=10**10, transcendentals=0, bytes_accessed=2**23),
        name="pack",
    )(q, g, o, k, v)


def start_all(copies, sems):
    started = [pltpu.make_async_copy(src, dst, sems.at[n]) for n, (src, dst) in enumerate(copies)]
    for copy in started:
        copy.start()
    return started


def unpack_kernel(back_ref, q_ref, k_ref, v_ref, sems):
    copies = []
    for h in range(KV_HEADS):
        thin = slice(h * HEAD_DIM, (h + 1) * HEAD_DIM)
        wide = slice(h * QW, (h + 1) * QW)
        copies.append((back_ref.at[h, :, 0:QW], q_ref.at[:, wide]))
        copies.append((back_ref.at[h, :, QW : QW + HEAD_DIM], k_ref.at[:, thin]))
        copies.append((back_ref.at[h, :, QW + HEAD_DIM :], v_ref.at[:, thin]))
    for copy in start_all(copies, sems):
        copy.wait()


def unpack(back):
    rows = back.shape[1]
    return pl.pallas_call(
        unpack_kernel,
        in_specs=[ANY],
        out_specs=[ANY] * 3,
        out_shape=[
            jax.ShapeDtypeStruct((rows, KV_HEADS * QW), BF16),
            jax.ShapeDtypeStruct((rows, KV_HEADS * HEAD_DIM), BF16),
            jax.ShapeDtypeStruct((rows, KV_HEADS * HEAD_DIM), BF16),
        ],
        scratch_shapes=[pltpu.SemaphoreType.DMA((3 * KV_HEADS,))],
        compiler_params=params(4),
        name="unpack",
    )(back)


def attend_kernel(place_ref, x_in, pkv_low, pkv_high, back_out, *refs):
    pg_out, refs = refs[:NEAR], refs[NEAR:]
    x_ref, pkv_ref, back_ref, pg_ref, sems, k_all, v_all, k_t, d_all, qs, gs, qs_t, gs_t = refs[:13]
    e_all, m_all, l_all, p_s, l_s, dq_t, dk, dv = refs[13:]
    prompt = pkv_ref.shape[0]
    slots = x_ref.shape[0]
    wide = GROUP * TILE
    heads, size, at = range(GROUP), QW, KVD
    parts = prompt // WIDE_TILE
    length, me_prefix = place_ref[0], place_ref[1]
    half = pkv_low.shape[0]
    sources = 2 * half
    share = prompt // sources
    copies = [(x_in, x_ref)] + [
        ((pkv_low, pkv_high)[f // half].at[f % half], pkv_ref.at[pl.ds(times(me_prefix ^ gather_mask(f), share), share)])
        for f in range(sources)
    ]
    copies = start_all(copies, sems)
    back_ref[...] = jnp.zeros_like(back_ref)
    dk[...] = jnp.zeros_like(dk)
    dv[...] = jnp.zeros_like(dv)
    for copy in copies:
        copy.wait()
    k_all[0:prompt] = pkv_ref[:, 0:HEAD_DIM]
    v_all[0:prompt] = pkv_ref[:, HEAD_DIM:]
    k_all[prompt:] = x_ref[:, 0:HEAD_DIM]
    v_all[prompt:] = x_ref[:, HEAD_DIM : 2 * HEAD_DIM]
    d_all[...] = x_ref[:, 2 * HEAD_DIM : KVD]
    for t in range((prompt + slots) // TILE):
        block = slice(t * TILE, (t + 1) * TILE)
        k_t[:, block] = k_all[block].astype(F32).T.astype(BF16)

    seen = lax.broadcasted_iota(jnp.int32, (TILE, TILE), 0) <= lax.broadcasted_iota(
        jnp.int32, (TILE, TILE), 1
    )

    def flip(a):
        return a.astype(F32).T.astype(BF16)

    def lanes(j):
        return slice(j * TILE, (j + 1) * TILE)

    def select(j, size):
        lane = lax.broadcasted_iota(jnp.int32, (size, HEAD_DIM), 1)
        return jnp.where((lane >= 3 * j) & (lane < 3 * j + 3), -1.0, 0.0).astype(BF16)

    def score_tile(block, index, diagonal):
        for j in heads:
            s = dot(k_all[block], qs_t[:, lanes(j)], NN)
            if diagonal:
                s = jnp.where(seen, s, -jnp.inf)
            top = jnp.max(s, axis=0, keepdims=True)
            e = jnp.exp2((s - top) * EXP2_SCALE)
            m_all[pl.ds(index, 1), lanes(j)] = top
            l_all[pl.ds(index, 1), lanes(j)] = jnp.sum(e, axis=0, keepdims=True)
            e_all[block, lanes(j)] = e

    def grad_tile(block, keys, index, at):
        for j in heads:
            shifted = dot(
                jnp.concatenate([v_all[block], select(j, keys)], axis=1), gs_t[:, lanes(j)], NN
            )
            p = e_all[block, lanes(j)] * m_all[pl.ds(index, 1), lanes(j)]
            p_s[at : at + keys, lanes(j)] = p.astype(BF16)
            l_s[at : at + keys, lanes(j)] = (p * shifted).astype(BF16)

    def grad_sums(block, keys):
        dv[block] += dot(p_s[0:keys], gs[...], NN)
        dk[block] += dot(l_s[0:keys], qs[...], NN)
        return dot(k_t[:, block], l_s[0:keys], NN)

    def slot_block(i, carry):
        here = pl.ds(times(i, TILE), TILE)
        delta_t = flip(d_all[here])
        for j in heads:
            col = at + j * HEAD_DIM
            q = x_ref[here, col : col + HEAD_DIM]
            g = x_ref[here, col + size : col + size + HEAD_DIM]
            qs[lanes(j)] = q
            gs[lanes(j)] = g
            qs_t[:, lanes(j)] = flip(q)
            gs_t[0:HEAD_DIM, lanes(j)] = flip(g)
            gs_t[HEAD_DIM:, lanes(j)] = delta_t

        def own(t):
            return pl.ds(pl.multiple_of(prompt + t * TILE, TILE), TILE)

        for t in range(parts):
            score_tile(slice(t * WIDE_TILE, (t + 1) * WIDE_TILE), t, False)
        score_tile(own(i), parts + i, True)

        def score_body(t, carry):
            score_tile(own(t), parts + t, False)
            return carry

        lax.fori_loop(0, i, score_body, 0)

        tile_index = lax.broadcasted_iota(jnp.int32, m_all.shape, 0)
        tops = jnp.where(tile_index <= parts + i, m_all[...], -jnp.inf)
        sums = jnp.where(tile_index <= parts + i, l_all[...], 0.0)
        weight = jnp.exp2((tops - jnp.max(tops, axis=0, keepdims=True)) * EXP2_SCALE)
        total = jnp.sum(weight * sums, axis=0, keepdims=True)
        slot = lax.broadcasted_iota(jnp.int32, (1, wide), 1) % TILE + i * TILE
        live = jnp.where(slot < length, 1.0, 0.0)
        m_all[...] = weight * (live / total)

        for t in range(parts):
            grad_tile(slice(t * WIDE_TILE, (t + 1) * WIDE_TILE), WIDE_TILE, t, t * WIDE_TILE)
        dq_t[...] = grad_sums(slice(0, prompt), prompt)

        def grad_body(t, carry):
            grad_tile(own(t), TILE, parts + t, 0)
            dq_t[...] += grad_sums(own(t), TILE)
            return carry

        lax.fori_loop(0, i + 1, grad_body, 0)
        for j in heads:
            back_ref[here, j * HEAD_DIM : (j + 1) * HEAD_DIM] = (
                (dq_t[:, lanes(j)] * SCALE).T.astype(BF16)
            )
        return carry

    lax.fori_loop(0, lax.div(length + TILE - 1, TILE), slot_block, 0)
    pg_ref[:, 0:HEAD_DIM] = (dk[0:prompt] * SCALE).astype(BF16)
    pg_ref[:, HEAD_DIM:] = dv[0:prompt].astype(BF16)
    back_ref[:, size : size + HEAD_DIM] = (dk[prompt:] * SCALE).astype(BF16)
    back_ref[:, size + HEAD_DIM :] = dv[prompt:].astype(BF16)
    near = me_prefix % NEAR
    copies = [
        (pg_ref.at[pl.ds(times(far * NEAR + (near ^ d), share), share)], out.at[far])
        for d, out in enumerate(pg_out)
        for far in range(sources // NEAR)
    ]
    for copy in start_all([(back_ref, back_out)] + copies, sems):
        copy.wait()


def attend(place, x, pkv):
    slots, width = x.shape
    half, share, prompt_width = pkv[0].shape
    responses = 2 * half
    prompt = responses * share
    keys = slots + prompt
    wide = GROUP * TILE
    part = ((responses // NEAR, share, prompt_width), BF16)
    outs = [((slots, BACK_W), BF16)] + [part] * NEAR
    return pl.pallas_call(
        attend_kernel,
        in_specs=[SMEM, ANY, ANY, ANY],
        out_specs=[HBM] * len(outs),
        out_shape=[jax.ShapeDtypeStruct(shape, dtype) for shape, dtype in outs],
        scratch_shapes=[
            pltpu.VMEM((slots, width), BF16),
            pltpu.VMEM((prompt, prompt_width), BF16),
            pltpu.VMEM((slots, BACK_W), BF16),
            pltpu.VMEM((prompt, prompt_width), BF16),
            pltpu.SemaphoreType.DMA((1 + responses,)),
            pltpu.VMEM((keys, HEAD_DIM), BF16),
            pltpu.VMEM((keys, HEAD_DIM), BF16),
            pltpu.VMEM((HEAD_DIM, keys), BF16),
            pltpu.VMEM((slots, HEAD_DIM), BF16),
            pltpu.VMEM((wide, HEAD_DIM), BF16),
            pltpu.VMEM((wide, HEAD_DIM), BF16),
            pltpu.VMEM((HEAD_DIM, wide), BF16),
            pltpu.VMEM((2 * HEAD_DIM, wide), BF16),
            pltpu.VMEM((keys, wide), F32),
            pltpu.VMEM((8, wide), F32),
            pltpu.VMEM((8, wide), F32),
            pltpu.VMEM((prompt, wide), BF16),
            pltpu.VMEM((prompt, wide), BF16),
            pltpu.VMEM((HEAD_DIM, wide), F32),
            pltpu.VMEM((keys, HEAD_DIM), F32),
            pltpu.VMEM((keys, HEAD_DIM), F32),
        ],
        compiler_params=params(44),
        cost_estimate=pl.CostEstimate(
            flops=10 * slots * keys * QW, transcendentals=0, bytes_accessed=8 * slots * QW
        ),
        name="attend",
    )(place, x, *pkv)


def near_kernel(place_ref, *refs):
    parts, outs, total = refs[:NEAR], refs[NEAR:-1], refs[-1]
    value = parts[0][...].astype(F32)
    for part in parts[1:]:
        value = value + part[...].astype(F32)
    total[...] = value
    for d, out in enumerate(outs):
        out[...] = total[(place_ref[1] // NEAR) ^ d]


def sum_near(place, parts):
    far, share, width = parts[0].shape
    return pl.pallas_call(
        near_kernel,
        in_specs=[SMEM] + [VMEM] * NEAR,
        out_specs=[VMEM] * far,
        out_shape=[jax.ShapeDtypeStruct((share, width), F32)] * far,
        scratch_shapes=[pltpu.VMEM((far, share, width), F32)],
        compiler_params=params(4),
        cost_estimate=pl.CostEstimate(flops=5 * 10**10, transcendentals=0, bytes_accessed=2**20),
        name="sum_near",
    )(place, *parts)


def swap(value, axis, d):
    return lax.ppermute(value, axis, [(i, i ^ d) for i in range(lax.axis_size(axis))])


def local(
    resp_query,
    resp_keys,
    resp_values,
    resp_out,
    resp_grad,
    prompt_keys,
    prompt_values,
    resp_lengths,
):
    head = lax.axis_index("resp")
    responses = lax.axis_size("prefix")
    rows = resp_query.shape[1]
    place = jnp.stack([resp_lengths[0], lax.axis_index("prefix")])
    cut = lambda a: lax.dynamic_slice_in_dim(a, head * HEAD_DIM, HEAD_DIM, 1)
    pkv = jnp.concatenate([cut(prompt_keys), cut(prompt_values)], axis=1)[None]
    first = swap(pkv, "prefix", 1 << GATHER_BITS[0])
    send = pack(resp_query[0], resp_grad[0], resp_out[0], resp_keys[0], resp_values[0])
    pkv, first, send = lax.optimization_barrier((pkv, first, send))
    x = lax.all_to_all(send, "resp", 0, 0, tiled=True)
    pkv = jnp.concatenate([pkv, first])
    for bit in GATHER_BITS[1:-1]:
        pkv = jnp.concatenate([pkv, swap(pkv, "prefix", 1 << bit)])
    pkv = [pkv, swap(pkv, "prefix", 1 << GATHER_BITS[-1])]
    outs = attend(place, x.reshape(KV_HEADS * rows, SEND_W), pkv)
    back, parts = outs[0], outs[1:]
    back = lax.all_to_all(back.reshape(KV_HEADS, rows, BACK_W), "resp", 0, 0, tiled=True)
    parts = [parts[0]] + [swap(parts[d], "prefix", d) for d in range(1, NEAR)]
    parts = sum_near(place, parts)
    parts = [parts[0]] + [swap(parts[d], "prefix", NEAR * d) for d in range(1, len(parts))]
    share, width = parts[0].shape
    total = sum(parts[1:], parts[0]).astype(BF16).reshape(KV_HEADS, share // KV_HEADS, width)
    back, total = lax.optimization_barrier((back, total))
    total = lax.all_to_all(total, "resp", 0, 0, tiled=True)
    total = total.reshape(KV_HEADS, share // KV_HEADS, 2, HEAD_DIM).transpose(2, 1, 0, 3)
    total = total.reshape(2, share // KV_HEADS, KV_HEADS * HEAD_DIM)
    grad_query, grad_keys, grad_values = unpack(back)
    return (grad_query[None], grad_keys[None], grad_values[None], total[0], total[1])


def solution(mesh):
    return jax.shard_map(
        local,
        mesh=mesh,
        in_specs=(
            P("prefix", "resp", None),
            P("prefix", "resp", None),
            P("prefix", "resp", None),
            P("prefix", "resp", None),
            P("prefix", "resp", None),
            P("prefix", None),
            P("prefix", None),
            P("prefix"),
        ),
        out_specs=(
            P("prefix", "resp", None),
            P("prefix", "resp", None),
            P("prefix", "resp", None),
            P(("prefix", "resp"), None),
            P(("prefix", "resp"), None),
        ),
        check_vma=False,
    )
```

```python
import jax
import jax.numpy as jnp
from jax import lax
from jax.experimental import pallas as pl
from jax.experimental.pallas import tpu as pltpu
from jax.sharding import PartitionSpec as P

HEADS = 40
KV_HEADS = 8
GROUP = HEADS // KV_HEADS
HEAD_DIM = 128
SCALE = HEAD_DIM ** (-0.5)
EXP2_SCALE = SCALE * 1.4426950408889634
QW = GROUP * HEAD_DIM
KVD = 3 * HEAD_DIM
TILE = 256
STATS = 16
UNSEEN = -1e30
PACK_ROWS = 32
GATHER_BITS = (1, 0, 2, 3)
SEND_W = KVD + 2 * QW
BACK_W = QW + 2 * HEAD_DIM
X_BIT, CORE_BIT = 2, 1

NN = (((1,), (0,)), ((), ()))
BF16 = jnp.bfloat16
F32 = jnp.float32
ANY = pl.BlockSpec(memory_space=pl.ANY)
HBM = pl.BlockSpec(memory_space=pltpu.HBM)
VMEM = pl.BlockSpec(memory_space=pltpu.VMEM)
SMEM = pl.BlockSpec(memory_space=pltpu.SMEM)


def dot(a, b, dims):
    return lax.dot_general(a, b, dims, preferred_element_type=F32)


def params(mib):
    return pltpu.CompilerParams(vmem_limit_bytes=mib * 1024 * 1024)


def times(index, size):
    return pl.multiple_of(index * size, size)


def gather_mask(index):
    return sum(((index >> step) & 1) << bit for step, bit in enumerate(GATHER_BITS))


def pack_kernel(q_ref, g_ref, o_ref, k_ref, v_ref, send_ref):
    rows = q_ref.shape[0]
    highs, lows = [], []
    for h in range(KV_HEADS):
        thin = slice(h * HEAD_DIM, (h + 1) * HEAD_DIM)
        wide = slice(h * QW, (h + 1) * QW)
        send_ref[h, :, 0:HEAD_DIM] = k_ref[:, thin]
        send_ref[h, :, HEAD_DIM : 2 * HEAD_DIM] = v_ref[:, thin]
        send_ref[h, :, KVD : KVD + QW] = q_ref[:, wide]
        send_ref[h, :, KVD + QW :] = g_ref[:, wide]
        product = g_ref[:, wide].astype(F32) * o_ref[:, wide].astype(F32)
        high = product.astype(BF16)
        highs.append(high)
        lows.append((product - high.astype(F32)).astype(BF16))
    row = lax.broadcasted_iota(jnp.int32, (QW, HEAD_DIM), 0) // HEAD_DIM
    lane = lax.broadcasted_iota(jnp.int32, (QW, HEAD_DIM), 1)
    ones = jnp.where((lane >= 3 * row) & (lane < 3 * row + 3), 1.0, 0.0).astype(BF16)
    left = dot(jnp.concatenate(highs), ones, NN) + dot(jnp.concatenate(lows), ones, NN)
    part = lax.broadcasted_iota(jnp.int32, left.shape, 1) % 3
    first = left.astype(BF16).astype(F32)
    second = (left - first).astype(BF16).astype(F32)
    third = left - first - second
    deltas = jnp.where(part == 0, first, jnp.where(part == 1, second, third)).astype(BF16)
    for h in range(KV_HEADS):
        send_ref[h, :, 2 * HEAD_DIM : KVD] = deltas[h * rows : (h + 1) * rows]


def pack(q, g, o, k, v):
    rows = q.shape[0]
    block = min(PACK_ROWS, rows)
    wide = pl.BlockSpec((block, KV_HEADS * QW), lambda i: (i, 0))
    thin = pl.BlockSpec((block, KV_HEADS * HEAD_DIM), lambda i: (i, 0))
    return pl.pallas_call(
        pack_kernel,
        grid=(rows // block,),
        in_specs=[wide, wide, wide, thin, thin],
        out_specs=pl.BlockSpec((KV_HEADS, block, SEND_W), lambda i: (0, i, 0)),
        out_shape=jax.ShapeDtypeStruct((KV_HEADS, rows, SEND_W), BF16),
        compiler_params=params(60),
        cost_estimate=pl.CostEstimate(flops=10**10, transcendentals=0, bytes_accessed=2**23),
        name="pack",
    )(q, g, o, k, v)


def start_all(copies, sems):
    started = [pltpu.make_async_copy(src, dst, sems.at[n]) for n, (src, dst) in enumerate(copies)]
    for copy in started:
        copy.start()
    return started


def unpack_kernel(back_ref, q_ref, k_ref, v_ref, sems):
    copies = []
    for h in range(KV_HEADS):
        thin = slice(h * HEAD_DIM, (h + 1) * HEAD_DIM)
        wide = slice(h * QW, (h + 1) * QW)
        copies.append((back_ref.at[h, :, 0:QW], q_ref.at[:, wide]))
        copies.append((back_ref.at[h, :, QW : QW + HEAD_DIM], k_ref.at[:, thin]))
        copies.append((back_ref.at[h, :, QW + HEAD_DIM :], v_ref.at[:, thin]))
    for copy in start_all(copies, sems):
        copy.wait()


def unpack(back):
    rows = back.shape[1]
    return pl.pallas_call(
        unpack_kernel,
        in_specs=[ANY],
        out_specs=[ANY] * 3,
        out_shape=[
            jax.ShapeDtypeStruct((rows, KV_HEADS * QW), BF16),
            jax.ShapeDtypeStruct((rows, KV_HEADS * HEAD_DIM), BF16),
            jax.ShapeDtypeStruct((rows, KV_HEADS * HEAD_DIM), BF16),
        ],
        scratch_shapes=[pltpu.SemaphoreType.DMA((3 * KV_HEADS,))],
        compiler_params=params(4),
        name="unpack",
    )(back)


def attend_kernel(place_ref, x_ref, pkv_low, pkv_high, back_out, pg_keep, pg_give, *refs):
    pkv_ref, back_ref, pg_ref, sems, k_all, v_all, k_t, d_all = refs[:8]
    p_s, l_s, dq_t, dk, dv = refs[8:13]
    sets = [refs[13:20], refs[20:27]]
    prompt = pkv_ref.shape[0]
    slots = x_ref.shape[0]
    wide = GROUP * TILE
    prompt_tiles = prompt // TILE
    length, me_prefix = place_ref[0], place_ref[1]
    half = pkv_low.shape[0]
    sources = 2 * half
    share = prompt // sources
    copies = [
        ((pkv_low, pkv_high)[f // half].at[f % half], pkv_ref.at[pl.ds(times(me_prefix ^ gather_mask(f), share), share)])
        for f in range(sources)
    ]
    copies = start_all(copies, sems)
    back_ref[...] = jnp.zeros_like(back_ref)
    dk[...] = jnp.zeros_like(dk)
    dv[...] = jnp.zeros_like(dv)
    for copy in copies:
        copy.wait()

    def flip(a):
        return a.astype(F32).T.astype(BF16)

    k_all[0:prompt] = pkv_ref[:, 0:HEAD_DIM]
    v_all[0:prompt] = pkv_ref[:, HEAD_DIM:]
    k_all[prompt:] = x_ref[:, 0:HEAD_DIM]
    v_all[prompt:] = x_ref[:, HEAD_DIM : 2 * HEAD_DIM]
    d_all[...] = x_ref[:, 2 * HEAD_DIM : KVD]
    for t in range((prompt + slots) // TILE):
        block = slice(t * TILE, (t + 1) * TILE)
        k_t[:, block] = flip(k_all[block])

    def lanes(j):
        return slice(j * TILE, (j + 1) * TILE)

    def tile_rows(t, count):
        return pl.ds(times(t, TILE), count * TILE)

    def stat_rows(t, count):
        return pl.ds(times(t, STATS), count * STATS)

    def sweep(body, tiles):
        def pair(n, carry):
            body(2 * n, 2)
            return carry

        lax.fori_loop(0, tiles // 2, pair, 0)
        if tiles % 2:
            body(tiles - 1, 1)

    def load_block(i, block):
        qs, gs, qs_t, gs_t = block[:4]
        here = slice(i * TILE, (i + 1) * TILE)
        delta_t = flip(d_all[here])
        for j in range(GROUP):
            col = KVD + j * HEAD_DIM
            q = x_ref[here, col : col + HEAD_DIM]
            g = x_ref[here, col + QW : col + QW + HEAD_DIM]
            qs[lanes(j)] = q
            gs[lanes(j)] = g
            qs_t[:, lanes(j)] = flip(q)
            gs_t[0:HEAD_DIM, lanes(j)] = flip(g)
            gs_t[HEAD_DIM:, lanes(j)] = delta_t

    def score_head(t, count, j, block, diagonal=False):
        qs_t, e_all, tops, sums = block[2], block[4], block[5], block[6]
        s = dot(k_all[tile_rows(t, count)], qs_t[:, lanes(j)], NN)
        if diagonal:
            seen = lax.broadcasted_iota(jnp.int32, s.shape, 0) <= lax.broadcasted_iota(
                jnp.int32, s.shape, 1
            )
            s = jnp.where(seen, s, UNSEEN)
        groups = count * STATS // 8
        s = s.reshape(groups, -1, 8, TILE)
        top = jnp.max(s, axis=1, keepdims=True)
        e = jnp.exp2((s - top) * EXP2_SCALE)
        tops[stat_rows(t, count), lanes(j)] = top.reshape(groups * 8, TILE)
        sums[stat_rows(t, count), lanes(j)] = jnp.sum(e, axis=1).reshape(groups * 8, TILE)
        e_all[tile_rows(t, count), lanes(j)] = e.reshape(count * TILE, TILE)

    def normalise(i, block):
        tops, sums = block[5], block[6]
        rows = STATS * (prompt_tiles + i + 1)
        top = tops[0:rows]
        weight = jnp.exp2((top - jnp.max(top, axis=0, keepdims=True)) * EXP2_SCALE)
        total = jnp.sum(weight * sums[0:rows], axis=0, keepdims=True)
        slot = lax.broadcasted_iota(jnp.int32, (1, wide), 1) % TILE + i * TILE
        tops[0:rows] = weight * (jnp.where(slot < length, 1.0, 0.0) / total)

    def grad_head(t, count, j, block):
        gs_t, e_all, factors = block[3], block[4], block[5]
        lane = lax.broadcasted_iota(jnp.int32, (count * TILE, HEAD_DIM), 1)
        select = jnp.where((lane >= 3 * j) & (lane < 3 * j + 3), -1.0, 0.0).astype(BF16)
        values = jnp.concatenate([v_all[tile_rows(t, count)], select], axis=1)
        shifted = dot(values, gs_t[:, lanes(j)], NN)
        groups = count * STATS // 8
        e = e_all[tile_rows(t, count), lanes(j)].reshape(groups, -1, 8, TILE)
        factor = factors[stat_rows(t, count), lanes(j)].reshape(groups, 1, 8, TILE)
        p = (e * factor).reshape(count * TILE, TILE)
        p_s[0 : count * TILE, lanes(j)] = p.astype(BF16)
        l_s[0 : count * TILE, lanes(j)] = (p * shifted).astype(BF16)

    def grad_sums(t, count, block):
        qs, gs = block[:2]
        rows, held = tile_rows(t, count), slice(0, count * TILE)
        dv[rows] += dot(p_s[held], gs[...], NN)
        dk[rows] += dot(l_s[held], qs[...], NN)
        dq_t[...] += dot(k_t[:, rows], l_s[held], NN)

    def finish(i):
        here = slice(i * TILE, (i + 1) * TILE)
        for j in range(GROUP):
            back_ref[here, j * HEAD_DIM : (j + 1) * HEAD_DIM] = (
                (dq_t[:, lanes(j)] * SCALE).T.astype(BF16)
            )

    def scores(t, count):
        for j in range(GROUP):
            score_head(t, count, j, sets[0])

    load_block(0, sets[0])
    sweep(scores, prompt_tiles)
    for j in range(GROUP):
        score_head(prompt_tiles, 1, j, sets[0], diagonal=True)
    normalise(0, sets[0])

    blocks = slots // TILE
    live = lax.div(length + TILE - 1, TILE)
    for i in range(blocks):
        now, later = sets[i % 2], sets[(i + 1) % 2]
        tiles = prompt_tiles + i + 1
        dq_t[...] = jnp.zeros_like(dq_t)

        def grads(t, count):
            for j in range(GROUP):
                grad_head(t, count, j, now)
            grad_sums(t, count, now)

        def both(t, count):
            for j in range(GROUP):
                grad_head(t, count, j, now)
                score_head(t, count, j, later)
            grad_sums(t, count, now)

        if i + 1 < blocks:

            @pl.when(live > i + 1)
            def _():
                load_block(i + 1, later)
                sweep(both, tiles)
                finish(i)
                for j in range(GROUP):
                    score_head(tiles, 1, j, later, diagonal=True)
                normalise(i + 1, later)

        @pl.when(live == i + 1)
        def _():
            sweep(grads, tiles)
            finish(i)

    pg_ref[:, 0:HEAD_DIM] = (dk[0:prompt] * SCALE).astype(BF16)
    pg_ref[:, HEAD_DIM:] = dv[0:prompt].astype(BF16)
    back_ref[:, QW : QW + HEAD_DIM] = (dk[prompt:] * SCALE).astype(BF16)
    back_ref[:, QW + HEAD_DIM :] = dv[prompt:].astype(BF16)
    mine = me_prefix & X_BIT
    copies = [
        (pg_ref.at[pl.ds(times(f + (f & -X_BIT) + (mine ^ bit), share), share)], out.at[f])
        for bit, out in ((0, pg_keep), (X_BIT, pg_give))
        for f in range(half)
    ]
    for copy in start_all([(back_ref, back_out)] + copies, sems):
        copy.wait()


def attend(place, x, pkv):
    slots = x.shape[0]
    half, share, prompt_width = pkv[0].shape
    responses = 2 * half
    prompt = responses * share
    keys = slots + prompt
    wide = GROUP * TILE
    outs = [((slots, BACK_W), BF16)] + [((half, share, prompt_width), BF16)] * 2
    stats = pltpu.VMEM((keys // TILE * STATS, wide), F32)
    one_set = [
        pltpu.VMEM((wide, HEAD_DIM), BF16),
        pltpu.VMEM((wide, HEAD_DIM), BF16),
        pltpu.VMEM((HEAD_DIM, wide), BF16),
        pltpu.VMEM((2 * HEAD_DIM, wide), BF16),
        pltpu.VMEM((keys, wide), F32),
        stats,
        stats,
    ]
    return pl.pallas_call(
        attend_kernel,
        in_specs=[SMEM, VMEM, ANY, ANY],
        out_specs=[HBM] * len(outs),
        out_shape=[pltpu.HBM(shape, dtype) for shape, dtype in outs],
        scratch_shapes=[
            pltpu.VMEM((prompt, prompt_width), BF16),
            pltpu.VMEM((slots, BACK_W), BF16),
            pltpu.VMEM((prompt, prompt_width), BF16),
            pltpu.SemaphoreType.DMA((1 + responses,)),
            pltpu.VMEM((keys, HEAD_DIM), BF16),
            pltpu.VMEM((keys, HEAD_DIM), BF16),
            pltpu.VMEM((HEAD_DIM, keys), BF16),
            pltpu.VMEM((slots, HEAD_DIM), BF16),
            pltpu.VMEM((2 * TILE, wide), BF16),
            pltpu.VMEM((2 * TILE, wide), BF16),
            pltpu.VMEM((HEAD_DIM, wide), F32),
            pltpu.VMEM((keys, HEAD_DIM), F32),
            pltpu.VMEM((keys, HEAD_DIM), F32),
        ]
        + one_set * 2,
        compiler_params=params(50),
        cost_estimate=pl.CostEstimate(
            flops=10 * slots * keys * QW, transcendentals=0, bytes_accessed=8 * slots * QW
        ),
        name="attend",
    )(place, pltpu.with_memory_space_constraint(x, pltpu.VMEM), *pkv)


def core_kernel(place_ref, mine_ref, got_ref, keep_ref, give_ref, total):
    total[...] = mine_ref[...].astype(F32) + got_ref[...].astype(F32)
    core = place_ref[1] & CORE_BIT
    for f in range(keep_ref.shape[0]):
        keep_ref[f] = total[2 * f + core]
        give_ref[f] = total[2 * f + 1 - core]


def sum_over_x(place, mine, got):
    count, share, width = mine.shape
    part = jax.ShapeDtypeStruct((count // 2, share, width), F32)
    return pl.pallas_call(
        core_kernel,
        in_specs=[SMEM, VMEM, VMEM],
        out_specs=[VMEM] * 2,
        out_shape=[part] * 2,
        scratch_shapes=[pltpu.VMEM(mine.shape, F32)],
        compiler_params=params(8),
        cost_estimate=pl.CostEstimate(flops=5 * 10**10, transcendentals=0, bytes_accessed=2**20),
        name="sum_over_x",
    )(place, mine, got)


def z_kernel(place_ref, mine_ref, got_ref, *refs):
    outs, total = refs[:-1], refs[-1]
    total[...] = mine_ref[...] + got_ref[...]
    z = place_ref[1] // (2 * X_BIT)
    for d, out in enumerate(outs):
        out[...] = total[z ^ d]


def sum_over_cores(place, mine, got):
    count, share, width = mine.shape
    return pl.pallas_call(
        z_kernel,
        in_specs=[SMEM, VMEM, VMEM],
        out_specs=[VMEM] * count,
        out_shape=[jax.ShapeDtypeStruct((share, width), F32)] * count,
        scratch_shapes=[pltpu.VMEM(mine.shape, F32)],
        compiler_params=params(8),
        name="sum_over_cores",
    )(place, mine, got)


def swap(value, axis, d):
    return lax.ppermute(value, axis, [(i, i ^ d) for i in range(lax.axis_size(axis))])


def local(
    resp_query,
    resp_keys,
    resp_values,
    resp_out,
    resp_grad,
    prompt_keys,
    prompt_values,
    resp_lengths,
):
    head = lax.axis_index("resp")
    rows = resp_query.shape[1]
    place = jnp.stack([resp_lengths[0], lax.axis_index("prefix")])
    cut = lambda a: lax.dynamic_slice_in_dim(a, head * HEAD_DIM, HEAD_DIM, 1)
    pkv = jnp.concatenate([cut(prompt_keys), cut(prompt_values)], axis=1)[None]
    first = swap(pkv, "prefix", 1 << GATHER_BITS[0])
    send = pack(resp_query[0], resp_grad[0], resp_out[0], resp_keys[0], resp_values[0])
    pkv, first, send = lax.optimization_barrier((pkv, first, send))
    x = lax.all_to_all(send, "resp", 0, 0, tiled=True)
    pkv = jnp.concatenate([pkv, first])
    for bit in GATHER_BITS[1:-1]:
        pkv = jnp.concatenate([pkv, swap(pkv, "prefix", 1 << bit)])
    pkv = [pkv, swap(pkv, "prefix", 1 << GATHER_BITS[-1])]
    back, keep, give = attend(place, x.reshape(KV_HEADS * rows, SEND_W), pkv)
    back = lax.all_to_all(back.reshape(KV_HEADS, rows, BACK_W), "resp", 0, 0, tiled=True)
    keep, give = sum_over_x(place, keep, swap(give, "prefix", X_BIT))
    parts = sum_over_cores(place, keep, swap(give, "prefix", CORE_BIT))
    parts = [parts[0]] + [swap(parts[d], "prefix", 2 * X_BIT * d) for d in range(1, len(parts))]
    share, width = parts[0].shape
    total = sum(parts[1:], parts[0]).astype(BF16).reshape(KV_HEADS, share // KV_HEADS, width)
    back, total = lax.optimization_barrier((back, total))
    total = lax.all_to_all(total, "resp", 0, 0, tiled=True)
    total = total.reshape(KV_HEADS, share // KV_HEADS, 2, HEAD_DIM).transpose(2, 1, 0, 3)
    total = total.reshape(2, share // KV_HEADS, KV_HEADS * HEAD_DIM)
    grad_query, grad_keys, grad_values = unpack(back)
    return (grad_query[None], grad_keys[None], grad_values[None], total[0], total[1])


def solution(mesh):
    return jax.shard_map(
        local,
        mesh=mesh,
        in_specs=(
            P("prefix", "resp", None),
            P("prefix", "resp", None),
            P("prefix", "resp", None),
            P("prefix", "resp", None),
            P("prefix", "resp", None),
            P("prefix", None),
            P("prefix", None),
            P("prefix"),
        ),
        out_specs=(
            P("prefix", "resp", None),
            P("prefix", "resp", None),
            P("prefix", "resp", None),
            P(("prefix", "resp"), None),
            P(("prefix", "resp"), None),
        ),
        check_vma=False,
    )
```

```python
import jax
import jax.numpy as jnp
from jax import lax
from jax.experimental import pallas as pl
from jax.experimental.pallas import tpu as pltpu
from jax.sharding import PartitionSpec as P

HEADS = 40
KV_HEADS = 8
GROUP = HEADS // KV_HEADS
HEAD_DIM = 128
SCALE = HEAD_DIM ** (-0.5)
EXP2_SCALE = SCALE * 1.4426950408889634
QW = GROUP * HEAD_DIM
TILE = 256
STATS = 16
UNSEEN = -1e30
PACK_ROWS = 32
GATHER_BITS = (1, 0, 2, 3)
COLUMNS = 2 + 2 * GROUP
DELTA_ROWS = 16
BACK_W = QW + 2 * HEAD_DIM
X_BIT, CORE_BIT = 2, 1

NN = (((1,), (0,)), ((), ()))
BF16 = jnp.bfloat16
F32 = jnp.float32
ANY = pl.BlockSpec(memory_space=pl.ANY)
HBM = pl.BlockSpec(memory_space=pltpu.HBM)
VMEM = pl.BlockSpec(memory_space=pltpu.VMEM)
SMEM = pl.BlockSpec(memory_space=pltpu.SMEM)


def dot(a, b, dims):
    return lax.dot_general(a, b, dims, preferred_element_type=F32)


def params(mib):
    return pltpu.CompilerParams(vmem_limit_bytes=mib * 1024 * 1024)


def times(index, size):
    return pl.multiple_of(index * size, size)


def send_rows(c, n):
    first = (c * COLUMNS + n) * PACK_ROWS
    return slice(first, first + PACK_ROWS)


def gather_mask(index):
    return sum(((index >> step) & 1) << bit for step, bit in enumerate(GATHER_BITS))


def start_all(copies, sems):
    started = [pltpu.make_async_copy(src, dst, sems.at[n]) for n, (src, dst) in enumerate(copies)]
    for copy in started:
        copy.start()
    return started


def pack_kernel(q_in, g_in, o_in, k_in, v_in, send_out, q_ref, g_ref, o_ref, k_ref, v_ref, send_ref, left_ref, sems, out_sems):
    ins = ((q_in, q_ref), (g_in, g_ref), (o_in, o_ref), (k_in, k_ref), (v_in, v_ref))
    steps = q_ref.shape[0] // PACK_ROWS
    arriving = []
    for c in range(steps):
        rows = slice(c * PACK_ROWS, (c + 1) * PACK_ROWS)
        arriving.append(start_all([(src.at[rows], dst.at[rows]) for src, dst in ins], sems.at[c]))
    row = lax.broadcasted_iota(jnp.int32, (QW, HEAD_DIM), 0) // HEAD_DIM
    lane = lax.broadcasted_iota(jnp.int32, (QW, HEAD_DIM), 1)
    ones = jnp.where((lane >= 3 * row) & (lane < 3 * row + 3), 1.0, 0.0).astype(BF16)
    leaving = []
    for c in range(steps):
        rows = slice(c * PACK_ROWS, (c + 1) * PACK_ROWS)
        for copy in arriving[c]:
            copy.wait()
        highs, lows = [], []
        for h in range(KV_HEADS):
            columns = [(k_ref, h), (v_ref, h)]
            columns += [(q_ref, h * GROUP + j) for j in range(GROUP)]
            columns += [(g_ref, h * GROUP + j) for j in range(GROUP)]
            for n, (ref, col) in enumerate(columns):
                send_ref[h, send_rows(c, n)] = ref[rows, col * HEAD_DIM : (col + 1) * HEAD_DIM]
            wide = slice(h * QW, (h + 1) * QW)
            product = g_ref[rows, wide].astype(F32) * o_ref[rows, wide].astype(F32)
            high = product.astype(BF16)
            highs.append(high)
            lows.append((product - high.astype(F32)).astype(BF16))
        part = slice(c * COLUMNS * PACK_ROWS, (c + 1) * COLUMNS * PACK_ROWS)
        leaving += start_all([(send_ref.at[:, part], send_out.at[:, part])], out_sems.at[pl.ds(c, 1)])
        left = dot(jnp.concatenate(highs), ones, NN) + dot(jnp.concatenate(lows), ones, NN)
        for h in range(KV_HEADS):
            left_ref[h, rows] = left[h * PACK_ROWS : (h + 1) * PACK_ROWS]
    part = lax.broadcasted_iota(jnp.int32, (DELTA_ROWS, q_ref.shape[0]), 0) % 3
    last = slice(steps * COLUMNS * PACK_ROWS, steps * COLUMNS * PACK_ROWS + DELTA_ROWS)
    for h in range(KV_HEADS):
        left = left_ref[h].T[0:DELTA_ROWS]
        first = left.astype(BF16).astype(F32)
        second = (left - first).astype(BF16).astype(F32)
        third = left - first - second
        send_ref[h, last] = jnp.where(part == 0, first, jnp.where(part == 1, second, third)).astype(BF16)
    leaving += start_all([(send_ref.at[:, last], send_out.at[:, last])], out_sems.at[pl.ds(steps, 1)])
    for copy in leaving:
        copy.wait()


def pack(q, g, o, k, v):
    rows = q.shape[0]
    steps = rows // PACK_ROWS
    send = (KV_HEADS, rows * COLUMNS + DELTA_ROWS, HEAD_DIM)
    return pl.pallas_call(
        pack_kernel,
        in_specs=[HBM] * 5,
        out_specs=HBM,
        out_shape=pltpu.HBM(send, BF16),
        scratch_shapes=[pltpu.VMEM(a.shape, BF16) for a in (q, g, o, k, v)]
        + [
            pltpu.VMEM(send, BF16),
            pltpu.VMEM((KV_HEADS, rows, HEAD_DIM), F32),
            pltpu.SemaphoreType.DMA((steps, 5)),
            pltpu.SemaphoreType.DMA((steps + 1,)),
        ],
        compiler_params=params(60),
        name="pack",
    )(q, g, o, k, v)


def unpack_kernel(back_ref, q_ref, k_ref, v_ref, sems):
    copies = []
    for h in range(KV_HEADS):
        thin = slice(h * HEAD_DIM, (h + 1) * HEAD_DIM)
        wide = slice(h * QW, (h + 1) * QW)
        copies.append((back_ref.at[h, :, 0:QW], q_ref.at[:, wide]))
        copies.append((back_ref.at[h, :, QW : QW + HEAD_DIM], k_ref.at[:, thin]))
        copies.append((back_ref.at[h, :, QW + HEAD_DIM :], v_ref.at[:, thin]))
    for copy in start_all(copies, sems):
        copy.wait()


def unpack(back):
    rows = back.shape[1]
    return pl.pallas_call(
        unpack_kernel,
        in_specs=[ANY],
        out_specs=[ANY] * 3,
        out_shape=[
            jax.ShapeDtypeStruct((rows, KV_HEADS * QW), BF16),
            jax.ShapeDtypeStruct((rows, KV_HEADS * HEAD_DIM), BF16),
            jax.ShapeDtypeStruct((rows, KV_HEADS * HEAD_DIM), BF16),
        ],
        scratch_shapes=[pltpu.SemaphoreType.DMA((3 * KV_HEADS,))],
        compiler_params=params(4),
        name="unpack",
    )(back)


def attend_kernel(place_ref, x_ref, pkv_low, pkv_high, back_out, pg_keep, pg_give, *refs):
    pkv_ref, back_ref, pg_ref, sems, k_all, v_all, k_t = refs[:7]
    p_s, l_s, dq_t, dk, dv = refs[7:12]
    sets = [refs[12:19], refs[19:26]]
    prompt = pkv_ref.shape[0]
    run = (x_ref.shape[1] - DELTA_ROWS) // COLUMNS
    slots = KV_HEADS * run
    wide = GROUP * TILE
    prompt_tiles = prompt // TILE
    length, me_prefix = place_ref[0], place_ref[1]
    half = pkv_low.shape[0]
    sources = 2 * half
    share = prompt // sources
    copies = [
        ((pkv_low, pkv_high)[f // half].at[f % half], pkv_ref.at[pl.ds(times(me_prefix ^ gather_mask(f), share), share)])
        for f in range(sources)
    ]
    copies = start_all(copies, sems)
    back_ref[...] = jnp.zeros_like(back_ref)
    dk[...] = jnp.zeros_like(dk)
    dv[...] = jnp.zeros_like(dv)
    for block in sets:
        block[3][HEAD_DIM + DELTA_ROWS :] = jnp.zeros((HEAD_DIM - DELTA_ROWS, wide), BF16)
    for copy in copies:
        copy.wait()

    def flip(a):
        return a.astype(F32).T.astype(BF16)

    def slots_of(b, n):
        return jnp.concatenate([x_ref[b, send_rows(c, n)] for c in range(run // PACK_ROWS)])

    k_all[0:prompt] = pkv_ref[:, 0:HEAD_DIM]
    v_all[0:prompt, 0:HEAD_DIM] = pkv_ref[:, HEAD_DIM:]
    for b in range(KV_HEADS):
        own = slice(prompt + b * run, prompt + (b + 1) * run)
        k_all[own] = slots_of(b, 0)
        v_all[own, 0:HEAD_DIM] = slots_of(b, 1)
    v_all[:, HEAD_DIM:] = jnp.full((prompt + slots, HEAD_DIM), -1.0, BF16)
    for t in range((prompt + slots) // TILE):
        block = slice(t * TILE, (t + 1) * TILE)
        k_t[:, block] = flip(k_all[block])

    def lanes(j):
        return slice(j * TILE, (j + 1) * TILE)

    def tile_rows(t, count):
        return pl.ds(times(t, TILE), count * TILE)

    def stat_rows(t, count):
        return pl.ds(times(t, STATS), count * STATS)

    def sweep(body, tiles):
        def pair(n, carry):
            body(2 * n, 2)
            return carry

        lax.fori_loop(0, tiles // 2, pair, 0)
        if tiles % 2:
            body(tiles - 1, 1)

    def load_block(i, block):
        qs, gs, qs_t, gs_t = block[:4]
        sources = range(i * TILE // run, (i + 1) * TILE // run)
        delta_t = jnp.concatenate([x_ref[b, run * COLUMNS :] for b in sources], axis=1).astype(F32)
        part = lax.broadcasted_iota(jnp.int32, delta_t.shape, 0)
        for j in range(GROUP):
            q = jnp.concatenate([slots_of(b, 2 + j) for b in sources])
            g = jnp.concatenate([slots_of(b, 2 + GROUP + j) for b in sources])
            qs[lanes(j)] = q
            gs[lanes(j)] = g
            qs_t[:, lanes(j)] = flip(q)
            gs_t[0:HEAD_DIM, lanes(j)] = flip(g)
            mine = (part >= 3 * j) & (part < 3 * j + 3)
            gs_t[HEAD_DIM : HEAD_DIM + DELTA_ROWS, lanes(j)] = jnp.where(mine, delta_t, 0.0).astype(BF16)

    def score_head(t, count, j, block, diagonal=False):
        qs_t, _, e_all, tops, sums = block[2:]
        s = dot(k_all[tile_rows(t, count)], qs_t[:, lanes(j)], NN)
        if diagonal:
            seen = lax.broadcasted_iota(jnp.int32, s.shape, 0) <= lax.broadcasted_iota(
                jnp.int32, s.shape, 1
            )
            s = jnp.where(seen, s, UNSEEN)
        groups = count * STATS // 8
        s = s.reshape(groups, -1, 8, TILE)
        top = jnp.max(s, axis=1, keepdims=True)
        e = jnp.exp2((s - top) * EXP2_SCALE)
        tops[stat_rows(t, count), lanes(j)] = top.reshape(groups * 8, TILE)
        sums[stat_rows(t, count), lanes(j)] = jnp.sum(e, axis=1).reshape(groups * 8, TILE)
        e_all[tile_rows(t, count), lanes(j)] = e.reshape(count * TILE, TILE)

    def normalise(i, block):
        tops, sums = block[5:]
        rows = STATS * (prompt_tiles + i + 1)
        top = tops[0:rows]
        weight = jnp.exp2((top - jnp.max(top, axis=0, keepdims=True)) * EXP2_SCALE)
        total = jnp.sum(weight * sums[0:rows], axis=0, keepdims=True)
        slot = lax.broadcasted_iota(jnp.int32, (1, wide), 1) % TILE + i * TILE
        tops[0:rows] = weight * (jnp.where(slot < length, 1.0, 0.0) / total)

    def grad_head(t, count, j, block):
        gs_t, e_all, factors = block[3:6]
        shifted = dot(v_all[tile_rows(t, count)], gs_t[:, lanes(j)], NN)
        groups = count * STATS // 8
        e = e_all[tile_rows(t, count), lanes(j)].reshape(groups, -1, 8, TILE)
        factor = factors[stat_rows(t, count), lanes(j)].reshape(groups, 1, 8, TILE)
        p = (e * factor).reshape(count * TILE, TILE)
        p_s[0 : count * TILE, lanes(j)] = p.astype(BF16)
        l_s[0 : count * TILE, lanes(j)] = (p * shifted).astype(BF16)

    def grad_sums(t, count, block):
        qs, gs = block[:2]
        keys, held = tile_rows(t, count), slice(0, count * TILE)
        dv[keys] += dot(p_s[held], gs[...], NN)
        dk[keys] += dot(l_s[held], qs[...], NN)
        dq_t[...] += dot(k_t[:, keys], l_s[held], NN)

    def finish(i):
        here = slice(i * TILE, (i + 1) * TILE)
        for j in range(GROUP):
            back_ref[here, j * HEAD_DIM : (j + 1) * HEAD_DIM] = (
                (dq_t[:, lanes(j)] * SCALE).T.astype(BF16)
            )

    def scores(t, count):
        for j in range(GROUP):
            score_head(t, count, j, sets[0])

    load_block(0, sets[0])
    sweep(scores, prompt_tiles)
    for j in range(GROUP):
        score_head(prompt_tiles, 1, j, sets[0], diagonal=True)
    normalise(0, sets[0])

    blocks = slots // TILE
    live = lax.div(length + TILE - 1, TILE)
    for i in range(blocks):
        now, later = sets[i % 2], sets[(i + 1) % 2]
        tiles = prompt_tiles + i + 1
        dq_t[...] = jnp.zeros_like(dq_t)

        def grads(t, count):
            for j in range(GROUP):
                grad_head(t, count, j, now)
            grad_sums(t, count, now)

        def both(t, count):
            for j in range(GROUP):
                grad_head(t, count, j, now)
                score_head(t, count, j, later)
            grad_sums(t, count, now)

        if i + 1 < blocks:

            @pl.when(live > i + 1)
            def _():
                load_block(i + 1, later)
                sweep(both, tiles)
                finish(i)
                for j in range(GROUP):
                    score_head(tiles, 1, j, later, diagonal=True)
                normalise(i + 1, later)

        @pl.when(live == i + 1)
        def _():
            sweep(grads, tiles)
            finish(i)

    pg_ref[:, 0:HEAD_DIM] = (dk[0:prompt] * SCALE).astype(BF16)
    pg_ref[:, HEAD_DIM:] = dv[0:prompt].astype(BF16)
    back_ref[:, QW : QW + HEAD_DIM] = (dk[prompt:] * SCALE).astype(BF16)
    back_ref[:, QW + HEAD_DIM :] = dv[prompt:].astype(BF16)
    mine = me_prefix & X_BIT
    copies = [
        (pg_ref.at[pl.ds(times(f + (f & -X_BIT) + (mine ^ bit), share), share)], out.at[f])
        for bit, out in ((0, pg_keep), (X_BIT, pg_give))
        for f in range(half)
    ]
    for copy in start_all([(back_ref, back_out)] + copies, sems):
        copy.wait()


def attend(place, x, pkv):
    slots = KV_HEADS * (x.shape[1] - DELTA_ROWS) // COLUMNS
    half, share, prompt_width = pkv[0].shape
    responses = 2 * half
    prompt = responses * share
    keys = slots + prompt
    wide = GROUP * TILE
    outs = [((slots, BACK_W), BF16)] + [((half, share, prompt_width), BF16)] * 2
    stats = pltpu.VMEM((keys // TILE * STATS, wide), F32)
    one_set = [
        pltpu.VMEM((wide, HEAD_DIM), BF16),
        pltpu.VMEM((wide, HEAD_DIM), BF16),
        pltpu.VMEM((HEAD_DIM, wide), BF16),
        pltpu.VMEM((2 * HEAD_DIM, wide), BF16),
        pltpu.VMEM((keys, wide), F32),
        stats,
        stats,
    ]
    return pl.pallas_call(
        attend_kernel,
        in_specs=[SMEM, VMEM, ANY, ANY],
        out_specs=[HBM] * len(outs),
        out_shape=[pltpu.HBM(shape, dtype) for shape, dtype in outs],
        scratch_shapes=[
            pltpu.VMEM((prompt, prompt_width), BF16),
            pltpu.VMEM((slots, BACK_W), BF16),
            pltpu.VMEM((prompt, prompt_width), BF16),
            pltpu.SemaphoreType.DMA((1 + responses,)),
            pltpu.VMEM((keys, HEAD_DIM), BF16),
            pltpu.VMEM((keys, 2 * HEAD_DIM), BF16),
            pltpu.VMEM((HEAD_DIM, keys), BF16),
            pltpu.VMEM((2 * TILE, wide), BF16),
            pltpu.VMEM((2 * TILE, wide), BF16),
            pltpu.VMEM((HEAD_DIM, wide), F32),
            pltpu.VMEM((keys, HEAD_DIM), F32),
            pltpu.VMEM((keys, HEAD_DIM), F32),
        ]
        + one_set * 2,
        compiler_params=params(50),
        cost_estimate=pl.CostEstimate(
            flops=10 * slots * keys * QW, transcendentals=0, bytes_accessed=8 * slots * QW
        ),
        name="attend",
    )(place, pltpu.with_memory_space_constraint(x, pltpu.VMEM), *pkv)


def core_kernel(place_ref, mine_ref, got_ref, keep_ref, give_ref, total):
    total[...] = mine_ref[...].astype(F32) + got_ref[...].astype(F32)
    core = place_ref[1] & CORE_BIT
    for f in range(keep_ref.shape[0]):
        keep_ref[f] = total[2 * f + core]
        give_ref[f] = total[2 * f + 1 - core]


def sum_over_x(place, mine, got):
    count, share, width = mine.shape
    part = jax.ShapeDtypeStruct((count // 2, share, width), F32)
    return pl.pallas_call(
        core_kernel,
        in_specs=[SMEM, VMEM, VMEM],
        out_specs=[VMEM] * 2,
        out_shape=[part] * 2,
        scratch_shapes=[pltpu.VMEM(mine.shape, F32)],
        compiler_params=params(8),
        cost_estimate=pl.CostEstimate(flops=5 * 10**10, transcendentals=0, bytes_accessed=2**20),
        name="sum_over_x",
    )(place, mine, got)


def z_kernel(place_ref, mine_ref, got_ref, *refs):
    outs, total = refs[:-1], refs[-1]
    total[...] = mine_ref[...] + got_ref[...]
    z = place_ref[1] // (2 * X_BIT)
    for d, out in enumerate(outs):
        out[...] = total[z ^ d]


def sum_over_cores(place, mine, got):
    count, share, width = mine.shape
    return pl.pallas_call(
        z_kernel,
        in_specs=[SMEM, VMEM, VMEM],
        out_specs=[VMEM] * count,
        out_shape=[jax.ShapeDtypeStruct((share, width), F32)] * count,
        scratch_shapes=[pltpu.VMEM(mine.shape, F32)],
        compiler_params=params(8),
        name="sum_over_cores",
    )(place, mine, got)


def swap(value, axis, d):
    return lax.ppermute(value, axis, [(i, i ^ d) for i in range(lax.axis_size(axis))])


def swap_across(value):
    sizes = lax.axis_size("prefix"), lax.axis_size("resp")
    pairs = [(p * sizes[1] + r, (p ^ X_BIT) * sizes[1] + (r ^ 1)) for p in range(sizes[0]) for r in range(sizes[1])]
    return lax.ppermute(value, ("prefix", "resp"), pairs)


def local(
    resp_query,
    resp_keys,
    resp_values,
    resp_out,
    resp_grad,
    prompt_keys,
    prompt_values,
    resp_lengths,
):
    head = lax.axis_index("resp")
    rows = resp_query.shape[1]
    place = jnp.stack([resp_lengths[0], lax.axis_index("prefix")])
    send = pack(resp_query[0], resp_grad[0], resp_out[0], resp_keys[0], resp_values[0])
    x = lax.all_to_all(send, "resp", 0, 0, tiled=True)
    prompt_keys, prompt_values, _ = lax.optimization_barrier((prompt_keys, prompt_values, send))
    cut = lambda a, h: lax.dynamic_slice_in_dim(a, h * HEAD_DIM, HEAD_DIM, 1)
    both = lambda h: jnp.concatenate([cut(prompt_keys, h), cut(prompt_values, h)], axis=1)[None]
    pkv, first = both(head), swap_across(both(head ^ 1))
    pkv = jnp.concatenate([pkv, first])
    for bit in GATHER_BITS[1:-1]:
        pkv = jnp.concatenate([pkv, swap(pkv, "prefix", 1 << bit)])
    pkv = [pkv, swap(pkv, "prefix", 1 << GATHER_BITS[-1])]
    back, keep, give = attend(place, x, pkv)
    back = lax.all_to_all(back.reshape(KV_HEADS, rows, BACK_W), "resp", 0, 0, tiled=True)
    keep, give = sum_over_x(place, keep, swap(give, "prefix", X_BIT))
    parts = sum_over_cores(place, keep, swap(give, "prefix", CORE_BIT))
    parts = [parts[0]] + [swap(parts[d], "prefix", 2 * X_BIT * d) for d in range(1, len(parts))]
    share, width = parts[0].shape
    total = sum(parts[1:], parts[0]).astype(BF16).reshape(KV_HEADS, share // KV_HEADS, width)
    back, total = lax.optimization_barrier((back, total))
    total = lax.all_to_all(total, "resp", 0, 0, tiled=True)
    total = total.reshape(KV_HEADS, share // KV_HEADS, 2, HEAD_DIM).transpose(2, 1, 0, 3)
    total = total.reshape(2, share // KV_HEADS, KV_HEADS * HEAD_DIM)
    grad_query, grad_keys, grad_values = unpack(back)
    return (grad_query[None], grad_keys[None], grad_values[None], total[0], total[1])


def solution(mesh):
    return jax.shard_map(
        local,
        mesh=mesh,
        in_specs=(
            P("prefix", "resp", None),
            P("prefix", "resp", None),
            P("prefix", "resp", None),
            P("prefix", "resp", None),
            P("prefix", "resp", None),
            P("prefix", None),
            P("prefix", None),
            P("prefix"),
        ),
        out_specs=(
            P("prefix", "resp", None),
            P("prefix", "resp", None),
            P("prefix", "resp", None),
            P(("prefix", "resp"), None),
            P(("prefix", "resp"), None),
        ),
        check_vma=False,
    )
```

```python
import jax
import jax.numpy as jnp
from jax import lax
from jax.experimental import pallas as pl
from jax.experimental.pallas import tpu as pltpu
from jax.sharding import PartitionSpec as P

HEADS = 40
KV_HEADS = 8
GROUP = HEADS // KV_HEADS
HEAD_DIM = 128
SCALE = HEAD_DIM ** (-0.5)
EXP2_SCALE = SCALE * 1.4426950408889634
QW = GROUP * HEAD_DIM
TILE = 256
STAT_KEYS = 128
UNSEEN = -1e30
PACK_ROWS = 32
GATHER_BITS = (1, 0, 2, 3)
COLUMNS = 2 + 2 * GROUP
DELTA_ROWS = 16
BACK_W = QW + 2 * HEAD_DIM
X_BIT, CORE_BIT = 2, 1

NN = (((1,), (0,)), ((), ()))
BF16 = jnp.bfloat16
F32 = jnp.float32
ANY = pl.BlockSpec(memory_space=pl.ANY)
HBM = pl.BlockSpec(memory_space=pltpu.HBM)
VMEM = pl.BlockSpec(memory_space=pltpu.VMEM)
SMEM = pl.BlockSpec(memory_space=pltpu.SMEM)


def dot(a, b, dims):
    return lax.dot_general(a, b, dims, preferred_element_type=F32)


def params(mib):
    return pltpu.CompilerParams(vmem_limit_bytes=mib * 1024 * 1024)


def times(index, size):
    return pl.multiple_of(index * size, size)


def send_rows(c, n):
    first = (c * COLUMNS + n) * PACK_ROWS
    return slice(first, first + PACK_ROWS)


def gather_mask(index):
    return sum(((index >> step) & 1) << bit for step, bit in enumerate(GATHER_BITS))


def start_all(copies, sems):
    started = [pltpu.make_async_copy(src, dst, sems.at[n]) for n, (src, dst) in enumerate(copies)]
    for copy in started:
        copy.start()
    return started


def pack_kernel(q_in, g_in, o_in, k_in, v_in, send_out, q_ref, g_ref, o_ref, k_ref, v_ref, send_ref, left_ref, sems, out_sems):
    ins = ((q_in, q_ref), (g_in, g_ref), (o_in, o_ref), (k_in, k_ref), (v_in, v_ref))
    steps = q_ref.shape[0] // PACK_ROWS
    arriving = []
    for c in range(steps):
        rows = slice(c * PACK_ROWS, (c + 1) * PACK_ROWS)
        arriving.append(start_all([(src.at[rows], dst.at[rows]) for src, dst in ins], sems.at[c]))
    row = lax.broadcasted_iota(jnp.int32, (QW, HEAD_DIM), 0) // HEAD_DIM
    lane = lax.broadcasted_iota(jnp.int32, (QW, HEAD_DIM), 1)
    ones = jnp.where((lane >= 3 * row) & (lane < 3 * row + 3), 1.0, 0.0).astype(BF16)
    leaving = []
    for c in range(steps):
        rows = slice(c * PACK_ROWS, (c + 1) * PACK_ROWS)
        for copy in arriving[c]:
            copy.wait()
        highs, lows = [], []
        for h in range(KV_HEADS):
            columns = [(k_ref, h), (v_ref, h)]
            columns += [(q_ref, h * GROUP + j) for j in range(GROUP)]
            columns += [(g_ref, h * GROUP + j) for j in range(GROUP)]
            for n, (ref, col) in enumerate(columns):
                send_ref[h, send_rows(c, n)] = ref[rows, col * HEAD_DIM : (col + 1) * HEAD_DIM]
            wide = slice(h * QW, (h + 1) * QW)
            product = g_ref[rows, wide].astype(F32) * o_ref[rows, wide].astype(F32)
            high = product.astype(BF16)
            highs.append(high)
            lows.append((product - high.astype(F32)).astype(BF16))
        part = slice(c * COLUMNS * PACK_ROWS, (c + 1) * COLUMNS * PACK_ROWS)
        leaving += start_all([(send_ref.at[:, part], send_out.at[:, part])], out_sems.at[pl.ds(c, 1)])
        left = dot(jnp.concatenate(highs), ones, NN) + dot(jnp.concatenate(lows), ones, NN)
        for h in range(KV_HEADS):
            left_ref[h, rows] = left[h * PACK_ROWS : (h + 1) * PACK_ROWS]
    part = lax.broadcasted_iota(jnp.int32, (DELTA_ROWS, q_ref.shape[0]), 0) % 3
    last = slice(steps * COLUMNS * PACK_ROWS, steps * COLUMNS * PACK_ROWS + DELTA_ROWS)
    for h in range(KV_HEADS):
        left = left_ref[h].T[0:DELTA_ROWS]
        first = left.astype(BF16).astype(F32)
        second = (left - first).astype(BF16).astype(F32)
        third = left - first - second
        send_ref[h, last] = jnp.where(part == 0, first, jnp.where(part == 1, second, third)).astype(BF16)
    leaving += start_all([(send_ref.at[:, last], send_out.at[:, last])], out_sems.at[pl.ds(steps, 1)])
    for copy in leaving:
        copy.wait()


def pack(q, g, o, k, v):
    rows = q.shape[0]
    steps = rows // PACK_ROWS
    send = (KV_HEADS, rows * COLUMNS + DELTA_ROWS, HEAD_DIM)
    return pl.pallas_call(
        pack_kernel,
        in_specs=[HBM] * 5,
        out_specs=HBM,
        out_shape=pltpu.HBM(send, BF16),
        scratch_shapes=[pltpu.VMEM(a.shape, BF16) for a in (q, g, o, k, v)]
        + [
            pltpu.VMEM(send, BF16),
            pltpu.VMEM((KV_HEADS, rows, HEAD_DIM), F32),
            pltpu.SemaphoreType.DMA((steps, 5)),
            pltpu.SemaphoreType.DMA((steps + 1,)),
        ],
        compiler_params=params(60),
        name="pack",
    )(q, g, o, k, v)


def unpack_kernel(back_ref, q_ref, k_ref, v_ref, sems):
    copies = []
    for h in range(KV_HEADS):
        thin = slice(h * HEAD_DIM, (h + 1) * HEAD_DIM)
        wide = slice(h * QW, (h + 1) * QW)
        copies.append((back_ref.at[h, :, 0:QW], q_ref.at[:, wide]))
        copies.append((back_ref.at[h, :, QW : QW + HEAD_DIM], k_ref.at[:, thin]))
        copies.append((back_ref.at[h, :, QW + HEAD_DIM :], v_ref.at[:, thin]))
    for copy in start_all(copies, sems):
        copy.wait()


def unpack(back):
    rows = back.shape[1]
    return pl.pallas_call(
        unpack_kernel,
        in_specs=[ANY],
        out_specs=[ANY] * 3,
        out_shape=[
            jax.ShapeDtypeStruct((rows, KV_HEADS * QW), BF16),
            jax.ShapeDtypeStruct((rows, KV_HEADS * HEAD_DIM), BF16),
            jax.ShapeDtypeStruct((rows, KV_HEADS * HEAD_DIM), BF16),
        ],
        scratch_shapes=[pltpu.SemaphoreType.DMA((3 * KV_HEADS,))],
        compiler_params=params(4),
        name="unpack",
    )(back)


def attend_kernel(place_ref, x_ref, pkv_low, pkv_high, back_out, pg_keep, pg_give, *refs):
    pkv_ref, back_ref, pg_ref, sems, k_all, v_all, k_t = refs[:7]
    p_s, l_s, dk, dv = refs[7:11]
    sets = [refs[11:18], refs[18:25]]
    prompt = pkv_ref.shape[0]
    run = (x_ref.shape[1] - DELTA_ROWS) // COLUMNS
    slots = KV_HEADS * run
    prompt_tiles = prompt // TILE
    length, me_prefix = place_ref[0], place_ref[1]
    half = pkv_low.shape[0]
    sources = 2 * half
    share = prompt // sources
    copies = [
        ((pkv_low, pkv_high)[f // half].at[f % half], pkv_ref.at[pl.ds(times(me_prefix ^ gather_mask(f), share), share)])
        for f in range(sources)
    ]
    copies = start_all(copies, sems)
    back_ref[...] = jnp.zeros_like(back_ref)
    dk[...] = jnp.zeros_like(dk)
    dv[...] = jnp.zeros_like(dv)
    for block in sets:
        block[3][:, HEAD_DIM + DELTA_ROWS :] = jnp.zeros((GROUP, HEAD_DIM - DELTA_ROWS, TILE), BF16)
    for copy in copies:
        copy.wait()

    def flip(a):
        return a.astype(F32).T.astype(BF16)

    def slots_of(b, n):
        return jnp.concatenate([x_ref[b, send_rows(c, n)] for c in range(run // PACK_ROWS)])

    k_all[0:prompt] = pkv_ref[:, 0:HEAD_DIM]
    v_all[0:prompt, 0:HEAD_DIM] = pkv_ref[:, HEAD_DIM:]
    for b in range(KV_HEADS):
        own = slice(prompt + b * run, prompt + (b + 1) * run)
        k_all[own] = slots_of(b, 0)
        v_all[own, 0:HEAD_DIM] = slots_of(b, 1)
    v_all[:, HEAD_DIM:] = jnp.full((prompt + slots, HEAD_DIM), -1.0, BF16)
    for t in range((prompt + slots) // TILE):
        block = slice(t * TILE, (t + 1) * TILE)
        k_t[:, block] = flip(k_all[block])

    def key_count(i):
        return prompt + (i + 1) * TILE

    def key_parts(i):
        return (0, prompt), (prompt, key_count(i))

    def load_head(i, j, block):
        qs, gs, qs_t, gs_t = block[:4]
        sources = range(i * TILE // run, (i + 1) * TILE // run)

        def column(n):
            return jnp.concatenate(
                [
                    x_ref[b, pl.ds(times(c * COLUMNS + n, PACK_ROWS), PACK_ROWS)]
                    for b in sources
                    for c in range(run // PACK_ROWS)
                ]
            )

        q, g = column(2 + j), column(2 + GROUP + j)
        qs[j] = q
        gs[j] = g
        qs_t[j] = flip(q)
        gs_t[j, 0:HEAD_DIM] = flip(g)
        delta_t = jnp.concatenate([x_ref[b, run * COLUMNS :] for b in sources], axis=1).astype(F32)
        part = lax.broadcasted_iota(jnp.int32, delta_t.shape, 0)
        mine = (part >= 3 * j) & (part < 3 * j + 3)
        gs_t[j, HEAD_DIM : HEAD_DIM + DELTA_ROWS] = jnp.where(mine, delta_t, 0.0).astype(BF16)

    def score_head(i, j, block):
        qs_t, _, e_all, tops, sums = block[2:]
        for start, stop in key_parts(i):
            s = dot(k_all[start:stop], qs_t[j], NN)
            for at in range(start, stop, STAT_KEYS):
                part = s[at - start : at - start + STAT_KEYS]
                past = at + TILE - stop
                if start == prompt and past >= 0:
                    key = past + lax.broadcasted_iota(jnp.int32, part.shape, 0)
                    seen = key <= lax.broadcasted_iota(jnp.int32, part.shape, 1)
                    part = jnp.where(seen, part, UNSEEN)
                part = part.reshape(-1, 8, TILE)
                top = jnp.max(part, axis=0)
                e = jnp.exp2((part - top[None]) * EXP2_SCALE)
                stat = slice(at // STAT_KEYS * 8, at // STAT_KEYS * 8 + 8)
                tops[j, stat] = top
                sums[j, stat] = jnp.sum(e, axis=0)
                e_all[j, at : at + STAT_KEYS] = e.reshape(STAT_KEYS, TILE)

    def normalise(i, j, block):
        tops, sums = block[5:]
        count = key_count(i) // STAT_KEYS * 8
        top = tops[j, 0:count]
        weight = jnp.exp2((top - jnp.max(top, axis=0, keepdims=True)) * EXP2_SCALE)
        total = jnp.sum(weight * sums[j, 0:count], axis=0, keepdims=True)
        slot = lax.broadcasted_iota(jnp.int32, (1, TILE), 1) + i * TILE
        tops[j, 0:count] = weight * (jnp.where(slot < length, 1.0, 0.0) / total)

    def prepare_head(i, j, block):
        load_head(i, j, block)
        score_head(i, j, block)
        normalise(i, j, block)

    def grad_head(i, j, block):
        qs, gs, _, gs_t, e_all, factors, _ = block
        for start, stop in key_parts(i):
            shifted = dot(v_all[start:stop], gs_t[j], NN)
            for at in range(start, stop, STAT_KEYS):
                keys = slice(at, at + STAT_KEYS)
                factor = factors[j, at // STAT_KEYS * 8 : at // STAT_KEYS * 8 + 8]
                p = (e_all[j, keys].reshape(-1, 8, TILE) * factor[None]).reshape(STAT_KEYS, TILE)
                p_s[keys] = p.astype(BF16)
                l_s[keys] = (p * shifted[at - start : at - start + STAT_KEYS]).astype(BF16)
        keys = slice(0, key_count(i))
        dv[keys] += dot(p_s[keys], gs[j], NN)
        dk[keys] += dot(l_s[keys], qs[j], NN)
        dq_t = dot(k_t[:, keys], l_s[keys], NN)
        back_ref[i * TILE : (i + 1) * TILE, pl.ds(times(j, HEAD_DIM), HEAD_DIM)] = (
            (dq_t * SCALE).T.astype(BF16)
        )

    def each_head(body):
        def step(j, carry):
            body(j)
            return carry

        lax.fori_loop(0, GROUP, step, 0)

    each_head(lambda j: prepare_head(0, j, sets[0]))

    blocks = slots // TILE
    live = lax.div(length + TILE - 1, TILE)
    for i in range(blocks):
        now, later = sets[i % 2], sets[(i + 1) % 2]

        def both(j):
            grad_head(i, j, now)
            prepare_head(i + 1, j, later)

        if i + 1 < blocks:

            @pl.when(live > i + 1)
            def _():
                each_head(both)

        @pl.when(live == i + 1)
        def _():
            each_head(lambda j: grad_head(i, j, now))

    pg_ref[:, 0:HEAD_DIM] = (dk[0:prompt] * SCALE).astype(BF16)
    pg_ref[:, HEAD_DIM:] = dv[0:prompt].astype(BF16)
    back_ref[:, QW : QW + HEAD_DIM] = (dk[prompt:] * SCALE).astype(BF16)
    back_ref[:, QW + HEAD_DIM :] = dv[prompt:].astype(BF16)
    mine = me_prefix & X_BIT
    copies = [
        (pg_ref.at[pl.ds(times(f + (f & -X_BIT) + (mine ^ bit), share), share)], out.at[f])
        for bit, out in ((0, pg_keep), (X_BIT, pg_give))
        for f in range(half)
    ]
    for copy in start_all([(back_ref, back_out)] + copies, sems):
        copy.wait()


def attend(place, x, pkv):
    slots = KV_HEADS * (x.shape[1] - DELTA_ROWS) // COLUMNS
    half, share, prompt_width = pkv[0].shape
    responses = 2 * half
    prompt = responses * share
    keys = slots + prompt
    outs = [((slots, BACK_W), BF16)] + [((half, share, prompt_width), BF16)] * 2
    stats = pltpu.VMEM((GROUP, keys // STAT_KEYS * 8, TILE), F32)
    one_set = [
        pltpu.VMEM((GROUP, TILE, HEAD_DIM), BF16),
        pltpu.VMEM((GROUP, TILE, HEAD_DIM), BF16),
        pltpu.VMEM((GROUP, HEAD_DIM, TILE), BF16),
        pltpu.VMEM((GROUP, 2 * HEAD_DIM, TILE), BF16),
        pltpu.VMEM((GROUP, keys, TILE), F32),
        stats,
        stats,
    ]
    return pl.pallas_call(
        attend_kernel,
        in_specs=[SMEM, VMEM, ANY, ANY],
        out_specs=[HBM] * len(outs),
        out_shape=[pltpu.HBM(shape, dtype) for shape, dtype in outs],
        scratch_shapes=[
            pltpu.VMEM((prompt, prompt_width), BF16),
            pltpu.VMEM((slots, BACK_W), BF16),
            pltpu.VMEM((prompt, prompt_width), BF16),
            pltpu.SemaphoreType.DMA((1 + responses,)),
            pltpu.VMEM((keys, HEAD_DIM), BF16),
            pltpu.VMEM((keys, 2 * HEAD_DIM), BF16),
            pltpu.VMEM((HEAD_DIM, keys), BF16),
            pltpu.VMEM((keys, TILE), BF16),
            pltpu.VMEM((keys, TILE), BF16),
            pltpu.VMEM((keys, HEAD_DIM), F32),
            pltpu.VMEM((keys, HEAD_DIM), F32),
        ]
        + one_set * 2,
        compiler_params=params(50),
        cost_estimate=pl.CostEstimate(
            flops=10 * slots * keys * QW, transcendentals=0, bytes_accessed=8 * slots * QW
        ),
        name="attend",
    )(place, pltpu.with_memory_space_constraint(x, pltpu.VMEM), *pkv)


def core_kernel(place_ref, mine_ref, got_ref, keep_ref, give_ref, total):
    total[...] = mine_ref[...].astype(F32) + got_ref[...].astype(F32)
    core = place_ref[1] & CORE_BIT
    for f in range(keep_ref.shape[0]):
        keep_ref[f] = total[2 * f + core]
        give_ref[f] = total[2 * f + 1 - core]


def sum_over_x(place, mine, got):
    count, share, width = mine.shape
    part = jax.ShapeDtypeStruct((count // 2, share, width), F32)
    return pl.pallas_call(
        core_kernel,
        in_specs=[SMEM, VMEM, VMEM],
        out_specs=[VMEM] * 2,
        out_shape=[part] * 2,
        scratch_shapes=[pltpu.VMEM(mine.shape, F32)],
        compiler_params=params(8),
        cost_estimate=pl.CostEstimate(flops=5 * 10**10, transcendentals=0, bytes_accessed=2**20),
        name="sum_over_x",
    )(place, mine, got)


def z_kernel(place_ref, mine_ref, got_ref, *refs):
    outs, total = refs[:-1], refs[-1]
    total[...] = mine_ref[...] + got_ref[...]
    z = place_ref[1] // (2 * X_BIT)
    for d, out in enumerate(outs):
        out[...] = total[z ^ d]


def sum_over_cores(place, mine, got):
    count, share, width = mine.shape
    return pl.pallas_call(
        z_kernel,
        in_specs=[SMEM, VMEM, VMEM],
        out_specs=[VMEM] * count,
        out_shape=[jax.ShapeDtypeStruct((share, width), F32)] * count,
        scratch_shapes=[pltpu.VMEM(mine.shape, F32)],
        compiler_params=params(8),
        name="sum_over_cores",
    )(place, mine, got)


def swap(value, axis, d):
    return lax.ppermute(value, axis, [(i, i ^ d) for i in range(lax.axis_size(axis))])


def swap_across(value):
    sizes = lax.axis_size("prefix"), lax.axis_size("resp")
    pairs = [(p * sizes[1] + r, (p ^ X_BIT) * sizes[1] + (r ^ 1)) for p in range(sizes[0]) for r in range(sizes[1])]
    return lax.ppermute(value, ("prefix", "resp"), pairs)


def local(
    resp_query,
    resp_keys,
    resp_values,
    resp_out,
    resp_grad,
    prompt_keys,
    prompt_values,
    resp_lengths,
):
    head = lax.axis_index("resp")
    rows = resp_query.shape[1]
    place = jnp.stack([resp_lengths[0], lax.axis_index("prefix")])
    send = pack(resp_query[0], resp_grad[0], resp_out[0], resp_keys[0], resp_values[0])
    x = lax.all_to_all(send, "resp", 0, 0, tiled=True)
    prompt_keys, prompt_values, _ = lax.optimization_barrier((prompt_keys, prompt_values, send))
    cut = lambda a, h: lax.dynamic_slice_in_dim(a, h * HEAD_DIM, HEAD_DIM, 1)
    both = lambda h: jnp.concatenate([cut(prompt_keys, h), cut(prompt_values, h)], axis=1)[None]
    pkv, first = both(head), swap_across(both(head ^ 1))
    pkv = jnp.concatenate([pkv, first])
    for bit in GATHER_BITS[1:-1]:
        pkv = jnp.concatenate([pkv, swap(pkv, "prefix", 1 << bit)])
    pkv = [pkv, swap(pkv, "prefix", 1 << GATHER_BITS[-1])]
    back, keep, give = attend(place, x, pkv)
    back = lax.all_to_all(back.reshape(KV_HEADS, rows, BACK_W), "resp", 0, 0, tiled=True)
    keep, give = sum_over_x(place, keep, swap(give, "prefix", X_BIT))
    parts = sum_over_cores(place, keep, swap(give, "prefix", CORE_BIT))
    parts = [parts[0]] + [swap(parts[d], "prefix", 2 * X_BIT * d) for d in range(1, len(parts))]
    share, width = parts[0].shape
    total = sum(parts[1:], parts[0]).astype(BF16).reshape(KV_HEADS, share // KV_HEADS, width)
    back, total = lax.optimization_barrier((back, total))
    total = lax.all_to_all(total, "resp", 0, 0, tiled=True)
    total = total.reshape(KV_HEADS, share // KV_HEADS, 2, HEAD_DIM).transpose(2, 1, 0, 3)
    total = total.reshape(2, share // KV_HEADS, KV_HEADS * HEAD_DIM)
    grad_query, grad_keys, grad_values = unpack(back)
    return (grad_query[None], grad_keys[None], grad_values[None], total[0], total[1])


def solution(mesh):
    return jax.shard_map(
        local,
        mesh=mesh,
        in_specs=(
            P("prefix", "resp", None),
            P("prefix", "resp", None),
            P("prefix", "resp", None),
            P("prefix", "resp", None),
            P("prefix", "resp", None),
            P("prefix", None),
            P("prefix", None),
            P("prefix"),
        ),
        out_specs=(
            P("prefix", "resp", None),
            P("prefix", "resp", None),
            P("prefix", "resp", None),
            P(("prefix", "resp"), None),
            P(("prefix", "resp"), None),
        ),
        check_vma=False,
    )
```

```python
import jax
import jax.numpy as jnp
from jax import lax
from jax.experimental import pallas as pl
from jax.experimental.pallas import tpu as pltpu
from jax.sharding import Mesh
from jax.sharding import PartitionSpec as P

HEADS = 40
KV_HEADS = 8
GROUP = HEADS // KV_HEADS
HEAD_DIM = 128
SCALE = HEAD_DIM ** (-0.5)
EXP2_SCALE = SCALE * 1.4426950408889634
QW = GROUP * HEAD_DIM
TILE = 256
STATS = 16
UNSEEN = -1e30
PACK_ROWS = 32
GATHER_BITS = (1, 0, 2, 3)
GATHER_STEPS = (("core", 1), ("z", 1), ("z", 2))
COLUMNS = 2 + 2 * GROUP
DELTA_ROWS = 16
BACK_W = QW + 2 * HEAD_DIM
PREFIX = (("z", 4), ("x", 2), ("core", 2))
AXES = tuple(name for name, size in PREFIX)

NN = (((1,), (0,)), ((), ()))
BF16 = jnp.bfloat16
F32 = jnp.float32
ANY = pl.BlockSpec(memory_space=pl.ANY)
HBM = pl.BlockSpec(memory_space=pltpu.HBM)
VMEM = pl.BlockSpec(memory_space=pltpu.VMEM)
SMEM = pl.BlockSpec(memory_space=pltpu.SMEM)


def dot(a, b, dims):
    return lax.dot_general(a, b, dims, preferred_element_type=F32)


def params(mib):
    return pltpu.CompilerParams(vmem_limit_bytes=mib * 1024 * 1024)


def times(index, size):
    return pl.multiple_of(index * size, size)


def send_rows(c, n):
    first = (c * COLUMNS + n) * PACK_ROWS
    return slice(first, first + PACK_ROWS)


def gather_mask(index):
    return sum(((index >> step) & 1) << bit for step, bit in enumerate(GATHER_BITS))


def start_all(copies, sems):
    started = [pltpu.make_async_copy(src, dst, sems.at[n]) for n, (src, dst) in enumerate(copies)]
    for copy in started:
        copy.start()
    return started


def pack_kernel(q_in, g_in, o_in, k_in, v_in, send_out, q_ref, g_ref, o_ref, k_ref, v_ref, send_ref, left_ref, sems, out_sems):
    ins = ((q_in, q_ref), (g_in, g_ref), (o_in, o_ref), (k_in, k_ref), (v_in, v_ref))
    steps = q_ref.shape[0] // PACK_ROWS
    arriving = []
    for c in range(steps):
        rows = slice(c * PACK_ROWS, (c + 1) * PACK_ROWS)
        arriving.append(start_all([(src.at[rows], dst.at[rows]) for src, dst in ins], sems.at[c]))
    row = lax.broadcasted_iota(jnp.int32, (QW, HEAD_DIM), 0) // HEAD_DIM
    lane = lax.broadcasted_iota(jnp.int32, (QW, HEAD_DIM), 1)
    ones = jnp.where((lane >= 3 * row) & (lane < 3 * row + 3), 1.0, 0.0).astype(BF16)
    leaving = []
    for c in range(steps):
        rows = slice(c * PACK_ROWS, (c + 1) * PACK_ROWS)
        for copy in arriving[c]:
            copy.wait()
        highs, lows = [], []
        for h in range(KV_HEADS):
            columns = [(k_ref, h), (v_ref, h)]
            columns += [(q_ref, h * GROUP + j) for j in range(GROUP)]
            columns += [(g_ref, h * GROUP + j) for j in range(GROUP)]
            for n, (ref, col) in enumerate(columns):
                send_ref[h, send_rows(c, n)] = ref[rows, col * HEAD_DIM : (col + 1) * HEAD_DIM]
            wide = slice(h * QW, (h + 1) * QW)
            product = g_ref[rows, wide].astype(F32) * o_ref[rows, wide].astype(F32)
            high = product.astype(BF16)
            highs.append(high)
            lows.append((product - high.astype(F32)).astype(BF16))
        part = slice(c * COLUMNS * PACK_ROWS, (c + 1) * COLUMNS * PACK_ROWS)
        leaving += start_all([(send_ref.at[:, part], send_out.at[:, part])], out_sems.at[pl.ds(c, 1)])
        left = dot(jnp.concatenate(highs), ones, NN) + dot(jnp.concatenate(lows), ones, NN)
        for h in range(KV_HEADS):
            left_ref[h, rows] = left[h * PACK_ROWS : (h + 1) * PACK_ROWS]
    part = lax.broadcasted_iota(jnp.int32, (DELTA_ROWS, q_ref.shape[0]), 0) % 3
    last = slice(steps * COLUMNS * PACK_ROWS, steps * COLUMNS * PACK_ROWS + DELTA_ROWS)
    for h in range(KV_HEADS):
        left = left_ref[h].T[0:DELTA_ROWS]
        first = left.astype(BF16).astype(F32)
        second = (left - first).astype(BF16).astype(F32)
        third = left - first - second
        send_ref[h, last] = jnp.where(part == 0, first, jnp.where(part == 1, second, third)).astype(BF16)
    leaving += start_all([(send_ref.at[:, last], send_out.at[:, last])], out_sems.at[pl.ds(steps, 1)])
    for copy in leaving:
        copy.wait()


def pack(q, g, o, k, v):
    rows = q.shape[0]
    steps = rows // PACK_ROWS
    send = (KV_HEADS, rows * COLUMNS + DELTA_ROWS, HEAD_DIM)
    return pl.pallas_call(
        pack_kernel,
        in_specs=[HBM] * 5,
        out_specs=HBM,
        out_shape=pltpu.HBM(send, BF16),
        scratch_shapes=[pltpu.VMEM(a.shape, BF16) for a in (q, g, o, k, v)]
        + [
            pltpu.VMEM(send, BF16),
            pltpu.VMEM((KV_HEADS, rows, HEAD_DIM), F32),
            pltpu.SemaphoreType.DMA((steps, 5)),
            pltpu.SemaphoreType.DMA((steps + 1,)),
        ],
        compiler_params=params(60),
        name="pack",
    )(q, g, o, k, v)


def unpack_kernel(back_ref, q_ref, k_ref, v_ref, sems):
    copies = []
    for h in range(KV_HEADS):
        thin = slice(h * HEAD_DIM, (h + 1) * HEAD_DIM)
        wide = slice(h * QW, (h + 1) * QW)
        copies.append((back_ref.at[h, :, 0:QW], q_ref.at[:, wide]))
        copies.append((back_ref.at[h, :, QW : QW + HEAD_DIM], k_ref.at[:, thin]))
        copies.append((back_ref.at[h, :, QW + HEAD_DIM :], v_ref.at[:, thin]))
    for copy in start_all(copies, sems):
        copy.wait()


def unpack(back):
    rows = back.shape[1]
    return pl.pallas_call(
        unpack_kernel,
        in_specs=[ANY],
        out_specs=[ANY] * 3,
        out_shape=[
            jax.ShapeDtypeStruct((rows, KV_HEADS * QW), BF16),
            jax.ShapeDtypeStruct((rows, KV_HEADS * HEAD_DIM), BF16),
            jax.ShapeDtypeStruct((rows, KV_HEADS * HEAD_DIM), BF16),
        ],
        scratch_shapes=[pltpu.SemaphoreType.DMA((3 * KV_HEADS,))],
        compiler_params=params(4),
        name="unpack",
    )(back)


def attend_kernel(place_ref, x_ref, pkv_low, pkv_high, back_out, pg_keep, pg_give, *refs):
    pkv_ref, back_ref, pg_ref, sems, block_sems, k_all, v_all, k_t = refs[:8]
    p_s, l_s, dq_t, dk, dv = refs[8:13]
    sets = [refs[13:20], refs[20:27]]
    prompt = pkv_ref.shape[0]
    run = (x_ref.shape[1] - DELTA_ROWS) // COLUMNS
    slots = KV_HEADS * run
    wide = GROUP * TILE
    prompt_tiles = prompt // TILE
    length, me_prefix = place_ref[0], place_ref[1]
    half = pkv_low.shape[0]
    sources = 2 * half
    share = prompt // sources
    copies = [
        ((pkv_low, pkv_high)[f // half].at[f % half], pkv_ref.at[pl.ds(times(me_prefix ^ gather_mask(f), share), share)])
        for f in range(sources)
    ]
    copies = start_all(copies, sems)
    back_ref[...] = jnp.zeros_like(back_ref)
    dk[...] = jnp.zeros_like(dk)
    dv[...] = jnp.zeros_like(dv)
    for block in sets:
        block[3][HEAD_DIM + DELTA_ROWS :] = jnp.zeros((HEAD_DIM - DELTA_ROWS, wide), BF16)
    for copy in copies:
        copy.wait()

    def flip(a):
        return a.astype(F32).T.astype(BF16)

    def slots_of(b, n):
        return jnp.concatenate([x_ref[b, send_rows(c, n)] for c in range(run // PACK_ROWS)])

    k_all[0:prompt] = pkv_ref[:, 0:HEAD_DIM]
    v_all[0:prompt, 0:HEAD_DIM] = pkv_ref[:, HEAD_DIM:]
    for b in range(KV_HEADS):
        own = slice(prompt + b * run, prompt + (b + 1) * run)
        k_all[own] = slots_of(b, 0)
        v_all[own, 0:HEAD_DIM] = slots_of(b, 1)
    v_all[:, HEAD_DIM:] = jnp.full((prompt + slots, HEAD_DIM), -1.0, BF16)
    for t in range((prompt + slots) // TILE):
        block = slice(t * TILE, (t + 1) * TILE)
        k_t[:, block] = flip(k_all[block])

    def lanes(j):
        return slice(j * TILE, (j + 1) * TILE)

    def tile_rows(t, count):
        return pl.ds(times(t, TILE), count * TILE)

    def stat_rows(t, count):
        return pl.ds(times(t, STATS), count * STATS)

    def sweep(body, tiles):
        def pair(n, carry):
            body(2 * n, 2)
            return carry

        lax.fori_loop(0, tiles // 2, pair, 0)
        if tiles % 2:
            body(tiles - 1, 1)

    def load_block(i, block):
        qs, gs, qs_t, gs_t = block[:4]
        sources = range(i * TILE // run, (i + 1) * TILE // run)
        delta_t = jnp.concatenate([x_ref[b, run * COLUMNS :] for b in sources], axis=1).astype(F32)
        part = lax.broadcasted_iota(jnp.int32, delta_t.shape, 0)
        for j in range(GROUP):
            q = jnp.concatenate([slots_of(b, 2 + j) for b in sources])
            g = jnp.concatenate([slots_of(b, 2 + GROUP + j) for b in sources])
            qs[lanes(j)] = q
            gs[lanes(j)] = g
            qs_t[:, lanes(j)] = flip(q)
            gs_t[0:HEAD_DIM, lanes(j)] = flip(g)
            mine = (part >= 3 * j) & (part < 3 * j + 3)
            gs_t[HEAD_DIM : HEAD_DIM + DELTA_ROWS, lanes(j)] = jnp.where(mine, delta_t, 0.0).astype(BF16)

    def score_head(t, count, j, block, diagonal=False):
        qs_t, _, e_all, tops, sums = block[2:]
        s = dot(k_all[tile_rows(t, count)], qs_t[:, lanes(j)], NN)
        if diagonal:
            seen = lax.broadcasted_iota(jnp.int32, s.shape, 0) <= lax.broadcasted_iota(
                jnp.int32, s.shape, 1
            )
            s = jnp.where(seen, s, UNSEEN)
        groups = count * STATS // 8
        s = s.reshape(groups, -1, 8, TILE)
        top = jnp.max(s, axis=1, keepdims=True)
        e = jnp.exp2((s - top) * EXP2_SCALE)
        tops[stat_rows(t, count), lanes(j)] = top.reshape(groups * 8, TILE)
        sums[stat_rows(t, count), lanes(j)] = jnp.sum(e, axis=1).reshape(groups * 8, TILE)
        e_all[tile_rows(t, count), lanes(j)] = e.reshape(count * TILE, TILE)

    def normalise(i, block):
        tops, sums = block[5:]
        rows = STATS * (prompt_tiles + i + 1)
        top = tops[0:rows]
        weight = jnp.exp2((top - jnp.max(top, axis=0, keepdims=True)) * EXP2_SCALE)
        total = jnp.sum(weight * sums[0:rows], axis=0, keepdims=True)
        slot = lax.broadcasted_iota(jnp.int32, (1, wide), 1) % TILE + i * TILE
        tops[0:rows] = weight * (jnp.where(slot < length, 1.0, 0.0) / total)

    def grad_head(t, count, j, block):
        gs_t, e_all, factors = block[3:6]
        shifted = dot(v_all[tile_rows(t, count)], gs_t[:, lanes(j)], NN)
        groups = count * STATS // 8
        e = e_all[tile_rows(t, count), lanes(j)].reshape(groups, -1, 8, TILE)
        factor = factors[stat_rows(t, count), lanes(j)].reshape(groups, 1, 8, TILE)
        p = (e * factor).reshape(count * TILE, TILE)
        p_s[0 : count * TILE, lanes(j)] = p.astype(BF16)
        l_s[0 : count * TILE, lanes(j)] = (p * shifted).astype(BF16)

    def grad_sums(t, count, block):
        qs, gs = block[:2]
        keys, held = tile_rows(t, count), slice(0, count * TILE)
        dv[keys] += dot(p_s[held], gs[...], NN)
        dk[keys] += dot(l_s[held], qs[...], NN)
        dq_t[...] += dot(k_t[:, keys], l_s[held], NN)

    def leaving(i):
        part = (slice(i * TILE, (i + 1) * TILE), slice(0, QW))
        return pltpu.make_async_copy(back_ref.at[part], back_out.at[part], block_sems.at[i])

    def finish(i):
        here = slice(i * TILE, (i + 1) * TILE)
        for j in range(GROUP):
            back_ref[here, j * HEAD_DIM : (j + 1) * HEAD_DIM] = (
                (dq_t[:, lanes(j)] * SCALE).T.astype(BF16)
            )
        leaving(i).start()

    def scores(t, count):
        for j in range(GROUP):
            score_head(t, count, j, sets[0])

    load_block(0, sets[0])
    sweep(scores, prompt_tiles)
    for j in range(GROUP):
        score_head(prompt_tiles, 1, j, sets[0], diagonal=True)
    normalise(0, sets[0])

    blocks = slots // TILE
    live = lax.div(length + TILE - 1, TILE)
    for i in range(blocks):
        now, later = sets[i % 2], sets[(i + 1) % 2]
        tiles = prompt_tiles + i + 1
        dq_t[...] = jnp.zeros_like(dq_t)

        def grads(t, count):
            for j in range(GROUP):
                grad_head(t, count, j, now)
            grad_sums(t, count, now)

        def both(t, count):
            for j in range(GROUP):
                grad_head(t, count, j, now)
                score_head(t, count, j, later)
            grad_sums(t, count, now)

        if i + 1 < blocks:

            @pl.when(live > i + 1)
            def _():
                load_block(i + 1, later)
                sweep(both, tiles)
                finish(i)
                for j in range(GROUP):
                    score_head(tiles, 1, j, later, diagonal=True)
                normalise(i + 1, later)

        @pl.when(live == i + 1)
        def _():
            sweep(grads, tiles)
            finish(i)

        @pl.when(live <= i)
        def _():
            leaving(i).start()

    pg_ref[:, 0:HEAD_DIM] = (dk[0:prompt] * SCALE).astype(BF16)
    pg_ref[:, HEAD_DIM:] = dv[0:prompt].astype(BF16)
    back_ref[:, QW : QW + HEAD_DIM] = (dk[prompt:] * SCALE).astype(BF16)
    back_ref[:, QW + HEAD_DIM :] = dv[prompt:].astype(BF16)
    core = me_prefix & 1
    copies = [
        (pg_ref.at[pl.ds(times(2 * f + (core ^ bit), share), share)], out.at[f])
        for bit, out in ((0, pg_keep), (1, pg_give))
        for f in range(half)
    ]
    copies.append((back_ref.at[:, QW:], back_out.at[:, QW:]))
    copies = start_all(copies, sems)
    for i in range(blocks):
        leaving(i).wait()
    for copy in copies:
        copy.wait()


def attend(place, x, pkv):
    slots = KV_HEADS * (x.shape[1] - DELTA_ROWS) // COLUMNS
    half, share, prompt_width = pkv[0].shape
    responses = 2 * half
    prompt = responses * share
    keys = slots + prompt
    wide = GROUP * TILE
    outs = [((slots, BACK_W), BF16)] + [((half, share, prompt_width), BF16)] * 2
    stats = pltpu.VMEM((keys // TILE * STATS, wide), F32)
    one_set = [
        pltpu.VMEM((wide, HEAD_DIM), BF16),
        pltpu.VMEM((wide, HEAD_DIM), BF16),
        pltpu.VMEM((HEAD_DIM, wide), BF16),
        pltpu.VMEM((2 * HEAD_DIM, wide), BF16),
        pltpu.VMEM((keys, wide), F32),
        stats,
        stats,
    ]
    return pl.pallas_call(
        attend_kernel,
        in_specs=[SMEM, VMEM, ANY, ANY],
        out_specs=[HBM] * len(outs),
        out_shape=[pltpu.HBM(shape, dtype) for shape, dtype in outs],
        scratch_shapes=[
            pltpu.VMEM((prompt, prompt_width), BF16),
            pltpu.VMEM((slots, BACK_W), BF16),
            pltpu.VMEM((prompt, prompt_width), BF16),
            pltpu.SemaphoreType.DMA((1 + responses,)),
            pltpu.SemaphoreType.DMA((slots // TILE,)),
            pltpu.VMEM((keys, HEAD_DIM), BF16),
            pltpu.VMEM((keys, 2 * HEAD_DIM), BF16),
            pltpu.VMEM((HEAD_DIM, keys), BF16),
            pltpu.VMEM((2 * TILE, wide), BF16),
            pltpu.VMEM((2 * TILE, wide), BF16),
            pltpu.VMEM((HEAD_DIM, wide), F32),
            pltpu.VMEM((keys, HEAD_DIM), F32),
            pltpu.VMEM((keys, HEAD_DIM), F32),
        ]
        + one_set * 2,
        compiler_params=params(50),
        cost_estimate=pl.CostEstimate(
            flops=10 * slots * keys * QW, transcendentals=0, bytes_accessed=8 * slots * QW
        ),
        name="attend",
    )(place, pltpu.with_memory_space_constraint(x, pltpu.VMEM), *pkv)


def core_kernel(place_ref, mine_ref, got_ref, *refs):
    outs, total = refs[:-1], refs[-1]
    total[...] = mine_ref[...].astype(F32) + got_ref[...].astype(F32)
    z, per = place_ref[1] // (total.shape[0] * 2 // len(outs)), total.shape[0] // len(outs)
    for d, out in enumerate(outs):
        out[...] = total[pl.ds((z ^ d) * per, per)]


def sum_over_cores(place, mine, got):
    count, share, width = mine.shape
    zs = lax.axis_size("z")
    return pl.pallas_call(
        core_kernel,
        in_specs=[SMEM, VMEM, VMEM],
        out_specs=[VMEM] * zs,
        out_shape=[jax.ShapeDtypeStruct((count // zs, share, width), F32)] * zs,
        scratch_shapes=[pltpu.VMEM(mine.shape, F32)],
        compiler_params=params(8),
        cost_estimate=pl.CostEstimate(flops=5 * 10**10, transcendentals=0, bytes_accessed=2**20),
        name="sum_over_cores",
    )(place, mine, got)


def swap(value, axis, d):
    return lax.ppermute(value, axis, [(i, i ^ d) for i in range(lax.axis_size(axis))])


def swap_across(value):
    resps = lax.axis_size("resp")
    pairs = [(x * resps + r, (x ^ 1) * resps + (r ^ 1)) for x in range(lax.axis_size("x")) for r in range(resps)]
    return lax.ppermute(value, ("x", "resp"), pairs)


def local(
    resp_query,
    resp_keys,
    resp_values,
    resp_out,
    resp_grad,
    prompt_keys,
    prompt_values,
    resp_lengths,
):
    head = lax.axis_index("resp")
    rows = resp_query.shape[1]
    place = jnp.stack([resp_lengths[0], lax.axis_index(AXES)])
    send = pack(resp_query[0], resp_grad[0], resp_out[0], resp_keys[0], resp_values[0])
    x = lax.all_to_all(send, "resp", 0, 0, tiled=True)
    prompt_keys, prompt_values, _ = lax.optimization_barrier((prompt_keys, prompt_values, send))
    cut = lambda a, h: lax.dynamic_slice_in_dim(a, h * HEAD_DIM, HEAD_DIM, 1)
    both = lambda h: jnp.concatenate([cut(prompt_keys, h), cut(prompt_values, h)], axis=1)[None]
    pkv, first = both(head), swap_across(both(head ^ 1))
    pkv = jnp.concatenate([pkv, first])
    for axis, d in GATHER_STEPS[:-1]:
        pkv = jnp.concatenate([pkv, swap(pkv, axis, d)])
    pkv = [pkv, swap(pkv, *GATHER_STEPS[-1])]
    back, keep, give = attend(place, x, pkv)
    back = lax.all_to_all(back.reshape(KV_HEADS, rows, BACK_W), "resp", 0, 0, tiled=True)
    parts = sum_over_cores(place, keep, swap(give, "core", 1))
    total = parts[0]
    for d in range(1, len(parts)):
        total = total + swap(parts[d], "z", d)
    xs, share, width = total.shape
    own = share // KV_HEADS
    back, total = lax.optimization_barrier((back, total.reshape(xs * KV_HEADS, own, width)))
    total = lax.all_to_all(total, ("x", "resp"), 0, 0, tiled=True)
    total = total.reshape(xs, KV_HEADS, own, 2, HEAD_DIM).sum(axis=0).astype(BF16)
    total = total.transpose(2, 1, 0, 3).reshape(2, own, KV_HEADS * HEAD_DIM)
    grad_query, grad_keys, grad_values = unpack(back)
    return (grad_query[None], grad_keys[None], grad_values[None], total[0], total[1])


def solution(mesh):
    parts = Mesh(mesh.devices.reshape([size for name, size in PREFIX] + [KV_HEADS]), AXES + ("resp",))
    slots = P(AXES, "resp", None)
    prompt = P(AXES, None)
    owned = P(AXES + ("resp",), None)
    return jax.shard_map(
        local,
        mesh=parts,
        in_specs=(slots, slots, slots, slots, slots, prompt, prompt, P(AXES)),
        out_specs=(slots, slots, slots, owned, owned),
        check_vma=False,
    )
```

```python
import jax
import jax.numpy as jnp
from jax import lax
from jax.experimental import pallas as pl
from jax.experimental.pallas import tpu as pltpu
from jax.sharding import PartitionSpec as P

HEADS = 40
KV_HEADS = 8
GROUP = HEADS // KV_HEADS
HEAD_DIM = 128
SCALE = HEAD_DIM ** (-0.5)
EXP2_SCALE = SCALE * 1.4426950408889634
QW = GROUP * HEAD_DIM
TILE = 256
STATS = 16
UNSEEN = -1e30
PACK_ROWS = 32
GATHER_BITS = (1, 0, 2, 3)
COLUMNS = 2 + 2 * GROUP
DELTA_ROWS = 16
BACK_W = QW + 2 * HEAD_DIM
X_BIT, CORE_BIT = 2, 1

NN = (((1,), (0,)), ((), ()))
BF16 = jnp.bfloat16
F32 = jnp.float32
ANY = pl.BlockSpec(memory_space=pl.ANY)
HBM = pl.BlockSpec(memory_space=pltpu.HBM)
VMEM = pl.BlockSpec(memory_space=pltpu.VMEM)
SMEM = pl.BlockSpec(memory_space=pltpu.SMEM)


def dot(a, b, dims):
    return lax.dot_general(a, b, dims, preferred_element_type=F32)


def params(mib):
    return pltpu.CompilerParams(vmem_limit_bytes=mib * 1024 * 1024)


def times(index, size):
    return pl.multiple_of(index * size, size)


def send_rows(c, n):
    first = (c * COLUMNS + n) * PACK_ROWS
    return slice(first, first + PACK_ROWS)


def gather_mask(index):
    return sum(((index >> step) & 1) << bit for step, bit in enumerate(GATHER_BITS))


def start_all(copies, sems):
    started = [pltpu.make_async_copy(src, dst, sems.at[n]) for n, (src, dst) in enumerate(copies)]
    for copy in started:
        copy.start()
    return started


def pack_kernel(q_in, g_in, o_in, k_in, v_in, send_out, q_ref, g_ref, o_ref, k_ref, v_ref, send_ref, left_ref, sems, out_sems):
    ins = ((q_in, q_ref), (g_in, g_ref), (o_in, o_ref), (k_in, k_ref), (v_in, v_ref))
    steps = q_ref.shape[0] // PACK_ROWS
    arriving = []
    for c in range(steps):
        rows = slice(c * PACK_ROWS, (c + 1) * PACK_ROWS)
        arriving.append(start_all([(src.at[rows], dst.at[rows]) for src, dst in ins], sems.at[c]))
    row = lax.broadcasted_iota(jnp.int32, (QW, HEAD_DIM), 0) // HEAD_DIM
    lane = lax.broadcasted_iota(jnp.int32, (QW, HEAD_DIM), 1)
    ones = jnp.where((lane >= 3 * row) & (lane < 3 * row + 3), 1.0, 0.0).astype(BF16)
    leaving = []
    for c in range(steps):
        rows = slice(c * PACK_ROWS, (c + 1) * PACK_ROWS)
        for copy in arriving[c]:
            copy.wait()
        highs, lows = [], []
        for h in range(KV_HEADS):
            columns = [(k_ref, h), (v_ref, h)]
            columns += [(q_ref, h * GROUP + j) for j in range(GROUP)]
            columns += [(g_ref, h * GROUP + j) for j in range(GROUP)]
            for n, (ref, col) in enumerate(columns):
                send_ref[h, send_rows(c, n)] = ref[rows, col * HEAD_DIM : (col + 1) * HEAD_DIM]
            wide = slice(h * QW, (h + 1) * QW)
            product = g_ref[rows, wide].astype(F32) * o_ref[rows, wide].astype(F32)
            high = product.astype(BF16)
            highs.append(high)
            lows.append((product - high.astype(F32)).astype(BF16))
        part = slice(c * COLUMNS * PACK_ROWS, (c + 1) * COLUMNS * PACK_ROWS)
        leaving += start_all([(send_ref.at[:, part], send_out.at[:, part])], out_sems.at[pl.ds(c, 1)])
        left = dot(jnp.concatenate(highs), ones, NN) + dot(jnp.concatenate(lows), ones, NN)
        for h in range(KV_HEADS):
            left_ref[h, rows] = left[h * PACK_ROWS : (h + 1) * PACK_ROWS]
    part = lax.broadcasted_iota(jnp.int32, (DELTA_ROWS, q_ref.shape[0]), 0) % 3
    last = slice(steps * COLUMNS * PACK_ROWS, steps * COLUMNS * PACK_ROWS + DELTA_ROWS)
    for h in range(KV_HEADS):
        left = left_ref[h].T[0:DELTA_ROWS]
        first = left.astype(BF16).astype(F32)
        second = (left - first).astype(BF16).astype(F32)
        third = left - first - second
        send_ref[h, last] = jnp.where(part == 0, first, jnp.where(part == 1, second, third)).astype(BF16)
    leaving += start_all([(send_ref.at[:, last], send_out.at[:, last])], out_sems.at[pl.ds(steps, 1)])
    for copy in leaving:
        copy.wait()


def pack(q, g, o, k, v):
    rows = q.shape[0]
    steps = rows // PACK_ROWS
    send = (KV_HEADS, rows * COLUMNS + DELTA_ROWS, HEAD_DIM)
    return pl.pallas_call(
        pack_kernel,
        in_specs=[HBM] * 5,
        out_specs=HBM,
        out_shape=pltpu.HBM(send, BF16),
        scratch_shapes=[pltpu.VMEM(a.shape, BF16) for a in (q, g, o, k, v)]
        + [
            pltpu.VMEM(send, BF16),
            pltpu.VMEM((KV_HEADS, rows, HEAD_DIM), F32),
            pltpu.SemaphoreType.DMA((steps, 5)),
            pltpu.SemaphoreType.DMA((steps + 1,)),
        ],
        compiler_params=params(60),
        name="pack",
    )(q, g, o, k, v)


def unpack_kernel(back_ref, q_ref, k_ref, v_ref, sems):
    copies = []
    for h in range(KV_HEADS):
        thin = slice(h * HEAD_DIM, (h + 1) * HEAD_DIM)
        wide = slice(h * QW, (h + 1) * QW)
        copies.append((back_ref.at[h, :, 0:QW], q_ref.at[:, wide]))
        copies.append((back_ref.at[h, :, QW : QW + HEAD_DIM], k_ref.at[:, thin]))
        copies.append((back_ref.at[h, :, QW + HEAD_DIM :], v_ref.at[:, thin]))
    for copy in start_all(copies, sems):
        copy.wait()


def unpack(back):
    rows = back.shape[1]
    return pl.pallas_call(
        unpack_kernel,
        in_specs=[ANY],
        out_specs=[ANY] * 3,
        out_shape=[
            jax.ShapeDtypeStruct((rows, KV_HEADS * QW), BF16),
            jax.ShapeDtypeStruct((rows, KV_HEADS * HEAD_DIM), BF16),
            jax.ShapeDtypeStruct((rows, KV_HEADS * HEAD_DIM), BF16),
        ],
        scratch_shapes=[pltpu.SemaphoreType.DMA((3 * KV_HEADS,))],
        compiler_params=params(4),
        name="unpack",
    )(back)


def attend_kernel(place_ref, x_ref, pkv_low, pkv_high, back_out, pg_keep, pg_give, *refs):
    pkv_ref, back_ref, pg_ref, sems, block_sems, k_all, v_all, k_t = refs[:8]
    p_s, l_s, dq_t, dk, dv = refs[8:13]
    sets = [refs[13:20], refs[20:27]]
    prompt = pkv_ref.shape[0]
    run = (x_ref.shape[1] - DELTA_ROWS) // COLUMNS
    slots = KV_HEADS * run
    wide = GROUP * TILE
    prompt_tiles = prompt // TILE
    length, me_prefix = place_ref[0], place_ref[1]
    half = pkv_low.shape[0]
    sources = 2 * half
    share = prompt // sources
    copies = [
        ((pkv_low, pkv_high)[f // half].at[f % half], pkv_ref.at[pl.ds(times(me_prefix ^ gather_mask(f), share), share)])
        for f in range(sources)
    ]
    copies = start_all(copies, sems)
    back_ref[...] = jnp.zeros_like(back_ref)
    dk[...] = jnp.zeros_like(dk)
    dv[...] = jnp.zeros_like(dv)
    for block in sets:
        block[3][HEAD_DIM + DELTA_ROWS :] = jnp.zeros((HEAD_DIM - DELTA_ROWS, wide), BF16)
    for copy in copies:
        copy.wait()

    def flip(a):
        return a.astype(F32).T.astype(BF16)

    def slots_of(b, n):
        return jnp.concatenate([x_ref[b, send_rows(c, n)] for c in range(run // PACK_ROWS)])

    k_all[0:prompt] = pkv_ref[:, 0:HEAD_DIM]
    v_all[0:prompt, 0:HEAD_DIM] = pkv_ref[:, HEAD_DIM:]
    for b in range(KV_HEADS):
        own = slice(prompt + b * run, prompt + (b + 1) * run)
        k_all[own] = slots_of(b, 0)
        v_all[own, 0:HEAD_DIM] = slots_of(b, 1)
    v_all[:, HEAD_DIM:] = jnp.full((prompt + slots, HEAD_DIM), -1.0, BF16)
    for t in range((prompt + slots) // TILE):
        block = slice(t * TILE, (t + 1) * TILE)
        k_t[:, block] = flip(k_all[block])

    def lanes(j):
        return slice(j * TILE, (j + 1) * TILE)

    def tile_rows(t, count):
        return pl.ds(times(t, TILE), count * TILE)

    def stat_rows(t, count):
        return pl.ds(times(t, STATS), count * STATS)

    def sweep(body, tiles):
        def pair(n, carry):
            body(2 * n, 2)
            return carry

        last = 2 - tiles % 2
        lax.fori_loop(0, (tiles - last) // 2, pair, 0)
        body(tiles - last, last)

    def load_block(i, block):
        qs, gs, qs_t, gs_t = block[:4]
        sources = range(i * TILE // run, (i + 1) * TILE // run)
        delta_t = jnp.concatenate([x_ref[b, run * COLUMNS :] for b in sources], axis=1).astype(F32)
        part = lax.broadcasted_iota(jnp.int32, delta_t.shape, 0)
        for j in range(GROUP):
            q = jnp.concatenate([slots_of(b, 2 + j) for b in sources])
            g = jnp.concatenate([slots_of(b, 2 + GROUP + j) for b in sources])
            qs[lanes(j)] = q
            gs[lanes(j)] = g
            qs_t[:, lanes(j)] = flip(q)
            gs_t[0:HEAD_DIM, lanes(j)] = flip(g)
            mine = (part >= 3 * j) & (part < 3 * j + 3)
            gs_t[HEAD_DIM : HEAD_DIM + DELTA_ROWS, lanes(j)] = jnp.where(mine, delta_t, 0.0).astype(BF16)

    def score_head(t, count, j, block, diagonal=False):
        qs_t, _, e_all, tops, sums = block[2:]
        s = dot(k_all[tile_rows(t, count)], qs_t[:, lanes(j)], NN)
        if diagonal:
            seen = lax.broadcasted_iota(jnp.int32, s.shape, 0) <= lax.broadcasted_iota(
                jnp.int32, s.shape, 1
            )
            s = jnp.where(seen, s, UNSEEN)
        groups = count * STATS // 8
        s = s.reshape(groups, -1, 8, TILE)
        top = jnp.max(s, axis=1, keepdims=True)
        e = jnp.exp2((s - top) * EXP2_SCALE)
        tops[stat_rows(t, count), lanes(j)] = top.reshape(groups * 8, TILE)
        sums[stat_rows(t, count), lanes(j)] = jnp.sum(e, axis=1).reshape(groups * 8, TILE)
        e_all[tile_rows(t, count), lanes(j)] = e.reshape(count * TILE, TILE)

    def normalise(i, block):
        tops, sums = block[5:]
        rows = STATS * (prompt_tiles + i + 1)
        top = tops[0:rows]
        weight = jnp.exp2((top - jnp.max(top, axis=0, keepdims=True)) * EXP2_SCALE)
        total = jnp.sum(weight * sums[0:rows], axis=0, keepdims=True)
        slot = lax.broadcasted_iota(jnp.int32, (1, wide), 1) % TILE + i * TILE
        tops[0:rows] = weight * (jnp.where(slot < length, 1.0, 0.0) / total)

    def grad_head(t, count, j, block):
        gs_t, e_all, factors = block[3:6]
        shifted = dot(v_all[tile_rows(t, count)], gs_t[:, lanes(j)], NN)
        groups = count * STATS // 8
        e = e_all[tile_rows(t, count), lanes(j)].reshape(groups, -1, 8, TILE)
        factor = factors[stat_rows(t, count), lanes(j)].reshape(groups, 1, 8, TILE)
        p = (e * factor).reshape(count * TILE, TILE)
        p_s[0 : count * TILE, lanes(j)] = p.astype(BF16)
        l_s[0 : count * TILE, lanes(j)] = (p * shifted).astype(BF16)

    def grad_sums(t, count, block):
        qs, gs = block[:2]
        keys, held = tile_rows(t, count), slice(0, count * TILE)
        dv[keys] += dot(p_s[held], gs[...], NN)
        dk[keys] += dot(l_s[held], qs[...], NN)
        dq_t[...] += dot(k_t[:, keys], l_s[held], NN)

    def leaving(i):
        part = (slice(i * TILE, (i + 1) * TILE), slice(0, QW))
        return pltpu.make_async_copy(back_ref.at[part], back_out.at[part], block_sems.at[i])

    def finish(i):
        here = slice(i * TILE, (i + 1) * TILE)
        for j in range(GROUP):
            back_ref[here, j * HEAD_DIM : (j + 1) * HEAD_DIM] = (
                (dq_t[:, lanes(j)] * SCALE).T.astype(BF16)
            )
        leaving(i).start()

    def scores(t, count):
        for j in range(GROUP):
            score_head(t, count, j, sets[0])

    load_block(0, sets[0])
    sweep(scores, prompt_tiles)
    for j in range(GROUP):
        score_head(prompt_tiles, 1, j, sets[0], diagonal=True)
    normalise(0, sets[0])
    load_block(1, sets[1])

    blocks = slots // TILE
    live = lax.div(length + TILE - 1, TILE)
    for i in range(blocks):
        now, later = sets[i % 2], sets[(i + 1) % 2]
        tiles = prompt_tiles + i + 1
        dq_t[...] = jnp.zeros_like(dq_t)

        def grads(t, count):
            for j in range(GROUP):
                grad_head(t, count, j, now)
            grad_sums(t, count, now)

        def both(t, count):
            for j in range(GROUP):
                grad_head(t, count, j, now)
                score_head(t, count, j, later)
            grad_sums(t, count, now)

        if i + 1 < blocks:

            @pl.when(live > i + 1)
            def _():
                sweep(both, tiles)
                for j in range(GROUP):
                    score_head(tiles, 1, j, later, diagonal=True)
                finish(i)
                normalise(i + 1, later)
                if i + 2 < blocks:
                    load_block(i + 2, now)

        @pl.when(live == i + 1)
        def _():
            sweep(grads, tiles)
            finish(i)

        @pl.when(live <= i)
        def _():
            leaving(i).start()

    pg_ref[:, 0:HEAD_DIM] = (dk[0:prompt] * SCALE).astype(BF16)
    pg_ref[:, HEAD_DIM:] = dv[0:prompt].astype(BF16)
    back_ref[:, QW : QW + HEAD_DIM] = (dk[prompt:] * SCALE).astype(BF16)
    back_ref[:, QW + HEAD_DIM :] = dv[prompt:].astype(BF16)
    mine = me_prefix & X_BIT
    copies = [
        (pg_ref.at[pl.ds(times(f + (f & -X_BIT) + (mine ^ bit), share), share)], out.at[f])
        for bit, out in ((0, pg_keep), (X_BIT, pg_give))
        for f in range(half)
    ]
    copies = start_all([(back_ref.at[:, QW:], back_out.at[:, QW:])] + copies, sems)
    for i in range(blocks):
        leaving(i).wait()
    for copy in copies:
        copy.wait()


def attend(place, x, pkv):
    slots = KV_HEADS * (x.shape[1] - DELTA_ROWS) // COLUMNS
    half, share, prompt_width = pkv[0].shape
    responses = 2 * half
    prompt = responses * share
    keys = slots + prompt
    wide = GROUP * TILE
    outs = [((slots, BACK_W), BF16)] + [((half, share, prompt_width), BF16)] * 2
    stats = pltpu.VMEM((keys // TILE * STATS, wide), F32)
    one_set = [
        pltpu.VMEM((wide, HEAD_DIM), BF16),
        pltpu.VMEM((wide, HEAD_DIM), BF16),
        pltpu.VMEM((HEAD_DIM, wide), BF16),
        pltpu.VMEM((2 * HEAD_DIM, wide), BF16),
        pltpu.VMEM((keys, wide), F32),
        stats,
        stats,
    ]
    return pl.pallas_call(
        attend_kernel,
        in_specs=[SMEM, VMEM, ANY, ANY],
        out_specs=[HBM] * len(outs),
        out_shape=[pltpu.HBM(shape, dtype) for shape, dtype in outs],
        scratch_shapes=[
            pltpu.VMEM((prompt, prompt_width), BF16),
            pltpu.VMEM((slots, BACK_W), BF16),
            pltpu.VMEM((prompt, prompt_width), BF16),
            pltpu.SemaphoreType.DMA((1 + responses,)),
            pltpu.SemaphoreType.DMA((slots // TILE,)),
            pltpu.VMEM((keys, HEAD_DIM), BF16),
            pltpu.VMEM((keys, 2 * HEAD_DIM), BF16),
            pltpu.VMEM((HEAD_DIM, keys), BF16),
            pltpu.VMEM((2 * TILE, wide), BF16),
            pltpu.VMEM((2 * TILE, wide), BF16),
            pltpu.VMEM((HEAD_DIM, wide), F32),
            pltpu.VMEM((keys, HEAD_DIM), F32),
            pltpu.VMEM((keys, HEAD_DIM), F32),
        ]
        + one_set * 2,
        compiler_params=params(50),
        cost_estimate=pl.CostEstimate(
            flops=10 * slots * keys * QW, transcendentals=0, bytes_accessed=8 * slots * QW
        ),
        name="attend",
    )(place, pltpu.with_memory_space_constraint(x, pltpu.VMEM), *pkv)


def core_kernel(place_ref, mine_ref, got_ref, keep_ref, give_ref, total):
    total[...] = mine_ref[...].astype(F32) + got_ref[...].astype(F32)
    core = place_ref[1] & CORE_BIT
    for f in range(keep_ref.shape[0]):
        keep_ref[f] = total[2 * f + core]
        give_ref[f] = total[2 * f + 1 - core]


def sum_over_x(place, mine, got):
    count, share, width = mine.shape
    part = jax.ShapeDtypeStruct((count // 2, share, width), F32)
    return pl.pallas_call(
        core_kernel,
        in_specs=[SMEM, VMEM, VMEM],
        out_specs=[VMEM] * 2,
        out_shape=[part] * 2,
        scratch_shapes=[pltpu.VMEM(mine.shape, F32)],
        compiler_params=params(8),
        cost_estimate=pl.CostEstimate(flops=5 * 10**10, transcendentals=0, bytes_accessed=2**20),
        name="sum_over_x",
    )(place, mine, got)


def z_kernel(place_ref, mine_ref, got_ref, *refs):
    outs, total = refs[:-1], refs[-1]
    total[...] = mine_ref[...] + got_ref[...]
    z = place_ref[1] // (2 * X_BIT)
    for d, out in enumerate(outs):
        out[...] = total[z ^ d]


def sum_over_cores(place, mine, got):
    count, share, width = mine.shape
    return pl.pallas_call(
        z_kernel,
        in_specs=[SMEM, VMEM, VMEM],
        out_specs=[VMEM] * count,
        out_shape=[jax.ShapeDtypeStruct((share, width), F32)] * count,
        scratch_shapes=[pltpu.VMEM(mine.shape, F32)],
        compiler_params=params(8),
        name="sum_over_cores",
    )(place, mine, got)


def sum_kernel(place_ref, *refs):
    parts, outs, total = refs[: -KV_HEADS - 1], refs[-KV_HEADS - 1 : -1], refs[-1]
    value = parts[0][...]
    for part in parts[1:]:
        value = value + part[...]
    total[...] = value
    own = outs[0].shape[0]
    for d, out in enumerate(outs):
        out[...] = total[pl.ds(times(place_ref[2] ^ d, own), own)]


def sum_parts(place, parts):
    rows, width = parts[0].shape
    own = rows // KV_HEADS
    return pl.pallas_call(
        sum_kernel,
        in_specs=[SMEM] + [VMEM] * len(parts),
        out_specs=[VMEM] * KV_HEADS,
        out_shape=[jax.ShapeDtypeStruct((own, width), F32)] * KV_HEADS,
        scratch_shapes=[pltpu.VMEM((rows, width), F32)],
        compiler_params=params(4),
        name="sum_parts",
    )(place, *parts)


def spread_kernel(place_ref, *refs):
    parts, (k_ref, v_ref) = refs[:KV_HEADS], refs[KV_HEADS:]
    for d, part in enumerate(parts):
        cols = pl.ds(times(place_ref[2] ^ d, HEAD_DIM), HEAD_DIM)
        k_ref[:, cols] = part[:, 0:HEAD_DIM].astype(BF16)
        v_ref[:, cols] = part[:, HEAD_DIM:].astype(BF16)


def spread_heads(place, parts):
    shape = jax.ShapeDtypeStruct((parts[0].shape[0], KV_HEADS * HEAD_DIM), BF16)
    return pl.pallas_call(
        spread_kernel,
        in_specs=[SMEM] + [VMEM] * KV_HEADS,
        out_specs=[VMEM] * 2,
        out_shape=[shape] * 2,
        compiler_params=params(4),
        name="spread_heads",
    )(place, *parts)


def swap(value, axis, d):
    return lax.ppermute(value, axis, [(i, i ^ d) for i in range(lax.axis_size(axis))])


def swap_all(values, axis, step=1):
    return [values[0]] + [swap(values[d], axis, step * d) for d in range(1, len(values))]


def swap_across(value):
    sizes = lax.axis_size("prefix"), lax.axis_size("resp")
    pairs = [(p * sizes[1] + r, (p ^ X_BIT) * sizes[1] + (r ^ 1)) for p in range(sizes[0]) for r in range(sizes[1])]
    return lax.ppermute(value, ("prefix", "resp"), pairs)


def local(
    resp_query,
    resp_keys,
    resp_values,
    resp_out,
    resp_grad,
    prompt_keys,
    prompt_values,
    resp_lengths,
):
    head = lax.axis_index("resp")
    rows = resp_query.shape[1]
    place = jnp.stack([resp_lengths[0], lax.axis_index("prefix"), head])
    send = pack(resp_query[0], resp_grad[0], resp_out[0], resp_keys[0], resp_values[0])
    x = lax.all_to_all(send, "resp", 0, 0, tiled=True)
    prompt_keys, prompt_values, _ = lax.optimization_barrier((prompt_keys, prompt_values, send))
    cut = lambda a, h: lax.dynamic_slice_in_dim(a, h * HEAD_DIM, HEAD_DIM, 1)
    both = lambda h: jnp.concatenate([cut(prompt_keys, h), cut(prompt_values, h)], axis=1)[None]
    pkv, first = both(head), swap_across(both(head ^ 1))
    pkv = jnp.concatenate([pkv, first])
    for bit in GATHER_BITS[1:-1]:
        pkv = jnp.concatenate([pkv, swap(pkv, "prefix", 1 << bit)])
    pkv = [pkv, swap(pkv, "prefix", 1 << GATHER_BITS[-1])]
    back, keep, give = attend(place, x, pkv)
    back = lax.all_to_all(back.reshape(KV_HEADS, rows, BACK_W), "resp", 0, 0, tiled=True)
    keep, give = sum_over_x(place, keep, swap(give, "prefix", X_BIT))
    parts = sum_over_cores(place, keep, swap(give, "prefix", CORE_BIT))
    parts = swap_all(sum_parts(place, swap_all(parts, "prefix", 2 * X_BIT)), "resp")
    total = spread_heads(place, parts)
    grad_query, grad_keys, grad_values = unpack(back)
    return (grad_query[None], grad_keys[None], grad_values[None], total[0], total[1])


def solution(mesh):
    return jax.shard_map(
        local,
        mesh=mesh,
        in_specs=(
            P("prefix", "resp", None),
            P("prefix", "resp", None),
            P("prefix", "resp", None),
            P("prefix", "resp", None),
            P("prefix", "resp", None),
            P("prefix", None),
            P("prefix", None),
            P("prefix"),
        ),
        out_specs=(
            P("prefix", "resp", None),
            P("prefix", "resp", None),
            P("prefix", "resp", None),
            P(("prefix", "resp"), None),
            P(("prefix", "resp"), None),
        ),
        check_vma=False,
    )
```

```python
import jax
import jax.numpy as jnp
from jax import lax
from jax.experimental import pallas as pl
from jax.experimental.pallas import tpu as pltpu
from jax.sharding import PartitionSpec as P

HEADS = 40
KV_HEADS = 8
GROUP = HEADS // KV_HEADS
HEAD_DIM = 128
SCALE = HEAD_DIM ** (-0.5)
EXP2_SCALE = SCALE * 1.4426950408889634
QW = GROUP * HEAD_DIM
TILE = 256
STATS = 16
UNSEEN = -1e30
PACK_ROWS = 32
GATHER_BITS = (1, 0, 2, 3)
COLUMNS = 2 + 2 * GROUP
DELTA_ROWS = 16
BACK_W = QW + 2 * HEAD_DIM
X_BIT, CORE_BIT = 2, 1

NN = (((1,), (0,)), ((), ()))
BF16 = jnp.bfloat16
F32 = jnp.float32
ANY = pl.BlockSpec(memory_space=pl.ANY)
HBM = pl.BlockSpec(memory_space=pltpu.HBM)
VMEM = pl.BlockSpec(memory_space=pltpu.VMEM)
SMEM = pl.BlockSpec(memory_space=pltpu.SMEM)


def dot(a, b, dims):
    return lax.dot_general(a, b, dims, preferred_element_type=F32)


def params(mib):
    return pltpu.CompilerParams(vmem_limit_bytes=mib * 1024 * 1024)


def times(index, size):
    return pl.multiple_of(index * size, size)


def send_rows(c, n):
    first = (c * COLUMNS + n) * PACK_ROWS
    return slice(first, first + PACK_ROWS)


def gather_mask(index):
    return sum(((index >> step) & 1) << bit for step, bit in enumerate(GATHER_BITS))


def start_all(copies, sems):
    started = [pltpu.make_async_copy(src, dst, sems.at[n]) for n, (src, dst) in enumerate(copies)]
    for copy in started:
        copy.start()
    return started


def pack_kernel(q_in, g_in, o_in, k_in, v_in, send_out, q_ref, g_ref, o_ref, k_ref, v_ref, send_ref, left_ref, sems, out_sems):
    ins = ((q_in, q_ref), (g_in, g_ref), (o_in, o_ref), (k_in, k_ref), (v_in, v_ref))
    steps = q_ref.shape[0] // PACK_ROWS
    arriving = []
    for c in range(steps):
        rows = slice(c * PACK_ROWS, (c + 1) * PACK_ROWS)
        arriving.append(start_all([(src.at[rows], dst.at[rows]) for src, dst in ins], sems.at[c]))
    row = lax.broadcasted_iota(jnp.int32, (QW, HEAD_DIM), 0) // HEAD_DIM
    lane = lax.broadcasted_iota(jnp.int32, (QW, HEAD_DIM), 1)
    ones = jnp.where((lane >= 3 * row) & (lane < 3 * row + 3), 1.0, 0.0).astype(BF16)
    leaving = []
    for c in range(steps):
        rows = slice(c * PACK_ROWS, (c + 1) * PACK_ROWS)
        for copy in arriving[c]:
            copy.wait()
        highs, lows = [], []
        for h in range(KV_HEADS):
            columns = [(k_ref, h), (v_ref, h)]
            columns += [(q_ref, h * GROUP + j) for j in range(GROUP)]
            columns += [(g_ref, h * GROUP + j) for j in range(GROUP)]
            for n, (ref, col) in enumerate(columns):
                send_ref[h, send_rows(c, n)] = ref[rows, col * HEAD_DIM : (col + 1) * HEAD_DIM]
            wide = slice(h * QW, (h + 1) * QW)
            product = g_ref[rows, wide].astype(F32) * o_ref[rows, wide].astype(F32)
            high = product.astype(BF16)
            highs.append(high)
            lows.append((product - high.astype(F32)).astype(BF16))
        part = slice(c * COLUMNS * PACK_ROWS, (c + 1) * COLUMNS * PACK_ROWS)
        leaving += start_all([(send_ref.at[:, part], send_out.at[:, part])], out_sems.at[pl.ds(c, 1)])
        left = dot(jnp.concatenate(highs), ones, NN) + dot(jnp.concatenate(lows), ones, NN)
        for h in range(KV_HEADS):
            left_ref[h, rows] = left[h * PACK_ROWS : (h + 1) * PACK_ROWS]
    part = lax.broadcasted_iota(jnp.int32, (DELTA_ROWS, q_ref.shape[0]), 0) % 3
    last = slice(steps * COLUMNS * PACK_ROWS, steps * COLUMNS * PACK_ROWS + DELTA_ROWS)
    for h in range(KV_HEADS):
        left = left_ref[h].T[0:DELTA_ROWS]
        first = left.astype(BF16).astype(F32)
        second = (left - first).astype(BF16).astype(F32)
        third = left - first - second
        send_ref[h, last] = jnp.where(part == 0, first, jnp.where(part == 1, second, third)).astype(BF16)
    leaving += start_all([(send_ref.at[:, last], send_out.at[:, last])], out_sems.at[pl.ds(steps, 1)])
    for copy in leaving:
        copy.wait()


def pack(q, g, o, k, v):
    rows = q.shape[0]
    steps = rows // PACK_ROWS
    send = (KV_HEADS, rows * COLUMNS + DELTA_ROWS, HEAD_DIM)
    return pl.pallas_call(
        pack_kernel,
        in_specs=[HBM] * 5,
        out_specs=HBM,
        out_shape=pltpu.HBM(send, BF16),
        scratch_shapes=[pltpu.VMEM(a.shape, BF16) for a in (q, g, o, k, v)]
        + [
            pltpu.VMEM(send, BF16),
            pltpu.VMEM((KV_HEADS, rows, HEAD_DIM), F32),
            pltpu.SemaphoreType.DMA((steps, 5)),
            pltpu.SemaphoreType.DMA((steps + 1,)),
        ],
        compiler_params=params(60),
        name="pack",
    )(q, g, o, k, v)


def unpack_kernel(back_ref, q_ref, k_ref, v_ref, sems):
    copies = []
    for h in range(KV_HEADS):
        thin = slice(h * HEAD_DIM, (h + 1) * HEAD_DIM)
        wide = slice(h * QW, (h + 1) * QW)
        copies.append((back_ref.at[h, :, 0:QW], q_ref.at[:, wide]))
        copies.append((back_ref.at[h, :, QW : QW + HEAD_DIM], k_ref.at[:, thin]))
        copies.append((back_ref.at[h, :, QW + HEAD_DIM :], v_ref.at[:, thin]))
    for copy in start_all(copies, sems):
        copy.wait()


def unpack(back):
    rows = back.shape[1]
    return pl.pallas_call(
        unpack_kernel,
        in_specs=[ANY],
        out_specs=[ANY] * 3,
        out_shape=[
            jax.ShapeDtypeStruct((rows, KV_HEADS * QW), BF16),
            jax.ShapeDtypeStruct((rows, KV_HEADS * HEAD_DIM), BF16),
            jax.ShapeDtypeStruct((rows, KV_HEADS * HEAD_DIM), BF16),
        ],
        scratch_shapes=[pltpu.SemaphoreType.DMA((3 * KV_HEADS,))],
        compiler_params=params(4),
        name="unpack",
    )(back)


def attend_kernel(place_ref, x_ref, pkv_low, pkv_high, back_out, *refs):
    pg_outs, refs = refs[:4], refs[4:]
    pkv_ref, back_ref, pg_ref, sems, block_sems, k_all, v_all, k_t = refs[:8]
    p_s, l_s, dq_t, dk, dv = refs[8:13]
    sets = [refs[13:20], refs[20:27]]
    prompt = pkv_ref.shape[0]
    run = (x_ref.shape[1] - DELTA_ROWS) // COLUMNS
    slots = KV_HEADS * run
    wide = GROUP * TILE
    prompt_tiles = prompt // TILE
    length, me_prefix = place_ref[0], place_ref[1]
    half = pkv_low.shape[0]
    sources = 2 * half
    share = prompt // sources
    copies = [
        ((pkv_low, pkv_high)[f // half].at[f % half], pkv_ref.at[pl.ds(times(me_prefix ^ gather_mask(f), share), share)])
        for f in range(sources)
    ]
    copies = start_all(copies, sems)
    back_ref[...] = jnp.zeros_like(back_ref)
    dk[...] = jnp.zeros_like(dk)
    dv[...] = jnp.zeros_like(dv)
    for block in sets:
        block[3][HEAD_DIM + DELTA_ROWS :] = jnp.zeros((HEAD_DIM - DELTA_ROWS, wide), BF16)
    for copy in copies:
        copy.wait()

    def flip(a):
        return a.astype(F32).T.astype(BF16)

    def slots_of(b, n):
        return jnp.concatenate([x_ref[b, send_rows(c, n)] for c in range(run // PACK_ROWS)])

    k_all[0:prompt] = pkv_ref[:, 0:HEAD_DIM]
    v_all[0:prompt, 0:HEAD_DIM] = pkv_ref[:, HEAD_DIM:]
    for b in range(KV_HEADS):
        own = slice(prompt + b * run, prompt + (b + 1) * run)
        k_all[own] = slots_of(b, 0)
        v_all[own, 0:HEAD_DIM] = slots_of(b, 1)
    v_all[:, HEAD_DIM:] = jnp.full((prompt + slots, HEAD_DIM), -1.0, BF16)
    for t in range((prompt + slots) // TILE):
        block = slice(t * TILE, (t + 1) * TILE)
        k_t[:, block] = flip(k_all[block])

    def lanes(j):
        return slice(j * TILE, (j + 1) * TILE)

    def tile_rows(t, count):
        return pl.ds(times(t, TILE), count * TILE)

    def stat_rows(t, count):
        return pl.ds(times(t, STATS), count * STATS)

    def sweep(body, tiles):
        def pair(n, carry):
            body(2 * n, 2)
            return carry

        last = 2 - tiles % 2
        lax.fori_loop(0, (tiles - last) // 2, pair, 0)
        body(tiles - last, last)

    def load_block(i, block):
        qs, gs, qs_t, gs_t = block[:4]
        sources = range(i * TILE // run, (i + 1) * TILE // run)
        delta_t = jnp.concatenate([x_ref[b, run * COLUMNS :] for b in sources], axis=1).astype(F32)
        part = lax.broadcasted_iota(jnp.int32, delta_t.shape, 0)
        for j in range(GROUP):
            q = jnp.concatenate([slots_of(b, 2 + j) for b in sources])
            g = jnp.concatenate([slots_of(b, 2 + GROUP + j) for b in sources])
            qs[lanes(j)] = q
            gs[lanes(j)] = g
            qs_t[:, lanes(j)] = flip(q)
            gs_t[0:HEAD_DIM, lanes(j)] = flip(g)
            mine = (part >= 3 * j) & (part < 3 * j + 3)
            gs_t[HEAD_DIM : HEAD_DIM + DELTA_ROWS, lanes(j)] = jnp.where(mine, delta_t, 0.0).astype(BF16)

    def score_head(t, count, j, block, diagonal=False):
        qs_t, _, e_all, tops, sums = block[2:]
        s = dot(k_all[tile_rows(t, count)], qs_t[:, lanes(j)], NN)
        if diagonal:
            seen = lax.broadcasted_iota(jnp.int32, s.shape, 0) <= lax.broadcasted_iota(
                jnp.int32, s.shape, 1
            )
            s = jnp.where(seen, s, UNSEEN)
        groups = count * STATS // 8
        s = s.reshape(groups, -1, 8, TILE)
        top = jnp.max(s, axis=1, keepdims=True)
        e = jnp.exp2((s - top) * EXP2_SCALE)
        tops[stat_rows(t, count), lanes(j)] = top.reshape(groups * 8, TILE)
        sums[stat_rows(t, count), lanes(j)] = jnp.sum(e, axis=1).reshape(groups * 8, TILE)
        e_all[tile_rows(t, count), lanes(j)] = e.reshape(count * TILE, TILE)

    def normalise(i, block):
        tops, sums = block[5:]
        rows = STATS * (prompt_tiles + i + 1)
        top = tops[0:rows]
        weight = jnp.exp2((top - jnp.max(top, axis=0, keepdims=True)) * EXP2_SCALE)
        total = jnp.sum(weight * sums[0:rows], axis=0, keepdims=True)
        slot = lax.broadcasted_iota(jnp.int32, (1, wide), 1) % TILE + i * TILE
        tops[0:rows] = weight * (jnp.where(slot < length, 1.0, 0.0) / total)

    def grad_head(t, count, j, block):
        gs_t, e_all, factors = block[3:6]
        shifted = dot(v_all[tile_rows(t, count)], gs_t[:, lanes(j)], NN)
        groups = count * STATS // 8
        e = e_all[tile_rows(t, count), lanes(j)].reshape(groups, -1, 8, TILE)
        factor = factors[stat_rows(t, count), lanes(j)].reshape(groups, 1, 8, TILE)
        p = (e * factor).reshape(count * TILE, TILE)
        p_s[0 : count * TILE, lanes(j)] = p.astype(BF16)
        l_s[0 : count * TILE, lanes(j)] = (p * shifted).astype(BF16)

    def grad_sums(t, count, block):
        qs, gs = block[:2]
        keys, held = tile_rows(t, count), slice(0, count * TILE)
        dv[keys] += dot(p_s[held], gs[...], NN)
        dk[keys] += dot(l_s[held], qs[...], NN)
        dq_t[...] += dot(k_t[:, keys], l_s[held], NN)

    def leaving(i):
        part = (slice(i * TILE, (i + 1) * TILE), slice(0, QW))
        return pltpu.make_async_copy(back_ref.at[part], back_out.at[part], block_sems.at[i])

    def finish(i):
        here = slice(i * TILE, (i + 1) * TILE)
        for j in range(GROUP):
            back_ref[here, j * HEAD_DIM : (j + 1) * HEAD_DIM] = (
                (dq_t[:, lanes(j)] * SCALE).T.astype(BF16)
            )
        leaving(i).start()

    def scores(t, count):
        for j in range(GROUP):
            score_head(t, count, j, sets[0])

    load_block(0, sets[0])
    sweep(scores, prompt_tiles)
    for j in range(GROUP):
        score_head(prompt_tiles, 1, j, sets[0], diagonal=True)
    normalise(0, sets[0])
    load_block(1, sets[1])

    blocks = slots // TILE
    live = lax.div(length + TILE - 1, TILE)
    for i in range(blocks):
        now, later = sets[i % 2], sets[(i + 1) % 2]
        tiles = prompt_tiles + i + 1
        dq_t[...] = jnp.zeros_like(dq_t)

        def grads(t, count):
            for j in range(GROUP):
                grad_head(t, count, j, now)
            grad_sums(t, count, now)

        def both(t, count):
            for j in range(GROUP):
                grad_head(t, count, j, now)
                score_head(t, count, j, later)
            grad_sums(t, count, now)

        if i + 1 < blocks:

            @pl.when(live > i + 1)
            def _():
                sweep(both, tiles)
                for j in range(GROUP):
                    score_head(tiles, 1, j, later, diagonal=True)
                finish(i)
                normalise(i + 1, later)
                if i + 2 < blocks:
                    load_block(i + 2, now)

        @pl.when(live == i + 1)
        def _():
            sweep(grads, tiles)
            finish(i)

        @pl.when(live <= i)
        def _():
            leaving(i).start()

    for n, (total, scale) in enumerate(((dk, SCALE), (dv, 1.0))):
        runs = (total[0:prompt] * scale).reshape(-1, 2, 8, HEAD_DIM)
        for lo in range(2):
            pg_ref[lo, :, n * HEAD_DIM : (n + 1) * HEAD_DIM] = runs[:, lo].reshape(prompt // 2, HEAD_DIM).astype(BF16)
    back_ref[:, QW : QW + HEAD_DIM] = (dk[prompt:] * SCALE).astype(BF16)
    back_ref[:, QW + HEAD_DIM :] = dv[prompt:].astype(BF16)
    mine, low = me_prefix & X_BIT, place_ref[2] & 1
    kept = share // 2
    copies = [
        (pg_ref.at[low ^ flip_low, pl.ds(times(f + (f & -X_BIT) + (mine ^ bit), kept), kept)], out.at[f])
        for (bit, flip_low), out in zip(((0, 0), (X_BIT, 0), (0, 1), (X_BIT, 1)), pg_outs)
        for f in range(half)
    ]
    copies = start_all([(back_ref.at[:, QW:], back_out.at[:, QW:])] + copies, sems)
    for i in range(blocks):
        leaving(i).wait()
    for copy in copies:
        copy.wait()


def attend(place, x, pkv):
    slots = KV_HEADS * (x.shape[1] - DELTA_ROWS) // COLUMNS
    half, share, prompt_width = pkv[0].shape
    responses = 2 * half
    prompt = responses * share
    keys = slots + prompt
    wide = GROUP * TILE
    outs = [((slots, BACK_W), BF16)] + [((half, share // 2, prompt_width), BF16)] * 4
    stats = pltpu.VMEM((keys // TILE * STATS, wide), F32)
    one_set = [
        pltpu.VMEM((wide, HEAD_DIM), BF16),
        pltpu.VMEM((wide, HEAD_DIM), BF16),
        pltpu.VMEM((HEAD_DIM, wide), BF16),
        pltpu.VMEM((2 * HEAD_DIM, wide), BF16),
        pltpu.VMEM((keys, wide), F32),
        stats,
        stats,
    ]
    return pl.pallas_call(
        attend_kernel,
        in_specs=[SMEM, VMEM, ANY, ANY],
        out_specs=[HBM] * len(outs),
        out_shape=[pltpu.HBM(shape, dtype) for shape, dtype in outs],
        scratch_shapes=[
            pltpu.VMEM((prompt, prompt_width), BF16),
            pltpu.VMEM((slots, BACK_W), BF16),
            pltpu.VMEM((2, prompt // 2, prompt_width), BF16),
            pltpu.SemaphoreType.DMA((1 + 2 * responses,)),
            pltpu.SemaphoreType.DMA((slots // TILE,)),
            pltpu.VMEM((keys, HEAD_DIM), BF16),
            pltpu.VMEM((keys, 2 * HEAD_DIM), BF16),
            pltpu.VMEM((HEAD_DIM, keys), BF16),
            pltpu.VMEM((2 * TILE, wide), BF16),
            pltpu.VMEM((2 * TILE, wide), BF16),
            pltpu.VMEM((HEAD_DIM, wide), F32),
            pltpu.VMEM((keys, HEAD_DIM), F32),
            pltpu.VMEM((keys, HEAD_DIM), F32),
        ]
        + one_set * 2,
        compiler_params=params(50),
        cost_estimate=pl.CostEstimate(
            flops=10 * slots * keys * QW, transcendentals=0, bytes_accessed=8 * slots * QW
        ),
        name="attend",
    )(place, pltpu.with_memory_space_constraint(x, pltpu.VMEM), *pkv)


def core_kernel(place_ref, mine_ref, over_x_ref, low_ref, both_ref, keep_ref, give_ref, total):
    width = mine_ref.shape[2]
    core, low = place_ref[1] & CORE_BIT, place_ref[2] & 1
    total[:, :, pl.ds(times(low, width), width)] = mine_ref[...].astype(F32) + over_x_ref[...].astype(F32)
    total[:, :, pl.ds(times(1 - low, width), width)] = low_ref[...].astype(F32) + both_ref[...].astype(F32)
    for f in range(keep_ref.shape[0]):
        keep_ref[f] = total[2 * f + core]
        give_ref[f] = total[2 * f + 1 - core]


def sum_over_x(place, parts):
    count, share, width = parts[0].shape
    part = jax.ShapeDtypeStruct((count // 2, share, 2 * width), F32)
    return pl.pallas_call(
        core_kernel,
        in_specs=[SMEM] + [VMEM] * 4,
        out_specs=[VMEM] * 2,
        out_shape=[part] * 2,
        scratch_shapes=[pltpu.VMEM((count, share, 2 * width), F32)],
        compiler_params=params(8),
        cost_estimate=pl.CostEstimate(flops=5 * 10**10, transcendentals=0, bytes_accessed=2**20),
        name="sum_over_x",
    )(place, *parts)


def z_kernel(place_ref, mine_ref, got_ref, *refs):
    outs, total = refs[:-1], refs[-1]
    total[...] = mine_ref[...] + got_ref[...]
    z = place_ref[1] // (2 * X_BIT)
    for d, out in enumerate(outs):
        out[...] = total[z ^ d]


def sum_over_cores(place, mine, got):
    count, share, width = mine.shape
    return pl.pallas_call(
        z_kernel,
        in_specs=[SMEM, VMEM, VMEM],
        out_specs=[VMEM] * count,
        out_shape=[jax.ShapeDtypeStruct((share, width), F32)] * count,
        scratch_shapes=[pltpu.VMEM(mine.shape, F32)],
        compiler_params=params(8),
        name="sum_over_cores",
    )(place, mine, got)


def sum_kernel(place_ref, *refs):
    parts, outs, total = refs[:4], refs[4:-1], refs[-1]
    value = parts[0][...]
    for part in parts[1:]:
        value = value + part[...]
    total[...] = value
    own = outs[0].shape[0]
    for d, out in enumerate(outs):
        out[...] = total[pl.ds(times((place_ref[2] // 2) ^ d, own), own)]


def sum_over_z(place, parts):
    rows, width = parts[0].shape
    count = KV_HEADS // 2
    return pl.pallas_call(
        sum_kernel,
        in_specs=[SMEM] + [VMEM] * len(parts),
        out_specs=[VMEM] * count,
        out_shape=[jax.ShapeDtypeStruct((rows // count, width), F32)] * count,
        scratch_shapes=[pltpu.VMEM((rows, width), F32)],
        compiler_params=params(4),
        name="sum_over_z",
    )(place, *parts)


def spread_kernel(place_ref, *refs):
    parts, (k_ref, v_ref) = refs[:-2], refs[-2:]
    for d, part in enumerate(parts):
        for low in range(2):
            cols = pl.ds(times(((place_ref[2] // 2) ^ d) * 2 + low, HEAD_DIM), HEAD_DIM)
            at = 2 * low * HEAD_DIM
            k_ref[:, cols] = part[:, at : at + HEAD_DIM].astype(BF16)
            v_ref[:, cols] = part[:, at + HEAD_DIM : at + 2 * HEAD_DIM].astype(BF16)


def spread_heads(place, parts):
    shape = jax.ShapeDtypeStruct((parts[0].shape[0], KV_HEADS * HEAD_DIM), BF16)
    return pl.pallas_call(
        spread_kernel,
        in_specs=[SMEM] + [VMEM] * len(parts),
        out_specs=[VMEM] * 2,
        out_shape=[shape] * 2,
        compiler_params=params(4),
        name="spread_heads",
    )(place, *parts)


def swap(value, axis, d):
    return lax.ppermute(value, axis, [(i, i ^ d) for i in range(lax.axis_size(axis))])


def swap_all(values, axis, step=1):
    return [values[0]] + [swap(values[d], axis, step * d) for d in range(1, len(values))]


def swap_across(value):
    sizes = lax.axis_size("prefix"), lax.axis_size("resp")
    pairs = [(p * sizes[1] + r, (p ^ X_BIT) * sizes[1] + (r ^ 1)) for p in range(sizes[0]) for r in range(sizes[1])]
    return lax.ppermute(value, ("prefix", "resp"), pairs)


def local(
    resp_query,
    resp_keys,
    resp_values,
    resp_out,
    resp_grad,
    prompt_keys,
    prompt_values,
    resp_lengths,
):
    head = lax.axis_index("resp")
    rows = resp_query.shape[1]
    place = jnp.stack([resp_lengths[0], lax.axis_index("prefix"), head])
    send = pack(resp_query[0], resp_grad[0], resp_out[0], resp_keys[0], resp_values[0])
    x = lax.all_to_all(send, "resp", 0, 0, tiled=True)
    prompt_keys, prompt_values, _ = lax.optimization_barrier((prompt_keys, prompt_values, send))
    cut = lambda a, h: lax.dynamic_slice_in_dim(a, h * HEAD_DIM, HEAD_DIM, 1)
    both = lambda h: jnp.concatenate([cut(prompt_keys, h), cut(prompt_values, h)], axis=1)[None]
    pkv, first = both(head), swap_across(both(head ^ 1))
    pkv = jnp.concatenate([pkv, first])
    for bit in GATHER_BITS[1:-1]:
        pkv = jnp.concatenate([pkv, swap(pkv, "prefix", 1 << bit)])
    pkv = [pkv, swap(pkv, "prefix", 1 << GATHER_BITS[-1])]
    back, *parts = attend(place, x, pkv)
    back = lax.all_to_all(back.reshape(KV_HEADS, rows, BACK_W), "resp", 0, 0, tiled=True)
    parts = [parts[0], swap(parts[1], "prefix", X_BIT), swap(parts[2], "resp", 1), swap_across(parts[3])]
    keep, give = sum_over_x(place, parts)
    parts = sum_over_cores(place, keep, swap(give, "prefix", CORE_BIT))
    parts = sum_over_z(place, swap_all(parts, "prefix", 2 * X_BIT))
    total = spread_heads(place, swap_all(parts, "resp", 2))
    grad_query, grad_keys, grad_values = unpack(back)
    return (grad_query[None], grad_keys[None], grad_values[None], total[0], total[1])


def solution(mesh):
    return jax.shard_map(
        local,
        mesh=mesh,
        in_specs=(
            P("prefix", "resp", None),
            P("prefix", "resp", None),
            P("prefix", "resp", None),
            P("prefix", "resp", None),
            P("prefix", "resp", None),
            P("prefix", None),
            P("prefix", None),
            P("prefix"),
        ),
        out_specs=(
            P("prefix", "resp", None),
            P("prefix", "resp", None),
            P("prefix", "resp", None),
            P(("prefix", "resp"), None),
            P(("prefix", "resp"), None),
        ),
        check_vma=False,
    )
```

```python
import jax
import jax.numpy as jnp
from jax import lax
from jax.experimental import pallas as pl
from jax.experimental.pallas import tpu as pltpu
from jax.sharding import PartitionSpec as P

HEADS = 40
KV_HEADS = 8
GROUP = HEADS // KV_HEADS
HEAD_DIM = 128
SCALE = HEAD_DIM ** (-0.5)
EXP2_SCALE = SCALE * 1.4426950408889634
QW = GROUP * HEAD_DIM
TILE = 256
STATS = 16
UNSEEN = -1e30
PACK_ROWS = 32
GATHER_BITS = (1, 0, 2, 3)
COLUMNS = 2 + 2 * GROUP
DELTA_ROWS = 16
BACK_W = QW + 2 * HEAD_DIM
X_BIT, CORE_BIT = 2, 1

NN = (((1,), (0,)), ((), ()))
BF16 = jnp.bfloat16
F32 = jnp.float32
ANY = pl.BlockSpec(memory_space=pl.ANY)
HBM = pl.BlockSpec(memory_space=pltpu.HBM)
VMEM = pl.BlockSpec(memory_space=pltpu.VMEM)
SMEM = pl.BlockSpec(memory_space=pltpu.SMEM)


def dot(a, b, dims):
    return lax.dot_general(a, b, dims, preferred_element_type=F32)


def params(mib):
    return pltpu.CompilerParams(vmem_limit_bytes=mib * 1024 * 1024)


def times(index, size):
    return pl.multiple_of(index * size, size)


def send_rows(c, n):
    first = (c * COLUMNS + n) * PACK_ROWS
    return slice(first, first + PACK_ROWS)


def gather_mask(index):
    return sum(((index >> step) & 1) << bit for step, bit in enumerate(GATHER_BITS))


def start_all(copies, sems):
    started = [pltpu.make_async_copy(src, dst, sems.at[n]) for n, (src, dst) in enumerate(copies)]
    for copy in started:
        copy.start()
    return started


def pack_kernel(q_in, g_in, o_in, k_in, v_in, send_out, q_ref, g_ref, o_ref, k_ref, v_ref, send_ref, left_ref, sems, out_sems):
    ins = ((q_in, q_ref), (g_in, g_ref), (o_in, o_ref), (k_in, k_ref), (v_in, v_ref))
    steps = q_ref.shape[0] // PACK_ROWS
    arriving = []
    for c in range(steps):
        rows = slice(c * PACK_ROWS, (c + 1) * PACK_ROWS)
        arriving.append(start_all([(src.at[rows], dst.at[rows]) for src, dst in ins], sems.at[c]))
    row = lax.broadcasted_iota(jnp.int32, (QW, HEAD_DIM), 0) // HEAD_DIM
    lane = lax.broadcasted_iota(jnp.int32, (QW, HEAD_DIM), 1)
    ones = jnp.where((lane >= 3 * row) & (lane < 3 * row + 3), 1.0, 0.0).astype(BF16)
    leaving = []
    for c in range(steps):
        rows = slice(c * PACK_ROWS, (c + 1) * PACK_ROWS)
        for copy in arriving[c]:
            copy.wait()
        highs, lows = [], []
        for h in range(KV_HEADS):
            columns = [(k_ref, h), (v_ref, h)]
            columns += [(q_ref, h * GROUP + j) for j in range(GROUP)]
            columns += [(g_ref, h * GROUP + j) for j in range(GROUP)]
            for n, (ref, col) in enumerate(columns):
                send_ref[h, send_rows(c, n)] = ref[rows, col * HEAD_DIM : (col + 1) * HEAD_DIM]
            wide = slice(h * QW, (h + 1) * QW)
            product = g_ref[rows, wide].astype(F32) * o_ref[rows, wide].astype(F32)
            high = product.astype(BF16)
            highs.append(high)
            lows.append((product - high.astype(F32)).astype(BF16))
        part = slice(c * COLUMNS * PACK_ROWS, (c + 1) * COLUMNS * PACK_ROWS)
        leaving += start_all([(send_ref.at[:, part], send_out.at[:, part])], out_sems.at[pl.ds(c, 1)])
        left = dot(jnp.concatenate(highs), ones, NN) + dot(jnp.concatenate(lows), ones, NN)
        for h in range(KV_HEADS):
            left_ref[h, rows] = left[h * PACK_ROWS : (h + 1) * PACK_ROWS]
    part = lax.broadcasted_iota(jnp.int32, (DELTA_ROWS, q_ref.shape[0]), 0) % 3
    last = slice(steps * COLUMNS * PACK_ROWS, steps * COLUMNS * PACK_ROWS + DELTA_ROWS)
    for h in range(KV_HEADS):
        left = left_ref[h].T[0:DELTA_ROWS]
        first = left.astype(BF16).astype(F32)
        second = (left - first).astype(BF16).astype(F32)
        third = left - first - second
        send_ref[h, last] = jnp.where(part == 0, first, jnp.where(part == 1, second, third)).astype(BF16)
    leaving += start_all([(send_ref.at[:, last], send_out.at[:, last])], out_sems.at[pl.ds(steps, 1)])
    for copy in leaving:
        copy.wait()


def pack(q, g, o, k, v):
    rows = q.shape[0]
    steps = rows // PACK_ROWS
    send = (KV_HEADS, rows * COLUMNS + DELTA_ROWS, HEAD_DIM)
    return pl.pallas_call(
        pack_kernel,
        in_specs=[HBM] * 5,
        out_specs=HBM,
        out_shape=pltpu.HBM(send, BF16),
        scratch_shapes=[pltpu.VMEM(a.shape, BF16) for a in (q, g, o, k, v)]
        + [
            pltpu.VMEM(send, BF16),
            pltpu.VMEM((KV_HEADS, rows, HEAD_DIM), F32),
            pltpu.SemaphoreType.DMA((steps, 5)),
            pltpu.SemaphoreType.DMA((steps + 1,)),
        ],
        compiler_params=params(60),
        name="pack",
    )(q, g, o, k, v)


def unpack_kernel(place_ref, back_ref, *refs):
    parts, (q_ref, k_ref, v_ref, prompt_k_ref, prompt_v_ref, sems) = refs[:-6], refs[-6:]
    copies = []
    for h in range(KV_HEADS):
        thin = slice(h * HEAD_DIM, (h + 1) * HEAD_DIM)
        wide = slice(h * QW, (h + 1) * QW)
        copies.append((back_ref.at[h, :, 0:QW], q_ref.at[:, wide]))
        copies.append((back_ref.at[h, :, QW : QW + HEAD_DIM], k_ref.at[:, thin]))
        copies.append((back_ref.at[h, :, QW + HEAD_DIM :], v_ref.at[:, thin]))
    copies = start_all(copies, sems)
    for d, part in enumerate(parts):
        for low in range(2):
            cols = pl.ds(times(((place_ref[2] // 2) ^ d) * 2 + low, HEAD_DIM), HEAD_DIM)
            at = 2 * low * HEAD_DIM
            prompt_k_ref[:, cols] = part[:, at : at + HEAD_DIM].astype(BF16)
            prompt_v_ref[:, cols] = part[:, at + HEAD_DIM : at + 2 * HEAD_DIM].astype(BF16)
    for copy in copies:
        copy.wait()


def unpack(place, back, parts):
    rows = back.shape[1]
    prompt = jax.ShapeDtypeStruct((parts[0].shape[0], KV_HEADS * HEAD_DIM), BF16)
    return pl.pallas_call(
        unpack_kernel,
        in_specs=[SMEM, ANY] + [VMEM] * len(parts),
        out_specs=[ANY] * 3 + [VMEM] * 2,
        out_shape=[
            jax.ShapeDtypeStruct((rows, KV_HEADS * QW), BF16),
            jax.ShapeDtypeStruct((rows, KV_HEADS * HEAD_DIM), BF16),
            jax.ShapeDtypeStruct((rows, KV_HEADS * HEAD_DIM), BF16),
            prompt,
            prompt,
        ],
        scratch_shapes=[pltpu.SemaphoreType.DMA((3 * KV_HEADS,))],
        compiler_params=params(4),
        name="unpack",
    )(place, back, *parts)


def attend_kernel(place_ref, x_ref, pkv_low, pkv_high, back_out, *refs):
    pg_outs, refs = refs[:4], refs[4:]
    pkv_ref, back_ref, pg_ref, sems, block_sems, k_all, v_all, k_t = refs[:8]
    p_s, l_s, dq_t, dk, dv = refs[8:13]
    sets = [refs[13:20], refs[20:27]]
    prompt = pkv_ref.shape[0]
    run = (x_ref.shape[1] - DELTA_ROWS) // COLUMNS
    slots = KV_HEADS * run
    wide = GROUP * TILE
    prompt_tiles = prompt // TILE
    length, me_prefix = place_ref[0], place_ref[1]
    half = pkv_low.shape[0]
    sources = 2 * half
    share = prompt // sources
    copies = [
        ((pkv_low, pkv_high)[f // half].at[f % half], pkv_ref.at[pl.ds(times(me_prefix ^ gather_mask(f), share), share)])
        for f in range(sources)
    ]
    copies = start_all(copies, sems)
    back_ref[...] = jnp.zeros_like(back_ref)
    dk[...] = jnp.zeros_like(dk)
    dv[...] = jnp.zeros_like(dv)
    for block in sets:
        block[3][HEAD_DIM + DELTA_ROWS :] = jnp.zeros((HEAD_DIM - DELTA_ROWS, wide), BF16)
    for copy in copies:
        copy.wait()

    def flip(a):
        return a.astype(F32).T.astype(BF16)

    def slots_of(b, n):
        return jnp.concatenate([x_ref[b, send_rows(c, n)] for c in range(run // PACK_ROWS)])

    k_all[0:prompt] = pkv_ref[:, 0:HEAD_DIM]
    v_all[0:prompt, 0:HEAD_DIM] = pkv_ref[:, HEAD_DIM:]
    for b in range(KV_HEADS):
        own = slice(prompt + b * run, prompt + (b + 1) * run)
        k_all[own] = slots_of(b, 0)
        v_all[own, 0:HEAD_DIM] = slots_of(b, 1)
    v_all[:, HEAD_DIM:] = jnp.full((prompt + slots, HEAD_DIM), -1.0, BF16)
    for t in range((prompt + slots) // TILE):
        block = slice(t * TILE, (t + 1) * TILE)
        k_t[:, block] = flip(k_all[block])

    def lanes(j):
        return slice(j * TILE, (j + 1) * TILE)

    def tile_rows(t, count):
        return pl.ds(times(t, TILE), count * TILE)

    def stat_rows(t, count):
        return pl.ds(times(t, STATS), count * STATS)

    def sweep(body, tiles):
        def pair(n, carry):
            body(2 * n, 2)
            return carry

        last = 2 - tiles % 2
        lax.fori_loop(0, (tiles - last) // 2, pair, 0)
        body(tiles - last, last)

    def load_block(i, block):
        qs, gs, qs_t, gs_t = block[:4]
        sources = range(i * TILE // run, (i + 1) * TILE // run)
        delta_t = jnp.concatenate([x_ref[b, run * COLUMNS :] for b in sources], axis=1).astype(F32)
        part = lax.broadcasted_iota(jnp.int32, delta_t.shape, 0)
        for j in range(GROUP):
            q = jnp.concatenate([slots_of(b, 2 + j) for b in sources])
            g = jnp.concatenate([slots_of(b, 2 + GROUP + j) for b in sources])
            qs[lanes(j)] = q
            gs[lanes(j)] = g
            qs_t[:, lanes(j)] = flip(q)
            gs_t[0:HEAD_DIM, lanes(j)] = flip(g)
            mine = (part >= 3 * j) & (part < 3 * j + 3)
            gs_t[HEAD_DIM : HEAD_DIM + DELTA_ROWS, lanes(j)] = jnp.where(mine, delta_t, 0.0).astype(BF16)

    def score_head(t, count, j, block, diagonal=False):
        qs_t, _, e_all, tops, sums = block[2:]
        s = dot(k_all[tile_rows(t, count)], qs_t[:, lanes(j)], NN)
        if diagonal:
            seen = lax.broadcasted_iota(jnp.int32, s.shape, 0) <= lax.broadcasted_iota(
                jnp.int32, s.shape, 1
            )
            s = jnp.where(seen, s, UNSEEN)
        groups = count * STATS // 8
        s = s.reshape(groups, -1, 8, TILE)
        top = jnp.max(s, axis=1, keepdims=True)
        e = jnp.exp2((s - top) * EXP2_SCALE)
        tops[stat_rows(t, count), lanes(j)] = top.reshape(groups * 8, TILE)
        sums[stat_rows(t, count), lanes(j)] = jnp.sum(e, axis=1).reshape(groups * 8, TILE)
        e_all[tile_rows(t, count), lanes(j)] = e.reshape(count * TILE, TILE)

    def normalise(i, block):
        tops, sums = block[5:]
        rows = STATS * (prompt_tiles + i + 1)
        top = tops[0:rows]
        weight = jnp.exp2((top - jnp.max(top, axis=0, keepdims=True)) * EXP2_SCALE)
        total = jnp.sum(weight * sums[0:rows], axis=0, keepdims=True)
        slot = lax.broadcasted_iota(jnp.int32, (1, wide), 1) % TILE + i * TILE
        tops[0:rows] = weight * (jnp.where(slot < length, 1.0, 0.0) / total)

    def grad_head(t, count, j, block):
        gs_t, e_all, factors = block[3:6]
        shifted = dot(v_all[tile_rows(t, count)], gs_t[:, lanes(j)], NN)
        groups = count * STATS // 8
        e = e_all[tile_rows(t, count), lanes(j)].reshape(groups, -1, 8, TILE)
        factor = factors[stat_rows(t, count), lanes(j)].reshape(groups, 1, 8, TILE)
        p = (e * factor).reshape(count * TILE, TILE)
        p_s[0 : count * TILE, lanes(j)] = p.astype(BF16)
        l_s[0 : count * TILE, lanes(j)] = (p * shifted).astype(BF16)

    def grad_sums(t, count, block):
        qs, gs = block[:2]
        keys, held = tile_rows(t, count), slice(0, count * TILE)
        dv[keys] += dot(p_s[held], gs[...], NN)
        dk[keys] += dot(l_s[held], qs[...], NN)
        dq_t[...] += dot(k_t[:, keys], l_s[held], NN)

    def leaving(i):
        part = (slice(i * TILE, (i + 1) * TILE), slice(0, QW))
        return pltpu.make_async_copy(back_ref.at[part], back_out.at[part], block_sems.at[i])

    def finish(i):
        here = slice(i * TILE, (i + 1) * TILE)
        for j in range(GROUP):
            back_ref[here, j * HEAD_DIM : (j + 1) * HEAD_DIM] = (
                (dq_t[:, lanes(j)] * SCALE).T.astype(BF16)
            )
        leaving(i).start()

    def scores(t, count):
        for j in range(GROUP):
            score_head(t, count, j, sets[0])

    load_block(0, sets[0])
    sweep(scores, prompt_tiles)
    for j in range(GROUP):
        score_head(prompt_tiles, 1, j, sets[0], diagonal=True)
    normalise(0, sets[0])
    load_block(1, sets[1])

    blocks = slots // TILE
    live = lax.div(length + TILE - 1, TILE)
    for i in range(blocks):
        now, later = sets[i % 2], sets[(i + 1) % 2]
        tiles = prompt_tiles + i + 1
        dq_t[...] = jnp.zeros_like(dq_t)

        def grads(t, count):
            for j in range(GROUP):
                grad_head(t, count, j, now)
            grad_sums(t, count, now)

        def both(t, count):
            for j in range(GROUP):
                grad_head(t, count, j, now)
                score_head(t, count, j, later)
            grad_sums(t, count, now)

        if i + 1 < blocks:

            @pl.when(live > i + 1)
            def _():
                sweep(both, tiles)
                for j in range(GROUP):
                    score_head(tiles, 1, j, later, diagonal=True)
                finish(i)
                normalise(i + 1, later)
                if i + 2 < blocks:
                    load_block(i + 2, now)

        @pl.when(live == i + 1)
        def _():
            sweep(grads, tiles)
            finish(i)

        @pl.when(live <= i)
        def _():
            leaving(i).start()

    for n, (total, scale) in enumerate(((dk, SCALE), (dv, 1.0))):
        runs = (total[0:prompt] * scale).reshape(-1, 2, 8, HEAD_DIM)
        for lo in range(2):
            pg_ref[lo, :, n * HEAD_DIM : (n + 1) * HEAD_DIM] = runs[:, lo].reshape(prompt // 2, HEAD_DIM).astype(BF16)
    back_ref[:, QW : QW + HEAD_DIM] = (dk[prompt:] * SCALE).astype(BF16)
    back_ref[:, QW + HEAD_DIM :] = dv[prompt:].astype(BF16)
    mine, low = me_prefix & X_BIT, place_ref[2] & 1
    kept = share // 2
    copies = [
        (pg_ref.at[low ^ flip_low, pl.ds(times(f + (f & -X_BIT) + (mine ^ bit), kept), kept)], out.at[f])
        for (bit, flip_low), out in zip(((0, 0), (X_BIT, 0), (0, 1), (X_BIT, 1)), pg_outs)
        for f in range(half)
    ]
    copies = start_all([(back_ref.at[:, QW:], back_out.at[:, QW:])] + copies, sems)
    for i in range(blocks):
        leaving(i).wait()
    for copy in copies:
        copy.wait()


def attend(place, x, pkv):
    slots = KV_HEADS * (x.shape[1] - DELTA_ROWS) // COLUMNS
    half, share, prompt_width = pkv[0].shape
    responses = 2 * half
    prompt = responses * share
    keys = slots + prompt
    wide = GROUP * TILE
    outs = [((slots, BACK_W), BF16)] + [((half, share // 2, prompt_width), BF16)] * 4
    stats = pltpu.VMEM((keys // TILE * STATS, wide), F32)
    one_set = [
        pltpu.VMEM((wide, HEAD_DIM), BF16),
        pltpu.VMEM((wide, HEAD_DIM), BF16),
        pltpu.VMEM((HEAD_DIM, wide), BF16),
        pltpu.VMEM((2 * HEAD_DIM, wide), BF16),
        pltpu.VMEM((keys, wide), F32),
        stats,
        stats,
    ]
    return pl.pallas_call(
        attend_kernel,
        in_specs=[SMEM, VMEM, ANY, ANY],
        out_specs=[HBM] * len(outs),
        out_shape=[pltpu.HBM(shape, dtype) for shape, dtype in outs],
        scratch_shapes=[
            pltpu.VMEM((prompt, prompt_width), BF16),
            pltpu.VMEM((slots, BACK_W), BF16),
            pltpu.VMEM((2, prompt // 2, prompt_width), BF16),
            pltpu.SemaphoreType.DMA((1 + 2 * responses,)),
            pltpu.SemaphoreType.DMA((slots // TILE,)),
            pltpu.VMEM((keys, HEAD_DIM), BF16),
            pltpu.VMEM((keys, 2 * HEAD_DIM), BF16),
            pltpu.VMEM((HEAD_DIM, keys), BF16),
            pltpu.VMEM((2 * TILE, wide), BF16),
            pltpu.VMEM((2 * TILE, wide), BF16),
            pltpu.VMEM((HEAD_DIM, wide), F32),
            pltpu.VMEM((keys, HEAD_DIM), F32),
            pltpu.VMEM((keys, HEAD_DIM), F32),
        ]
        + one_set * 2,
        compiler_params=params(50),
        cost_estimate=pl.CostEstimate(
            flops=10 * slots * keys * QW, transcendentals=0, bytes_accessed=8 * slots * QW
        ),
        name="attend",
    )(place, pltpu.with_memory_space_constraint(x, pltpu.VMEM), *pkv)


def core_kernel(place_ref, mine_ref, over_x_ref, low_ref, both_ref, keep_ref, give_ref, total):
    width = mine_ref.shape[2]
    core, low = place_ref[1] & CORE_BIT, place_ref[2] & 1
    total[:, :, pl.ds(times(low, width), width)] = mine_ref[...].astype(F32) + over_x_ref[...].astype(F32)
    total[:, :, pl.ds(times(1 - low, width), width)] = low_ref[...].astype(F32) + both_ref[...].astype(F32)
    for f in range(keep_ref.shape[0]):
        keep_ref[f] = total[2 * f + core]
        give_ref[f] = total[2 * f + 1 - core]


def sum_over_x(place, parts):
    count, share, width = parts[0].shape
    part = jax.ShapeDtypeStruct((count // 2, share, 2 * width), F32)
    return pl.pallas_call(
        core_kernel,
        in_specs=[SMEM] + [VMEM] * 4,
        out_specs=[VMEM] * 2,
        out_shape=[part] * 2,
        scratch_shapes=[pltpu.VMEM((count, share, 2 * width), F32)],
        compiler_params=params(8),
        cost_estimate=pl.CostEstimate(flops=5 * 10**10, transcendentals=0, bytes_accessed=2**20),
        name="sum_over_x",
    )(place, *parts)


def z_kernel(place_ref, mine_ref, got_ref, *refs):
    outs, total = refs[:-1], refs[-1]
    total[...] = mine_ref[...] + got_ref[...]
    z = place_ref[1] // (2 * X_BIT)
    for d, out in enumerate(outs):
        out[...] = total[z ^ d]


def sum_over_cores(place, mine, got):
    count, share, width = mine.shape
    return pl.pallas_call(
        z_kernel,
        in_specs=[SMEM, VMEM, VMEM],
        out_specs=[VMEM] * count,
        out_shape=[jax.ShapeDtypeStruct((share, width), F32)] * count,
        scratch_shapes=[pltpu.VMEM(mine.shape, F32)],
        compiler_params=params(8),
        name="sum_over_cores",
    )(place, mine, got)


def sum_kernel(place_ref, *refs):
    parts, outs, total = refs[:4], refs[4:-1], refs[-1]
    value = parts[0][...]
    for part in parts[1:]:
        value = value + part[...]
    total[...] = value
    own = outs[0].shape[0]
    for d, out in enumerate(outs):
        out[...] = total[pl.ds(times((place_ref[2] // 2) ^ d, own), own)]


def sum_over_z(place, parts):
    rows, width = parts[0].shape
    count = KV_HEADS // 2
    return pl.pallas_call(
        sum_kernel,
        in_specs=[SMEM] + [VMEM] * len(parts),
        out_specs=[VMEM] * count,
        out_shape=[jax.ShapeDtypeStruct((rows // count, width), F32)] * count,
        scratch_shapes=[pltpu.VMEM((rows, width), F32)],
        compiler_params=params(4),
        name="sum_over_z",
    )(place, *parts)


def swap(value, axis, d):
    return lax.ppermute(value, axis, [(i, i ^ d) for i in range(lax.axis_size(axis))])


def swap_all(values, axis, step=1):
    return [values[0]] + [swap(values[d], axis, step * d) for d in range(1, len(values))]


def swap_across(value):
    sizes = lax.axis_size("prefix"), lax.axis_size("resp")
    pairs = [(p * sizes[1] + r, (p ^ X_BIT) * sizes[1] + (r ^ 1)) for p in range(sizes[0]) for r in range(sizes[1])]
    return lax.ppermute(value, ("prefix", "resp"), pairs)


def local(
    resp_query,
    resp_keys,
    resp_values,
    resp_out,
    resp_grad,
    prompt_keys,
    prompt_values,
    resp_lengths,
):
    head = lax.axis_index("resp")
    rows = resp_query.shape[1]
    place = jnp.stack([resp_lengths[0], lax.axis_index("prefix"), head])
    send = pack(resp_query[0], resp_grad[0], resp_out[0], resp_keys[0], resp_values[0])
    x = lax.all_to_all(send, "resp", 0, 0, tiled=True)
    prompt_keys, prompt_values, _ = lax.optimization_barrier((prompt_keys, prompt_values, send))
    cut = lambda a, h: lax.dynamic_slice_in_dim(a, h * HEAD_DIM, HEAD_DIM, 1)
    both = lambda h: jnp.concatenate([cut(prompt_keys, h), cut(prompt_values, h)], axis=1)[None]
    pkv, first = both(head), swap_across(both(head ^ 1))
    pkv = jnp.concatenate([pkv, first])
    for bit in GATHER_BITS[1:-1]:
        pkv = jnp.concatenate([pkv, swap(pkv, "prefix", 1 << bit)])
    pkv = [pkv, swap(pkv, "prefix", 1 << GATHER_BITS[-1])]
    back, *parts = attend(place, x, pkv)
    back = lax.all_to_all(back.reshape(KV_HEADS, rows, BACK_W), "resp", 0, 0, tiled=True)
    parts = [parts[0], swap(parts[1], "prefix", X_BIT), swap(parts[2], "resp", 1), swap_across(parts[3])]
    keep, give = sum_over_x(place, parts)
    parts = sum_over_cores(place, keep, swap(give, "prefix", CORE_BIT))
    parts = sum_over_z(place, swap_all(parts, "prefix", 2 * X_BIT))
    outs = unpack(place, back, swap_all(parts, "resp", 2))
    return (*(out[None] for out in outs[:3]), outs[3], outs[4])


def solution(mesh):
    return jax.shard_map(
        local,
        mesh=mesh,
        in_specs=(
            P("prefix", "resp", None),
            P("prefix", "resp", None),
            P("prefix", "resp", None),
            P("prefix", "resp", None),
            P("prefix", "resp", None),
            P("prefix", None),
            P("prefix", None),
            P("prefix"),
        ),
        out_specs=(
            P("prefix", "resp", None),
            P("prefix", "resp", None),
            P("prefix", "resp", None),
            P(("prefix", "resp"), None),
            P(("prefix", "resp"), None),
        ),
        check_vma=False,
    )
```

```python
import jax
import jax.numpy as jnp
from jax import lax
from jax.experimental import pallas as pl
from jax.experimental.pallas import tpu as pltpu
from jax.sharding import PartitionSpec as P

HEADS = 40
KV_HEADS = 8
GROUP = HEADS // KV_HEADS
HEAD_DIM = 128
SCALE = HEAD_DIM ** (-0.5)
EXP2_SCALE = SCALE * 1.4426950408889634
QW = GROUP * HEAD_DIM
TILE = 256
STATS = 16
UNSEEN = -1e30
PACK_ROWS = 16
GATHER_BITS = (1, 0, 2, 3)
COLUMNS = 2 + 2 * GROUP
DELTA_ROWS = 16
BACK_W = QW + 2 * HEAD_DIM
X_BIT, CORE_BIT = 2, 1

NN = (((1,), (0,)), ((), ()))
BF16 = jnp.bfloat16
F32 = jnp.float32
ANY = pl.BlockSpec(memory_space=pl.ANY)
HBM = pl.BlockSpec(memory_space=pltpu.HBM)
VMEM = pl.BlockSpec(memory_space=pltpu.VMEM)
SMEM = pl.BlockSpec(memory_space=pltpu.SMEM)


def dot(a, b, dims):
    return lax.dot_general(a, b, dims, preferred_element_type=F32)


def params(mib):
    return pltpu.CompilerParams(vmem_limit_bytes=mib * 1024 * 1024)


def times(index, size):
    return pl.multiple_of(index * size, size)


def send_rows(c, n):
    first = (c * COLUMNS + n) * PACK_ROWS
    return slice(first, first + PACK_ROWS)


def gather_mask(index):
    return sum(((index >> step) & 1) << bit for step, bit in enumerate(GATHER_BITS))


def start_all(copies, sems):
    started = [pltpu.make_async_copy(src, dst, sems.at[n]) for n, (src, dst) in enumerate(copies)]
    for copy in started:
        copy.start()
    return started


def pack_kernel(q_in, g_in, o_in, k_in, v_in, send_out, q_ref, g_ref, o_ref, k_ref, v_ref, send_ref, left_ref, sems, out_sems):
    ins = ((q_in, q_ref), (g_in, g_ref), (o_in, o_ref), (k_in, k_ref), (v_in, v_ref))
    steps = q_ref.shape[0] // PACK_ROWS
    arriving = []
    for c in range(steps):
        rows = slice(c * PACK_ROWS, (c + 1) * PACK_ROWS)
        arriving.append(start_all([(src.at[rows], dst.at[rows]) for src, dst in ins], sems.at[c]))
    row = lax.broadcasted_iota(jnp.int32, (QW, HEAD_DIM), 0) // HEAD_DIM
    lane = lax.broadcasted_iota(jnp.int32, (QW, HEAD_DIM), 1)
    ones = jnp.where((lane >= 3 * row) & (lane < 3 * row + 3), 1.0, 0.0).astype(BF16)
    leaving = []
    for c in range(steps):
        rows = slice(c * PACK_ROWS, (c + 1) * PACK_ROWS)
        for copy in arriving[c]:
            copy.wait()
        highs, lows = [], []
        for h in range(KV_HEADS):
            columns = [(k_ref, h), (v_ref, h)]
            columns += [(q_ref, h * GROUP + j) for j in range(GROUP)]
            columns += [(g_ref, h * GROUP + j) for j in range(GROUP)]
            for n, (ref, col) in enumerate(columns):
                send_ref[h, send_rows(c, n)] = ref[rows, col * HEAD_DIM : (col + 1) * HEAD_DIM]
            wide = slice(h * QW, (h + 1) * QW)
            product = g_ref[rows, wide].astype(F32) * o_ref[rows, wide].astype(F32)
            high = product.astype(BF16)
            highs.append(high)
            lows.append((product - high.astype(F32)).astype(BF16))
        part = slice(c * COLUMNS * PACK_ROWS, (c + 1) * COLUMNS * PACK_ROWS)
        leaving += start_all([(send_ref.at[:, part], send_out.at[:, part])], out_sems.at[pl.ds(c, 1)])
        left = dot(jnp.concatenate(highs), ones, NN) + dot(jnp.concatenate(lows), ones, NN)
        for h in range(KV_HEADS):
            left_ref[h, rows] = left[h * PACK_ROWS : (h + 1) * PACK_ROWS]
    part = lax.broadcasted_iota(jnp.int32, (DELTA_ROWS, q_ref.shape[0]), 0) % 3
    last = slice(steps * COLUMNS * PACK_ROWS, steps * COLUMNS * PACK_ROWS + DELTA_ROWS)
    for h in range(KV_HEADS):
        left = left_ref[h].T[0:DELTA_ROWS]
        first = left.astype(BF16).astype(F32)
        second = (left - first).astype(BF16).astype(F32)
        third = left - first - second
        send_ref[h, last] = jnp.where(part == 0, first, jnp.where(part == 1, second, third)).astype(BF16)
    leaving += start_all([(send_ref.at[:, last], send_out.at[:, last])], out_sems.at[pl.ds(steps, 1)])
    for copy in leaving:
        copy.wait()


def pack(q, g, o, k, v):
    rows = q.shape[0]
    steps = rows // PACK_ROWS
    send = (KV_HEADS, rows * COLUMNS + DELTA_ROWS, HEAD_DIM)
    return pl.pallas_call(
        pack_kernel,
        in_specs=[HBM] * 5,
        out_specs=HBM,
        out_shape=pltpu.HBM(send, BF16),
        scratch_shapes=[pltpu.VMEM(a.shape, BF16) for a in (q, g, o, k, v)]
        + [
            pltpu.VMEM(send, BF16),
            pltpu.VMEM((KV_HEADS, rows, HEAD_DIM), F32),
            pltpu.SemaphoreType.DMA((steps, 5)),
            pltpu.SemaphoreType.DMA((steps + 1,)),
        ],
        compiler_params=params(60),
        name="pack",
    )(q, g, o, k, v)


def unpack_kernel(place_ref, back_ref, *refs):
    parts, (q_ref, k_ref, v_ref, prompt_k_ref, prompt_v_ref, sems) = refs[:-6], refs[-6:]
    copies = []
    for h in range(KV_HEADS):
        thin = slice(h * HEAD_DIM, (h + 1) * HEAD_DIM)
        wide = slice(h * QW, (h + 1) * QW)
        copies.append((back_ref.at[h, :, 0:QW], q_ref.at[:, wide]))
        copies.append((back_ref.at[h, :, QW : QW + HEAD_DIM], k_ref.at[:, thin]))
        copies.append((back_ref.at[h, :, QW + HEAD_DIM :], v_ref.at[:, thin]))
    copies = start_all(copies, sems)
    for d, part in enumerate(parts):
        for low in range(2):
            cols = pl.ds(times(((place_ref[2] // 2) ^ d) * 2 + low, HEAD_DIM), HEAD_DIM)
            at = 2 * low * HEAD_DIM
            prompt_k_ref[:, cols] = part[:, at : at + HEAD_DIM].astype(BF16)
            prompt_v_ref[:, cols] = part[:, at + HEAD_DIM : at + 2 * HEAD_DIM].astype(BF16)
    for copy in copies:
        copy.wait()


def unpack(place, back, parts):
    rows = back.shape[1]
    prompt = jax.ShapeDtypeStruct((parts[0].shape[0], KV_HEADS * HEAD_DIM), BF16)
    return pl.pallas_call(
        unpack_kernel,
        in_specs=[SMEM, ANY] + [VMEM] * len(parts),
        out_specs=[ANY] * 3 + [VMEM] * 2,
        out_shape=[
            jax.ShapeDtypeStruct((rows, KV_HEADS * QW), BF16),
            jax.ShapeDtypeStruct((rows, KV_HEADS * HEAD_DIM), BF16),
            jax.ShapeDtypeStruct((rows, KV_HEADS * HEAD_DIM), BF16),
            prompt,
            prompt,
        ],
        scratch_shapes=[pltpu.SemaphoreType.DMA((3 * KV_HEADS,))],
        compiler_params=params(4),
        name="unpack",
    )(place, back, *parts)


def attend_kernel(place_ref, x_ref, pkv_low, pkv_high, back_out, *refs):
    pg_outs, refs = refs[:4], refs[4:]
    pkv_ref, back_ref, pg_ref, sems, block_sems, k_all, v_all, k_t = refs[:8]
    p_s, l_s, dq_t, dk, dv = refs[8:13]
    sets = [refs[13:20], refs[20:27]]
    prompt = pkv_ref.shape[0]
    run = (x_ref.shape[1] - DELTA_ROWS) // COLUMNS
    slots = KV_HEADS * run
    wide = GROUP * TILE
    prompt_tiles = prompt // TILE
    length, me_prefix = place_ref[0], place_ref[1]
    half = pkv_low.shape[0]
    sources = 2 * half
    share = prompt // sources
    copies = [
        ((pkv_low, pkv_high)[f // half].at[f % half], pkv_ref.at[pl.ds(times(me_prefix ^ gather_mask(f), share), share)])
        for f in range(sources)
    ]
    copies = start_all(copies, sems)
    back_ref[...] = jnp.zeros_like(back_ref)
    dk[...] = jnp.zeros_like(dk)
    dv[...] = jnp.zeros_like(dv)
    for block in sets:
        block[3][HEAD_DIM + DELTA_ROWS :] = jnp.zeros((HEAD_DIM - DELTA_ROWS, wide), BF16)
    for copy in copies:
        copy.wait()

    def flip(a):
        return a.astype(F32).T.astype(BF16)

    def slots_of(b, n):
        return jnp.concatenate([x_ref[b, send_rows(c, n)] for c in range(run // PACK_ROWS)])

    k_all[0:prompt] = pkv_ref[:, 0:HEAD_DIM]
    v_all[0:prompt, 0:HEAD_DIM] = pkv_ref[:, HEAD_DIM:]
    for b in range(KV_HEADS):
        own = slice(prompt + b * run, prompt + (b + 1) * run)
        k_all[own] = slots_of(b, 0)
        v_all[own, 0:HEAD_DIM] = slots_of(b, 1)
    v_all[:, HEAD_DIM:] = jnp.full((prompt + slots, HEAD_DIM), -1.0, BF16)
    for t in range((prompt + slots) // TILE):
        block = slice(t * TILE, (t + 1) * TILE)
        k_t[:, block] = flip(k_all[block])

    def lanes(j):
        return slice(j * TILE, (j + 1) * TILE)

    def tile_rows(t, count):
        return pl.ds(times(t, TILE), count * TILE)

    def stat_rows(t, count):
        return pl.ds(times(t, STATS), count * STATS)

    def sweep(body, tiles):
        def pair(n, carry):
            body(2 * n, 2)
            return carry

        last = 2 - tiles % 2
        lax.fori_loop(0, (tiles - last) // 2, pair, 0)
        body(tiles - last, last)

    def load_block(i, block):
        qs, gs, qs_t, gs_t = block[:4]
        sources = range(i * TILE // run, (i + 1) * TILE // run)
        delta_t = jnp.concatenate([x_ref[b, run * COLUMNS :] for b in sources], axis=1).astype(F32)
        part = lax.broadcasted_iota(jnp.int32, delta_t.shape, 0)
        for j in range(GROUP):
            q = jnp.concatenate([slots_of(b, 2 + j) for b in sources])
            g = jnp.concatenate([slots_of(b, 2 + GROUP + j) for b in sources])
            qs[lanes(j)] = q
            gs[lanes(j)] = g
            qs_t[:, lanes(j)] = flip(q)
            gs_t[0:HEAD_DIM, lanes(j)] = flip(g)
            mine = (part >= 3 * j) & (part < 3 * j + 3)
            gs_t[HEAD_DIM : HEAD_DIM + DELTA_ROWS, lanes(j)] = jnp.where(mine, delta_t, 0.0).astype(BF16)

    def score_head(t, count, j, block, diagonal=False):
        qs_t, _, e_all, tops, sums = block[2:]
        s = dot(k_all[tile_rows(t, count)], qs_t[:, lanes(j)], NN)
        if diagonal:
            seen = lax.broadcasted_iota(jnp.int32, s.shape, 0) <= lax.broadcasted_iota(
                jnp.int32, s.shape, 1
            )
            s = jnp.where(seen, s, UNSEEN)
        groups = count * STATS // 8
        s = s.reshape(groups, -1, 8, TILE)
        top = jnp.max(s, axis=1, keepdims=True)
        e = jnp.exp2((s - top) * EXP2_SCALE)
        tops[stat_rows(t, count), lanes(j)] = top.reshape(groups * 8, TILE)
        sums[stat_rows(t, count), lanes(j)] = jnp.sum(e, axis=1).reshape(groups * 8, TILE)
        e_all[tile_rows(t, count), lanes(j)] = e.reshape(count * TILE, TILE)

    def normalise(i, block):
        tops, sums = block[5:]
        rows = STATS * (prompt_tiles + i + 1)
        top = tops[0:rows]
        weight = jnp.exp2((top - jnp.max(top, axis=0, keepdims=True)) * EXP2_SCALE)
        total = jnp.sum(weight * sums[0:rows], axis=0, keepdims=True)
        slot = lax.broadcasted_iota(jnp.int32, (1, wide), 1) % TILE + i * TILE
        tops[0:rows] = weight * (jnp.where(slot < length, 1.0, 0.0) / total)

    def grad_head(t, count, j, block):
        gs_t, e_all, factors = block[3:6]
        shifted = dot(v_all[tile_rows(t, count)], gs_t[:, lanes(j)], NN)
        groups = count * STATS // 8
        e = e_all[tile_rows(t, count), lanes(j)].reshape(groups, -1, 8, TILE)
        factor = factors[stat_rows(t, count), lanes(j)].reshape(groups, 1, 8, TILE)
        p = (e * factor).reshape(count * TILE, TILE)
        p_s[0 : count * TILE, lanes(j)] = p.astype(BF16)
        l_s[0 : count * TILE, lanes(j)] = (p * shifted).astype(BF16)

    def grad_sums(t, count, block):
        qs, gs = block[:2]
        keys, held = tile_rows(t, count), slice(0, count * TILE)
        dv[keys] += dot(p_s[held], gs[...], NN)
        dk[keys] += dot(l_s[held], qs[...], NN)
        dq_t[...] += dot(k_t[:, keys], l_s[held], NN)

    def leaving(i):
        part = (slice(i * TILE, (i + 1) * TILE), slice(0, QW))
        return pltpu.make_async_copy(back_ref.at[part], back_out.at[part], block_sems.at[i])

    def finish(i):
        here = slice(i * TILE, (i + 1) * TILE)
        for j in range(GROUP):
            back_ref[here, j * HEAD_DIM : (j + 1) * HEAD_DIM] = (
                (dq_t[:, lanes(j)] * SCALE).T.astype(BF16)
            )
        leaving(i).start()

    def scores(t, count):
        for j in range(GROUP):
            score_head(t, count, j, sets[0])

    load_block(0, sets[0])
    sweep(scores, prompt_tiles)
    for j in range(GROUP):
        score_head(prompt_tiles, 1, j, sets[0], diagonal=True)
    normalise(0, sets[0])
    load_block(1, sets[1])

    blocks = slots // TILE
    live = lax.div(length + TILE - 1, TILE)
    for i in range(blocks):
        now, later = sets[i % 2], sets[(i + 1) % 2]
        tiles = prompt_tiles + i + 1
        dq_t[...] = jnp.zeros_like(dq_t)

        def grads(t, count):
            for j in range(GROUP):
                grad_head(t, count, j, now)
            grad_sums(t, count, now)

        def both(t, count):
            for j in range(GROUP):
                grad_head(t, count, j, now)
                score_head(t, count, j, later)
            grad_sums(t, count, now)

        if i + 1 < blocks:

            @pl.when(live > i + 1)
            def _():
                sweep(both, tiles)
                for j in range(GROUP):
                    score_head(tiles, 1, j, later, diagonal=True)
                finish(i)
                normalise(i + 1, later)
                if i + 2 < blocks:
                    load_block(i + 2, now)

        @pl.when(live == i + 1)
        def _():
            sweep(grads, tiles)
            finish(i)

        @pl.when(live <= i)
        def _():
            leaving(i).start()

    for n, (total, scale) in enumerate(((dk, SCALE), (dv, 1.0))):
        runs = (total[0:prompt] * scale).reshape(-1, 2, 8, HEAD_DIM)
        for lo in range(2):
            pg_ref[lo, :, n * HEAD_DIM : (n + 1) * HEAD_DIM] = runs[:, lo].reshape(prompt // 2, HEAD_DIM).astype(BF16)
    back_ref[:, QW : QW + HEAD_DIM] = (dk[prompt:] * SCALE).astype(BF16)
    back_ref[:, QW + HEAD_DIM :] = dv[prompt:].astype(BF16)
    mine, low = me_prefix & X_BIT, place_ref[2] & 1
    kept = share // 2
    copies = [
        (pg_ref.at[low ^ flip_low, pl.ds(times(f + (f & -X_BIT) + (mine ^ bit), kept), kept)], out.at[f])
        for (bit, flip_low), out in zip(((0, 0), (X_BIT, 0), (0, 1), (X_BIT, 1)), pg_outs)
        for f in range(half)
    ]
    copies = start_all([(back_ref.at[:, QW:], back_out.at[:, QW:])] + copies, sems)
    for i in range(blocks):
        leaving(i).wait()
    for copy in copies:
        copy.wait()


def attend(place, x, pkv):
    slots = KV_HEADS * (x.shape[1] - DELTA_ROWS) // COLUMNS
    half, share, prompt_width = pkv[0].shape
    responses = 2 * half
    prompt = responses * share
    keys = slots + prompt
    wide = GROUP * TILE
    outs = [((slots, BACK_W), BF16)] + [((half, share // 2, prompt_width), BF16)] * 4
    stats = pltpu.VMEM((keys // TILE * STATS, wide), F32)
    one_set = [
        pltpu.VMEM((wide, HEAD_DIM), BF16),
        pltpu.VMEM((wide, HEAD_DIM), BF16),
        pltpu.VMEM((HEAD_DIM, wide), BF16),
        pltpu.VMEM((2 * HEAD_DIM, wide), BF16),
        pltpu.VMEM((keys, wide), F32),
        stats,
        stats,
    ]
    return pl.pallas_call(
        attend_kernel,
        in_specs=[SMEM, VMEM, ANY, ANY],
        out_specs=[HBM] * len(outs),
        out_shape=[pltpu.HBM(shape, dtype) for shape, dtype in outs],
        scratch_shapes=[
            pltpu.VMEM((prompt, prompt_width), BF16),
            pltpu.VMEM((slots, BACK_W), BF16),
            pltpu.VMEM((2, prompt // 2, prompt_width), BF16),
            pltpu.SemaphoreType.DMA((1 + 2 * responses,)),
            pltpu.SemaphoreType.DMA((slots // TILE,)),
            pltpu.VMEM((keys, HEAD_DIM), BF16),
            pltpu.VMEM((keys, 2 * HEAD_DIM), BF16),
            pltpu.VMEM((HEAD_DIM, keys), BF16),
            pltpu.VMEM((2 * TILE, wide), BF16),
            pltpu.VMEM((2 * TILE, wide), BF16),
            pltpu.VMEM((HEAD_DIM, wide), F32),
            pltpu.VMEM((keys, HEAD_DIM), F32),
            pltpu.VMEM((keys, HEAD_DIM), F32),
        ]
        + one_set * 2,
        compiler_params=params(50),
        cost_estimate=pl.CostEstimate(
            flops=10 * slots * keys * QW, transcendentals=0, bytes_accessed=8 * slots * QW
        ),
        name="attend",
    )(place, pltpu.with_memory_space_constraint(x, pltpu.VMEM), *pkv)


def core_kernel(place_ref, mine_ref, over_x_ref, low_ref, both_ref, keep_ref, give_ref, total):
    width = mine_ref.shape[2]
    core, low = place_ref[1] & CORE_BIT, place_ref[2] & 1
    total[:, :, pl.ds(times(low, width), width)] = mine_ref[...].astype(F32) + over_x_ref[...].astype(F32)
    total[:, :, pl.ds(times(1 - low, width), width)] = low_ref[...].astype(F32) + both_ref[...].astype(F32)
    for f in range(keep_ref.shape[0]):
        keep_ref[f] = total[2 * f + core]
        give_ref[f] = total[2 * f + 1 - core]


def sum_over_x(place, parts):
    count, share, width = parts[0].shape
    part = jax.ShapeDtypeStruct((count // 2, share, 2 * width), F32)
    return pl.pallas_call(
        core_kernel,
        in_specs=[SMEM] + [VMEM] * 4,
        out_specs=[VMEM] * 2,
        out_shape=[part] * 2,
        scratch_shapes=[pltpu.VMEM((count, share, 2 * width), F32)],
        compiler_params=params(8),
        cost_estimate=pl.CostEstimate(flops=5 * 10**10, transcendentals=0, bytes_accessed=2**20),
        name="sum_over_x",
    )(place, *parts)


def z_kernel(place_ref, mine_ref, got_ref, *refs):
    outs, total = refs[:-1], refs[-1]
    total[...] = mine_ref[...] + got_ref[...]
    z = place_ref[1] // (2 * X_BIT)
    for d, out in enumerate(outs):
        out[...] = total[z ^ d]


def sum_over_cores(place, mine, got):
    count, share, width = mine.shape
    return pl.pallas_call(
        z_kernel,
        in_specs=[SMEM, VMEM, VMEM],
        out_specs=[VMEM] * count,
        out_shape=[jax.ShapeDtypeStruct((share, width), F32)] * count,
        scratch_shapes=[pltpu.VMEM(mine.shape, F32)],
        compiler_params=params(8),
        name="sum_over_cores",
    )(place, mine, got)


def sum_kernel(place_ref, *refs):
    parts, outs, total = refs[:4], refs[4:-1], refs[-1]
    value = parts[0][...]
    for part in parts[1:]:
        value = value + part[...]
    total[...] = value
    own = outs[0].shape[0]
    for d, out in enumerate(outs):
        out[...] = total[pl.ds(times((place_ref[2] // 2) ^ d, own), own)]


def sum_over_z(place, parts):
    rows, width = parts[0].shape
    count = KV_HEADS // 2
    return pl.pallas_call(
        sum_kernel,
        in_specs=[SMEM] + [VMEM] * len(parts),
        out_specs=[VMEM] * count,
        out_shape=[jax.ShapeDtypeStruct((rows // count, width), F32)] * count,
        scratch_shapes=[pltpu.VMEM((rows, width), F32)],
        compiler_params=params(4),
        name="sum_over_z",
    )(place, *parts)


def swap(value, axis, d):
    return lax.ppermute(value, axis, [(i, i ^ d) for i in range(lax.axis_size(axis))])


def swap_all(values, axis, step=1):
    return [values[0]] + [swap(values[d], axis, step * d) for d in range(1, len(values))]


def swap_across(value):
    sizes = lax.axis_size("prefix"), lax.axis_size("resp")
    pairs = [(p * sizes[1] + r, (p ^ X_BIT) * sizes[1] + (r ^ 1)) for p in range(sizes[0]) for r in range(sizes[1])]
    return lax.ppermute(value, ("prefix", "resp"), pairs)


def local(
    resp_query,
    resp_keys,
    resp_values,
    resp_out,
    resp_grad,
    prompt_keys,
    prompt_values,
    resp_lengths,
):
    head = lax.axis_index("resp")
    rows = resp_query.shape[1]
    place = jnp.stack([resp_lengths[0], lax.axis_index("prefix"), head])
    send = pack(resp_query[0], resp_grad[0], resp_out[0], resp_keys[0], resp_values[0])
    x = lax.all_to_all(send, "resp", 0, 0, tiled=True)
    prompt_keys, prompt_values, _ = lax.optimization_barrier((prompt_keys, prompt_values, send))
    cut = lambda a, h: lax.dynamic_slice_in_dim(a, h * HEAD_DIM, HEAD_DIM, 1)
    both = lambda h: jnp.concatenate([cut(prompt_keys, h), cut(prompt_values, h)], axis=1)[None]
    pkv, first = both(head), swap_across(both(head ^ 1))
    pkv = jnp.concatenate([pkv, first])
    for bit in GATHER_BITS[1:-1]:
        pkv = jnp.concatenate([pkv, swap(pkv, "prefix", 1 << bit)])
    pkv = [pkv, swap(pkv, "prefix", 1 << GATHER_BITS[-1])]
    back, *parts = attend(place, x, pkv)
    back = lax.all_to_all(back.reshape(KV_HEADS, rows, BACK_W), "resp", 0, 0, tiled=True)
    parts = [parts[0], swap(parts[1], "prefix", X_BIT), swap(parts[2], "resp", 1), swap_across(parts[3])]
    keep, give = sum_over_x(place, parts)
    parts = sum_over_cores(place, keep, swap(give, "prefix", CORE_BIT))
    parts = sum_over_z(place, swap_all(parts, "prefix", 2 * X_BIT))
    outs = unpack(place, back, swap_all(parts, "resp", 2))
    return (*(out[None] for out in outs[:3]), outs[3], outs[4])


def solution(mesh):
    return jax.shard_map(
        local,
        mesh=mesh,
        in_specs=(
            P("prefix", "resp", None),
            P("prefix", "resp", None),
            P("prefix", "resp", None),
            P("prefix", "resp", None),
            P("prefix", "resp", None),
            P("prefix", None),
            P("prefix", None),
            P("prefix"),
        ),
        out_specs=(
            P("prefix", "resp", None),
            P("prefix", "resp", None),
            P("prefix", "resp", None),
            P(("prefix", "resp"), None),
            P(("prefix", "resp"), None),
        ),
        check_vma=False,
    )
```
